32 devices in a mesh: dp: 8 (over y, x, core), band: 4 (over z).
Axes of the slice: x: 2, y: 2, z: 4, core: 2. Of those that a mesh axis runs over, the one named last changes fastest.
Arguments:
- visible: bfloat16 [13056, 768], P(('dp', 'band')), may hold values from -6 to 6
- clip_long: int32 [32], P(('dp', 'band')), may hold values from 0 to 1, as said below
- patch_order: int32 [32, 2048], P(('dp', 'band')), may hold values from 0 to 2047, as said below
- embed_weight: bfloat16 [768, 512], replicated, may hold values from -0.21875 to 0.21875
- embed_bias: float32 [512], replicated, may hold values from -3 to 3
- mask_token: float32 [512], replicated, may hold values from -4 to 4
- norm1_gain: float32 [512], replicated, may hold values from 0.1 to 1.9
- norm1_bias: float32 [512], replicated, may hold values from -2 to 2
- qkv_weight: bfloat16 [512, 1536], replicated, may hold values from -0.375 to 0.375
- qv_bias: float32 [2, 512], replicated, may hold values from -2 to 2
- proj_weight: bfloat16 [512, 512], replicated, may hold values from -1 to 1
- proj_bias: float32 [512], replicated, may hold values from -2 to 2
- norm2_gain: float32 [512], replicated, may hold values from 0.1 to 1.9
- norm2_bias: float32 [512], replicated, may hold values from -2 to 2
- fc1_weight: bfloat16 [512, 2048], replicated, may hold values from -0.25 to 0.25
- fc1_bias: float32 [2048], replicated, may hold values from -3 to 3
- fc2_weight: bfloat16 [2048, 512], replicated, may hold values from -0.125 to 0.125
- fc2_bias: float32 [512], replicated, may hold values from -2 to 2
- cotangent: bfloat16 [65536, 512], P(('dp', 'band')), may hold values from -6 to 6
Outputs:
- block_out: bfloat16 [65536, 512], P(('dp', 'band'))
- visible_grad: bfloat16 [13056, 768], P(('dp', 'band'))
- embed_weight_grad: float32 [768, 512], replicated
- embed_bias_grad: float32 [512], replicated
- mask_token_grad: float32 [512], replicated
- norm1_gain_grad: float32 [512], replicated
- norm1_bias_grad: float32 [512], replicated
- qkv_weight_grad: float32 [512, 1536], replicated
- qv_bias_grad: float32 [2, 512], replicated
- proj_weight_grad: float32 [512, 512], replicated
- proj_bias_grad: float32 [512], replicated
- norm2_gain_grad: float32 [512], replicated
- norm2_bias_grad: float32 [512], replicated
- fc1_weight_grad: float32 [512, 2048], replicated
- fc1_bias_grad: float32 [2048], replicated
- fc2_weight_grad: float32 [2048, 512], replicated
- fc2_bias_grad: float32 [512], replicated
The draws below stay inside these ranges and needn't reach their ends.
Inputs may be any that keep to these rules, and one draw needn't show every extreme that they name: `clip_long`: 1 where a device holds one clip of 256 time frames, 0 where it holds two clips of 128 frames. `patch_order`: row d orders device d's patches (index 8 * frame + frequency bin): where clip_long[d] is 1 a permutation of 0 to 2047; else its first 1024 entries permute 0 to 1023 and the rest permute 2048 / 2 to 2047.
All inputs are finite; a program needn't handle non-finite values.
Results may differ from the reference program's by a relative error of at most 0.013.
The reference program's roundings to bfloat16 on the way count: a program that leaves them out, or rounds other values in their place, can miss the bound.
Values may be sent and summed in bfloat16 or wider, within the bound.
No kernel may reach another device: no remote copies, remote signals or barrier semaphores. Data moves between devices by JAX's collectives and lax.ppermute only.
A program may use at most 256 MiB of HBM per device.

```python
import jax
import jax.numpy as jnp
from jax import lax

D_ENC = 768
D = 512
HEADS = 16
FF = 2048
FREQ = 8
WIN = 4
VIS_SHORT = 204
VIS_DEV = 408
ROWS_DEV = 2048
N_DP = 8
DEVICES = 32


def long_flags(key):
    return jax.random.randint(jax.random.fold_in(key, 11), (DEVICES,), 0, 2).astype(jnp.int32)


def draw_clip_long(key, part):
    long_flag = long_flags(key)
    return long_flag


def draw_patch_order(key, part):
    long_flag = long_flags(key)
    key = jax.random.fold_in(key, 5)
    half_rows = ROWS_DEV // 2

    def one_row(device):
        row_key = jax.random.fold_in(key, device)
        whole_perm = jax.random.permutation(jax.random.fold_in(row_key, 1), ROWS_DEV)
        first_perm = jax.random.permutation(jax.random.fold_in(row_key, 2), half_rows)
        second_perm = jax.random.permutation(jax.random.fold_in(row_key, 3), half_rows) + half_rows
        return (whole_perm, jnp.concatenate([first_perm, second_perm]))
    whole_rows, paired_rows = jax.vmap(one_row)(jnp.arange(DEVICES))
    return jnp.where(long_flag[:, None] == 1, whole_rows, paired_rows).astype(jnp.int32)


def shard_levels(rng, extent, pieces, smallest, largest):
    level, own = 1.0, jax.random.fold_in(rng, 6)
    for dim, shards_of in pieces:
        steps = jnp.exp(jax.random.uniform(jax.random.fold_in(own, dim), (shards_of,), jnp.float32, smallest / len(pieces), largest / len(pieces)))
        level = level * jnp.repeat(steps, extent[dim] // shards_of).reshape([-1 if axis == dim else 1 for axis in range(len(extent))])
    return level


def centred(own_key, extent, width, limit, split=(), kind=jnp.bfloat16):
    values = width * jax.random.normal(own_key, extent, jnp.float32)
    if split:
        values = values * shard_levels(own_key, extent, split, -0.22, 0.18)
    return jnp.clip(values, -limit, limit).astype(kind)


def setup_inputs(seed: int = 0) -> dict:
    key_of = jax.random.split(jax.random.key(seed), 20)
    return {
        "visible": centred(key_of[0], (DEVICES * VIS_DEV, D_ENC), 1.0, 6.0, ((0, 32),)),
        "clip_long": draw_clip_long(jax.random.fold_in(key_of[19], 71), 0),
        "patch_order": draw_patch_order(jax.random.fold_in(key_of[19], 71), 0),
        "embed_weight": centred(key_of[3], (D_ENC, D), D_ENC ** -0.5, 0.21875),
        "embed_bias": centred(key_of[4], (D,), 0.5, 3.0, (), jnp.float32),
        "mask_token": centred(key_of[5], (D,), 1.0, 4.0, (), jnp.float32),
        "norm1_gain": jnp.clip(1.0 + 0.18 * jax.random.normal(key_of[6], (D,), jnp.float32), 0.1, 1.9),
        "norm1_bias": centred(key_of[7], (D,), 0.3, 2.0, (), jnp.float32),
        "qkv_weight": centred(key_of[8], (D, 3 * D), (D // 2) ** -0.5, 0.375),
        "qv_bias": centred(key_of[9], (2, D), 0.3, 2.0, (), jnp.float32),
        "proj_weight": centred(key_of[10], (D, D), (D // 16) ** -0.5, 1.0),
        "proj_bias": centred(key_of[11], (D,), 0.3, 2.0, (), jnp.float32),
        "norm2_gain": jnp.clip(1.0 + 0.18 * jax.random.normal(key_of[12], (D,), jnp.float32), 0.1, 1.9),
        "norm2_bias": centred(key_of[13], (D,), 0.3, 2.0, (), jnp.float32),
        "fc1_weight": centred(key_of[14], (D, FF), D ** -0.5, 0.25),
        "fc1_bias": centred(key_of[15], (FF,), 0.5, 3.0, (), jnp.float32),
        "fc2_weight": centred(key_of[16], (FF, D), FF ** -0.5, 0.125),
        "fc2_bias": centred(key_of[17], (D,), 0.3, 2.0, (), jnp.float32),
        "cotangent": centred(key_of[18], (DEVICES * ROWS_DEV, D), 1.0, 6.0, ((0, 32),)),
    }


epsilon = 1e-06
highest = lax.Precision.HIGHEST

@jax.custom_vjp
def low(v):
    return lax.optimization_barrier(v.astype(jnp.bfloat16)).astype(jnp.float32)

@jax.custom_vjp
def low_back(v):
    return v

def low_keep(v):
    return (low(v), None)

def low_pass(kept, grad):
    return (grad,)

def back_keep(v):
    return (v, None)

def back_low(kept, grad):
    return (low(grad),)
low.defvjp(low_keep, low_pass)
low_back.defvjp(back_keep, back_low)

def matmul(left, right):
    return jnp.dot(left, right, precision=highest)

def sincos(places, features):
    halfway = features // 2
    omega = 1.0 / 10000.0 ** (jnp.arange(halfway, dtype=jnp.float32) / halfway)
    angles = places.astype(jnp.float32)[:, None] * omega[None, :]
    return jnp.concatenate([jnp.sin(angles), jnp.cos(angles)], axis=1)

def positions(frame_time, column, features):
    return jnp.concatenate([sincos(frame_time, features // 2), sincos(column, features // 2)], axis=1)

def row_layout(long_clip, row_count, freq_bins):
    quarter = row_count // 4
    span = row_count // (2 * freq_bins)
    halfspan = span // 2
    rowid = jnp.arange(row_count, dtype=jnp.int32)
    target = rowid // quarter
    inner = rowid % quarter
    column = target // 2 * WIN + inner % WIN
    local = inner // WIN
    halves = target % 2
    short_time = halves * halfspan + local % halfspan
    short_frame = local // halfspan * span + short_time
    long_frame = halves * span + local
    is_long = long_clip == 1
    frame_time = jnp.where(is_long, long_frame, short_time)
    frame_place = jnp.where(is_long, long_frame, short_frame)
    return (frame_place * freq_bins + column, frame_time, column)

def visible_places(long_clip, ordering, vis_short):
    slots = jnp.arange(2 * vis_short, dtype=jnp.int32)
    halfway = ordering.shape[0] // 2
    paired = jnp.where(slots < vis_short, slots, halfway + slots - vis_short)
    chosen = jnp.where(long_clip == 1, slots, paired)
    return jnp.take(ordering, chosen)

def layer_norm(values, gain, bias):
    center = values - lax.optimization_barrier(jnp.mean(values, axis=-1, keepdims=True))
    spread = lax.optimization_barrier(jnp.mean(center * center, axis=-1, keepdims=True))
    return center * lax.rsqrt(spread + epsilon) * gain + bias

def gelu(values):
    return 0.5 * values * (1.0 + lax.erf(values * 0.7071067811865476))

def entry(encoder_rows, long_clip, ordering, embed_w, embed_b, mask_vec):
    embedded = low(matmul(encoder_rows, embed_w) + embed_b)
    places, frame_time, column = row_layout(long_clip, ordering.shape[0], FREQ)
    visible_at = visible_places(long_clip, ordering, VIS_SHORT)
    chooser = (places[:, None] == visible_at[None, :]).astype(embedded.dtype)
    filled = lax.optimization_barrier(jnp.sum(chooser, axis=1, keepdims=True))
    start = matmul(chooser, embedded) + (1.0 - filled) * mask_vec + positions(frame_time, column, D)
    return low(low_back(start))

def windowed(values):
    return values.reshape(values.shape[0] // (WIN * WIN), WIN * WIN, HEADS, D // HEADS)

def block(inputs, params):
    gain_one, bias_one, qkv_w, qv_b, proj_w, proj_b, gain_two, bias_two, up_w, up_b, down_w, down_b = params
    normed = low(layer_norm(inputs, gain_one, bias_one))
    projected = matmul(normed, qkv_w)
    queries = low(low_back(projected[:, :D] + qv_b[0]))
    key_rows = low(low_back(projected[:, D:2 * D]))
    value_rows = low(low_back(projected[:, 2 * D:] + qv_b[1]))
    scores = low_back(jnp.einsum('wqhe,wkhe->whqk', windowed(queries), windowed(key_rows), precision=highest) * (D // HEADS) ** (-0.5))
    shifted = jnp.exp(scores - lax.optimization_barrier(jnp.max(scores, axis=-1, keepdims=True)))
    attn_probs = shifted / lax.optimization_barrier(jnp.sum(shifted, axis=-1, keepdims=True))
    mixed_rows = jnp.einsum('whqk,wkhe->wqhe', low(attn_probs), windowed(value_rows), precision=highest)
    attended = low(low_back(mixed_rows.reshape(inputs.shape)))
    residual = inputs + low_back(matmul(attended, proj_w) + proj_b)
    normed_two = low(layer_norm(residual, gain_two, bias_two))
    activated = low(gelu(low_back(matmul(normed_two, up_w) + up_b)))
    return residual + low_back(matmul(activated, down_w) + down_b)

def reference(visible, clip_long, patch_order, embed_weight, embed_bias, mask_token, norm1_gain, norm1_bias, qkv_weight, qv_bias, proj_weight, proj_bias, norm2_gain, norm2_bias, fc1_weight, fc1_bias, fc2_weight, fc2_bias, cotangent):
    row_count = patch_order.shape[1]
    weights = (embed_weight.astype(jnp.float32), embed_bias, mask_token, norm1_gain, norm1_bias, qkv_weight.astype(jnp.float32), qv_bias, proj_weight.astype(jnp.float32), proj_bias, norm2_gain, norm2_bias, fc1_weight.astype(jnp.float32), fc1_bias, fc2_weight.astype(jnp.float32), fc2_bias)

    def forward(encoder_rows, tensors):
        params = tensors[3:]
        starts = jax.vmap(entry, in_axes=(0, 0, 0, None, None, None))(encoder_rows.reshape(-1, VIS_DEV, D_ENC), clip_long, patch_order, tensors[0], tensors[1], tensors[2])
        groups = starts.reshape(N_DP, 4, 4, row_count // 4, D).transpose(0, 2, 1, 3, 4).reshape(N_DP, 4 * row_count, D)
        outputs = lax.map(jax.checkpoint(lambda group: block(group, params)), groups)
        return outputs.reshape(-1, D)
    block_out, pull = jax.vjp(forward, visible.astype(jnp.float32), weights)
    visible_grad, grads = pull(cotangent.astype(jnp.float32))
    return (block_out.astype(jnp.bfloat16), visible_grad.astype(jnp.bfloat16), grads[0], grads[1], grads[2], grads[3], grads[4], grads[5], grads[6], grads[7], grads[8], grads[9], grads[10], grads[11], grads[12], grads[13], grads[14])
```

```python
import functools

import jax
import jax.numpy as jnp
from jax import lax
from jax.experimental import pallas as pl
from jax.experimental.pallas import tpu as pltpu
from jax.sharding import PartitionSpec as P

HEADS = 16
FREQ = 8
WIN = 4
EPS = 1e-06
BF = jnp.bfloat16
F32 = jnp.float32
LANES = 128
MIB = 1024 * 1024


def row_layout(is_long, rowid, row_count):
    quarter = row_count // 4
    span = row_count // (2 * FREQ)
    halfspan = span // 2
    target = rowid // quarter
    inner = rowid % quarter
    column = target // 2 * WIN + inner % WIN
    local = inner // WIN
    halves = target % 2
    if is_long:
        frame_time = halves * span + local
        frame = frame_time
    else:
        frame_time = halves * halfspan + local % halfspan
        frame = local // halfspan * span + frame_time
    return frame * FREQ + column, frame_time, column


def sincos_rows(places, features):
    halfway = features // 2
    omega = 1.0 / 10000.0 ** (jnp.arange(halfway, dtype=F32) / halfway)
    angles = omega[:, None] * places.astype(F32)[None, :]
    return jnp.concatenate([jnp.sin(angles), jnp.cos(angles)], axis=0)


def positions_t(frame_time, column, features):
    return jnp.concatenate(
        [sincos_rows(frame_time, features // 2), sincos_rows(column, features // 2)], axis=0
    )


def mm(a, b):
    return lax.dot_general(a, b, (((1,), (0,)), ((), ())), preferred_element_type=F32)


def mm_nt(a, b):
    return lax.dot_general(a, b, (((1,), (1,)), ((), ())), preferred_element_type=F32)


def lane_block(t):
    return pl.ds(pl.multiple_of(t * LANES, LANES), LANES)


def window_of_lane(rows, columns):
    lane = lax.broadcasted_iota(jnp.int32, (rows, columns), 1)
    return (lane % LANES) // (WIN * WIN)


def compact(square, win):
    size = WIN * WIN
    out = square[0:size]
    for w in range(1, LANES // size):
        out = jnp.where(win == w, square[w * size : (w + 1) * size], out)
    return out


def expand(rows, win):
    size = WIN * WIN
    return jnp.concatenate(
        [jnp.where(win == w, rows, 0.0).astype(BF) for w in range(LANES // size)], axis=0
    )


def stacked(wide):
    return jnp.concatenate(
        [wide[:, j * LANES : (j + 1) * LANES] for j in range(wide.shape[1] // LANES)], axis=0
    )


def heads_apart(group, width):
    count = LANES // width
    blocks = []
    for j in range(count):
        parts = []
        if j:
            parts.append(jnp.zeros((j * width, LANES), BF))
        parts.append(group[j * width : (j + 1) * width])
        if j < count - 1:
            parts.append(jnp.zeros(((count - 1 - j) * width, LANES), BF))
        blocks.append(jnp.concatenate(parts, axis=0))
    return jnp.concatenate(blocks, axis=1)


def heads_of(wide, width):
    return jnp.concatenate(
        [
            wide[j * width : (j + 1) * width, j * LANES : (j + 1) * LANES]
            for j in range(LANES // width)
        ],
        axis=0,
    )


def normalize_t(x):
    count = x.shape[0]
    center = x - jnp.sum(x, axis=0, keepdims=True) * (1.0 / count)
    var = jnp.sum(center * center, axis=0, keepdims=True) * (1.0 / count)
    scale = lax.rsqrt(var + EPS)
    return center * scale, scale


def normalize_back_t(grad, unit, scale, gain):
    count = grad.shape[0]
    inner = grad * gain
    mean = jnp.sum(inner, axis=0, keepdims=True) * (1.0 / count)
    mixed = jnp.sum(inner * unit, axis=0, keepdims=True) * (1.0 / count)
    return scale * (inner - mean - unit * mixed)


def lane_sums(acc):
    return jnp.sum(acc.T, axis=0, keepdims=True)


def chooser_t(vis, place):
    return jnp.where(vis == place, 1.0, 0.0)


C_MASK, C_G1, C_B1, C_QB, C_VB, C_PB, C_G2, C_B2, C_F2B = range(9)


def forward_kernel(
    sk, flags,
    emb, vis, place, pos_long, pos_short, cols, fc1b, cot,
    wqkv_t, wproj_t, w1_t, w1, w2_t, w2,
    block_out, x_t, qkv_t, probs, o_t, act_t, gh_t, c_out, gx1_t, sums,
    emb_pad, a_t, x1_t, c_t, cot_t, unit2, scale2, wide, acc,
):
    features = x_t.shape[0]
    rows = x_t.shape[1]
    tiles = rows // LANES
    width = features // HEADS
    factor = width ** (-0.5)
    step = pl.program_id(0)
    is_long = flags[step] == 1

    def col(i):
        return cols[:, i : i + 1]

    count = emb.shape[0]
    emb_pad[0:count, :] = emb[...]
    emb_pad[count:, :] = jnp.zeros((emb_pad.shape[0] - count, features), BF)
    wide[...] = mm(emb_pad[...].T, chooser_t(vis[...], place[...]).astype(BF))

    def entry_step(t, _):
        sl = lane_block(t)
        filled = jnp.sum(chooser_t(vis[...], place[:, sl]), axis=0, keepdims=True)
        pos = jnp.where(is_long, pos_long[:, sl], pos_short[:, sl])
        start = (wide[:, sl] + (1.0 - filled) * col(C_MASK)) + pos
        start = start.astype(BF)
        x_t[:, sl] = start
        unit, _scale = normalize_t(start.astype(F32))
        a_t[:, sl] = (unit * col(C_G1) + col(C_B1)).astype(BF)
        cot_t[:, sl] = cot[pl.ds(pl.multiple_of(t * LANES, LANES), LANES), :].T
        return 0

    lax.fori_loop(0, tiles, entry_step, 0)

    for i, bias in ((0, C_QB), (1, None), (2, C_VB)):
        part = pl.ds(i * features, features)
        prod = mm(wqkv_t[part, :], a_t[...])
        if bias is not None:
            prod = prod + col(bias)
        qkv_t[part, :] = prod.astype(BF)

    def attention_step(t, _):
        sl = lane_block(t)
        win = window_of_lane(WIN * WIN, 4 * LANES)
        for g in range(features // LANES):
            q_g = qkv_t[pl.ds(g * LANES, LANES), sl]
            k_g = qkv_t[pl.ds(features + g * LANES, LANES), sl]
            v_g = qkv_t[pl.ds(2 * features + g * LANES, LANES), sl]
            scores = compact(mm(k_g.T, heads_apart(q_g, width)), win) * factor
            shifted = jnp.exp(scores - jnp.max(scores, axis=0, keepdims=True))
            prob = shifted / jnp.sum(shifted, axis=0, keepdims=True)
            probs[t, :, g * 4 * LANES : (g + 1) * 4 * LANES] = prob
            mixed = mm(v_g, expand(prob, win))
            o_t[pl.ds(g * LANES, LANES), sl] = heads_of(mixed, width).astype(BF)
        return 0

    lax.fori_loop(0, tiles, attention_step, 0)

    wide[...] = mm(wproj_t[...], o_t[...])

    def norm2_step(t, _):
        sl = lane_block(t)
        x1 = x_t[:, sl].astype(F32) + (wide[:, sl] + col(C_PB))
        x1_t[:, sl] = x1
        unit, scale = normalize_t(x1)
        unit2[:, sl] = unit
        scale2[:, sl] = scale
        low = (unit * col(C_G2) + col(C_B2)).astype(BF)
        c_t[:, sl] = low
        c_out[pl.ds(pl.multiple_of(t * LANES, LANES), LANES), :] = low.T
        return 0

    lax.fori_loop(0, tiles, norm2_step, 0)

    chunk = features

    def hidden_step(f, _):
        part = pl.ds(pl.multiple_of(f * chunk, chunk), chunk)
        hidden = mm(w1_t[part, :], c_t[...]) + fc1b[part, :]
        cumulative = 0.5 * (1.0 + lax.erf(hidden * 0.7071067811865476))
        act_t[part, :] = (hidden * cumulative).astype(BF)
        slope = cumulative + hidden * jnp.exp(-0.5 * hidden * hidden) * 0.3989422804014327
        gact = mm(w2[part, :], cot_t[...])
        gh_t[part, :] = (gact * slope).astype(BF)
        return 0

    lax.fori_loop(0, w1_t.shape[0] // chunk, hidden_step, 0)

    half = features // 2

    def out_step(i, _):
        part = pl.ds(pl.multiple_of(i * half, half), half)
        wide[part, :] = mm(w2_t[part, :], act_t[...])
        return 0

    lax.fori_loop(0, 2, out_step, 0)

    def finish_step(t, _):
        sl = lane_block(t)
        out = x1_t[:, sl] + (wide[:, sl] + col(C_F2B))
        block_out[pl.ds(pl.multiple_of(t * LANES, LANES), LANES), :] = out.astype(BF).T
        return 0

    lax.fori_loop(0, tiles, finish_step, 0)

    def back_step(i, _):
        part = pl.ds(pl.multiple_of(i * half, half), half)
        wide[part, :] = mm(w1[part, :], gh_t[...])
        return 0

    lax.fori_loop(0, 2, back_step, 0)

    acc[...] = jnp.zeros_like(acc)

    def norm2_back_step(t, _):
        sl = lane_block(t)
        gc = wide[:, sl]
        unit = unit2[:, sl]
        acc[0] += gc * unit
        acc[1] += gc
        back = normalize_back_t(gc, unit, scale2[:, sl], col(C_G2))
        gx1_t[:, sl] = cot_t[:, sl].astype(F32) + back
        return 0

    lax.fori_loop(0, tiles, norm2_back_step, 0)
    sums[...] = jnp.zeros_like(sums)
    sums[0:1, :] = lane_sums(acc[0])
    sums[1:2, :] = lane_sums(acc[1])


def backward_kernel(
    sk,
    vis, place, cols, x_t, qkv_t, probs, gx1_t, wproj, wqkv,
    gqkv_t, a_out, gy_out, gemb, sums,
    gy_t, go_t, gx, wide, acc,
):
    features = x_t.shape[0]
    rows = x_t.shape[1]
    tiles = rows // LANES
    width = features // HEADS
    factor = width ** (-0.5)

    def col(i):
        return cols[:, i : i + 1]

    acc[...] = jnp.zeros_like(acc)

    def branch_step(t, _):
        sl = lane_block(t)
        low = gx1_t[:, sl].astype(BF)
        gy_t[:, sl] = low
        gy_out[pl.ds(pl.multiple_of(t * LANES, LANES), LANES), :] = low.T
        acc[0] += low.astype(F32)
        return 0

    lax.fori_loop(0, tiles, branch_step, 0)
    go_t[...] = mm(wproj[...], gy_t[...]).astype(BF)

    def attention_step(t, _):
        sl = lane_block(t)
        win = window_of_lane(WIN * WIN, 4 * LANES)
        for g in range(features // LANES):
            part = pl.ds(g * LANES, LANES)
            q_g = qkv_t[part, sl]
            k_g = qkv_t[pl.ds(features + g * LANES, LANES), sl]
            v_g = qkv_t[pl.ds(2 * features + g * LANES, LANES), sl]
            go_g = go_t[part, sl]
            gp = compact(mm(v_g.T, heads_apart(go_g, width)), win)
            prob = probs[t, :, g * 4 * LANES : (g + 1) * 4 * LANES]
            gs = prob * (gp - jnp.sum(gp * prob, axis=0, keepdims=True))
            gs_wide = expand(gs, win)
            prob_wide = expand(prob, win)
            gq = (heads_of(mm(k_g, gs_wide), width) * factor).astype(BF)
            gk = (heads_of(mm_nt(q_g, stacked(gs_wide)), width) * factor).astype(BF)
            gv = heads_of(mm_nt(go_g, stacked(prob_wide)), width).astype(BF)
            gqkv_t[part, sl] = gq
            gqkv_t[pl.ds(features + g * LANES, LANES), sl] = gk
            gqkv_t[pl.ds(2 * features + g * LANES, LANES), sl] = gv
            acc[1, part] += gq.astype(F32)
            acc[2, part] += gv.astype(F32)
        return 0

    lax.fori_loop(0, tiles, attention_step, 0)

    half = features // 2

    def back_step(i, _):
        part = pl.ds(pl.multiple_of(i * half, half), half)
        wide[part, :] = mm(wqkv[part, :], gqkv_t[...])
        return 0

    lax.fori_loop(0, 2, back_step, 0)

    def norm1_back_step(t, _):
        sl = lane_block(t)
        rows_t = pl.ds(pl.multiple_of(t * LANES, LANES), LANES)
        unit, scale = normalize_t(x_t[:, sl].astype(F32))
        a_out[rows_t, :] = (unit * col(C_G1) + col(C_B1)).astype(BF).T
        ga = wide[:, sl]
        acc[3] += ga * unit
        acc[4] += ga
        back = normalize_back_t(ga, unit, scale, col(C_G1))
        low = (gx1_t[:, sl] + back).astype(BF)
        gx[rows_t, :] = low.T
        filled = jnp.sum(chooser_t(vis[...], place[:, sl]), axis=0, keepdims=True)
        acc[5] += low.astype(F32) * (1.0 - filled)
        return 0

    lax.fori_loop(0, tiles, norm1_back_step, 0)
    chosen = mm(chooser_t(vis[...], place[...]).astype(BF), gx[...])
    gemb[...] = chosen[0 : gemb.shape[0]].astype(BF)
    sums[...] = jnp.zeros_like(sums)
    for i in range(6):
        sums[i : i + 1, :] = lane_sums(acc[i])


def product_kernel(left, right, out):
    out[...] = mm(left[...], right[...]).astype(BF)


def product_bias_kernel(left, right, out, bias):
    out[...] = mm(left[...], right[...]).astype(BF)
    total = left[:, 0:LANES].astype(F32)
    for i in range(1, left.shape[1] // LANES):
        total += left[:, i * LANES : (i + 1) * LANES].astype(F32)
    bias[...] = jnp.sum(total.T, axis=0, keepdims=True)


def product(left, right, with_bias=False, block=256):
    m, depth = left.shape
    n = right.shape[1]
    steps = m // block
    out_shape = [jax.ShapeDtypeStruct((m, n), BF)]
    out_specs = [pl.BlockSpec((block, n), lambda i: (i, 0))]
    if with_bias:
        out_shape.append(jax.ShapeDtypeStruct((steps, 1, block), F32))
        out_specs.append(pl.BlockSpec((None, 1, block), lambda i: (i, 0, 0)))
    out = pl.pallas_call(
        product_bias_kernel if with_bias else product_kernel,
        grid=(steps,),
        in_specs=[
            pl.BlockSpec((block, depth), lambda i: (i, 0)),
            pl.BlockSpec((depth, n), lambda i: (0, 0)),
        ],
        out_specs=out_specs,
        out_shape=out_shape,
        cost_estimate=pl.CostEstimate(
            flops=2 * m * n * depth, bytes_accessed=2 * (m * depth + n * depth + m * n),
            transcendentals=0,
        ),
        compiler_params=pltpu.CompilerParams(vmem_limit_bytes=32 * MIB),
    )(left, right)
    return out if with_bias else out[0]


def whole(shape):
    zeros = (0,) * len(shape)
    return pl.BlockSpec(shape, lambda i, *_: zeros, pipeline_mode=pl.Buffered(1))


def forward(sk, flags, emb, vis, place, pos_long, pos_short, cols, fc1b, cot, weights):
    count, features = emb.shape[1:]
    rows = place.shape[2]
    total = cot.shape[0]
    hidden = fc1b.shape[0]
    n = emb.shape[0]
    tiles = rows // LANES
    per_k = lambda k, *_: (k, 0, 0)
    lanes_s = lambda k, sk, *_: (0, sk[k])
    rows_s = lambda k, sk, *_: (sk[k], 0)
    s = jax.ShapeDtypeStruct
    return pl.pallas_call(
        forward_kernel,
        grid_spec=pltpu.PrefetchScalarGridSpec(
            num_scalar_prefetch=2,
            grid=(n,),
            in_specs=[
                pl.BlockSpec((None, count, features), per_k),
                pl.BlockSpec((None, rows, 1), per_k),
                pl.BlockSpec((None, 1, rows), per_k),
                whole(pos_long.shape),
                whole(pos_short.shape),
                whole(cols.shape),
                whole(fc1b.shape),
                pl.BlockSpec((rows, features), rows_s),
            ]
            + [whole(w.shape) for w in weights],
            out_specs=[
                pl.BlockSpec((rows, features), rows_s),
                pl.BlockSpec((features, rows), lanes_s),
                pl.BlockSpec((3 * features, rows), lanes_s),
                pl.BlockSpec((None, tiles, WIN * WIN, HEADS * LANES), lambda k, sk, *_: (sk[k], 0, 0, 0)),
                pl.BlockSpec((features, rows), lanes_s),
                pl.BlockSpec((hidden, rows), lanes_s),
                pl.BlockSpec((hidden, rows), lanes_s),
                pl.BlockSpec((rows, features), rows_s),
                pl.BlockSpec((features, rows), lanes_s),
                pl.BlockSpec((None, 8, features), per_k),
            ],
            scratch_shapes=[
                pltpu.VMEM((rows, features), BF),
                pltpu.VMEM((features, rows), BF),
                pltpu.VMEM((features, rows), F32),
                pltpu.VMEM((features, rows), BF),
                pltpu.VMEM((features, rows), BF),
                pltpu.VMEM((features, rows), F32),
                pltpu.VMEM((1, rows), F32),
                pltpu.VMEM((features, rows), F32),
                pltpu.VMEM((2, features, LANES), F32),
            ],
        ),
        out_shape=[
            s((total, features), BF),
            s((features, total), BF),
            s((3 * features, total), BF),
            s((total // rows, tiles, WIN * WIN, HEADS * LANES), F32),
            s((features, total), BF),
            s((hidden, total), BF),
            s((hidden, total), BF),
            s((total, features), BF),
            s((features, total), F32),
            s((n, 8, features), F32),
        ],
        cost_estimate=pl.CostEstimate(
            flops=2 * n * rows * features * (4 * features + 4 * hidden + 2 * rows),
            bytes_accessed=28 * MIB,
            transcendentals=3 * n * rows * hidden,
        ),
        compiler_params=pltpu.CompilerParams(vmem_limit_bytes=56 * MIB),
    )(sk, flags, emb, vis, place, pos_long, pos_short, cols, fc1b, cot, *weights)


def backward(sk, count, vis, place, cols, x_t, qkv_t, probs, gx1_t, wproj, wqkv):
    features, total = x_t.shape
    n, _, rows = place.shape
    tiles = rows // LANES
    per_k = lambda k, *_: (k, 0, 0)
    lanes_s = lambda k, sk, *_: (0, sk[k])
    rows_s = lambda k, sk, *_: (sk[k], 0)
    s = jax.ShapeDtypeStruct
    return pl.pallas_call(
        backward_kernel,
        grid_spec=pltpu.PrefetchScalarGridSpec(
            num_scalar_prefetch=1,
            grid=(n,),
            in_specs=[
                pl.BlockSpec((None, rows, 1), per_k),
                pl.BlockSpec((None, 1, rows), per_k),
                whole(cols.shape),
                pl.BlockSpec((features, rows), lanes_s),
                pl.BlockSpec((3 * features, rows), lanes_s),
                pl.BlockSpec((None, tiles, WIN * WIN, HEADS * LANES), lambda k, sk, *_: (sk[k], 0, 0, 0)),
                pl.BlockSpec((features, rows), lanes_s),
                whole(wproj.shape),
                whole(wqkv.shape),
            ],
            out_specs=[
                pl.BlockSpec((3 * features, rows), lanes_s),
                pl.BlockSpec((rows, features), rows_s),
                pl.BlockSpec((rows, features), rows_s),
                pl.BlockSpec((None, count, features), per_k),
                pl.BlockSpec((None, 8, features), per_k),
            ],
            scratch_shapes=[
                pltpu.VMEM((features, rows), BF),
                pltpu.VMEM((features, rows), BF),
                pltpu.VMEM((rows, features), BF),
                pltpu.VMEM((features, rows), F32),
                pltpu.VMEM((6, features, LANES), F32),
            ],
        ),
        out_shape=[
            s((3 * features, total), BF),
            s((total, features), BF),
            s((total, features), BF),
            s((n, count, features), BF),
            s((n, 8, features), F32),
        ],
        cost_estimate=pl.CostEstimate(
            flops=2 * n * rows * features * (4 * features + 5 * rows),
            bytes_accessed=22 * MIB,
            transcendentals=0,
        ),
        compiler_params=pltpu.CompilerParams(vmem_limit_bytes=56 * MIB),
    )(sk, vis, place, cols, x_t, qkv_t, probs, gx1_t, wproj, wqkv)


def shift(x, by, size):
    return lax.ppermute(x, "band", [(i, (i + by) % size) for i in range(size)])


def swap(x, bit, size):
    return lax.ppermute(x, "dp", [(i, i ^ (1 << bit)) for i in range(size)])


def pick(x, index):
    return lax.dynamic_index_in_dim(x, index, 0, keepdims=False)


def reduce_rows(grad, bits, dp, band):
    me, z = lax.axis_index("dp"), lax.axis_index("band")
    for bit in bits:
        mine = (me >> bit) & 1
        halves = grad.reshape(2, grad.shape[0] // 2, grad.shape[1])
        got = swap(pick(halves, 1 - mine), bit, dp)
        grad = (pick(halves, mine).astype(F32) + got.astype(F32)).astype(BF)
    parts = grad.reshape(band, grad.shape[0] // band, grad.shape[1])
    total = pick(parts, z).astype(F32)
    for d in range(1, band):
        total = total + shift(pick(parts, (z + d) % band), d, band).astype(F32)
    return total.astype(BF)


def gather_rows(share, bits, dp, band):
    me, z = lax.axis_index("dp"), lax.axis_index("band")
    full = jnp.zeros((band,) + share.shape, share.dtype)
    full = lax.dynamic_update_index_in_dim(full, share, z, 0)
    for d in range(1, band):
        full = lax.dynamic_update_index_in_dim(full, shift(share, d, band), (z - d) % band, 0)
    full = full.reshape(band * share.shape[0], share.shape[1])
    for bit in reversed(bits):
        mine = (me >> bit) & 1
        got = swap(full, bit, dp)
        full = jnp.where(
            mine == 0, jnp.concatenate([full, got], 0), jnp.concatenate([got, full], 0)
        )
    return full


def reduce_small(x, bits, dp, band):
    for bit in bits:
        x = x + swap(x, bit, dp)
    total = x
    step = 1
    while step < band:
        total = total + lax.ppermute(total, "band", [(i, i ^ step) for i in range(band)])
        step *= 2
    return total


def body(
    dp, band,
    visible, clip_long, patch_order, embed_weight, embed_bias, mask_token,
    norm1_gain, norm1_bias, qkv_weight, qv_bias, proj_weight, proj_bias,
    norm2_gain, norm2_bias, fc1_weight, fc1_bias, fc2_weight, fc2_bias, cotangent,
):
    features = embed_weight.shape[1]
    hidden = fc1_weight.shape[1]
    total = patch_order.shape[1]
    rows = total // band
    vis_count = visible.shape[0]
    count = -(-vis_count // 16) * 16
    z = lax.axis_index("band")
    bits = []
    while (1 << len(bits)) < dp:
        bits.append(len(bits))

    order = patch_order[0]
    half = vis_count // 2
    middle = total // 2
    visible_at = jnp.where(
        clip_long[0] == 1,
        order[:vis_count],
        jnp.concatenate([order[:half], order[middle : middle + vis_count - half]]),
    )
    note = jnp.concatenate(
        [visible_at, jnp.full((rows - vis_count - 1,), -1, jnp.int32), clip_long]
    ).reshape(1, rows)
    notes = jnp.concatenate([note] + [shift(note, d, band) for d in range(1, band)], axis=0)
    flags = notes[:, rows - 1]
    vis = jnp.where(jnp.arange(rows)[None, :] < vis_count, notes, -1)[:, :, None]
    sk = (z - jnp.arange(band, dtype=jnp.int32)) % band

    embedded = (
        jnp.dot(visible, embed_weight, preferred_element_type=F32) + embed_bias
    ).astype(BF)
    embedded = jnp.pad(embedded, ((0, count - vis_count), (0, 0)))
    ring = [embedded]
    for _ in range(1, band):
        ring.append(shift(ring[-1], 1, band))
    emb = jnp.stack(ring)

    rowid = z * rows + jnp.arange(rows, dtype=jnp.int32)
    place_long, time_long, column = row_layout(True, rowid, total)
    place_short, time_short, _ = row_layout(False, rowid, total)
    place = jnp.where(flags[:, None] == 1, place_long[None, :], place_short[None, :])[:, None, :]
    pos_long = positions_t(time_long, column, features)
    pos_short = positions_t(time_short, column, features)

    cols = jnp.stack(
        [
            mask_token, norm1_gain, norm1_bias, qv_bias[0], qv_bias[1], proj_bias,
            norm2_gain, norm2_bias, fc2_bias,
        ]
        + [jnp.zeros_like(fc2_bias)] * 7,
        axis=1,
    )
    weights = (qkv_weight.T, proj_weight.T, fc1_weight.T, fc1_weight, fc2_weight.T, fc2_weight)
    block_out, x_t, qkv_t, probs, o_t, act_t, gh_t, c, gx1_t, sums_f = forward(
        sk, flags, emb, vis, place, pos_long, pos_short, cols, fc1_bias[:, None], cotangent, weights
    )

    fc2_grad = product(act_t, cotangent)
    fc1_grad_t, fc1b_grad = product(gh_t, c, with_bias=True)
    gqkv_t, a, gy, gemb, sums_b = backward(
        sk, count, vis, place, cols, x_t, qkv_t, probs, gx1_t, proj_weight, qkv_weight
    )
    qkv_grad_t = product(gqkv_t, a)
    proj_grad = product(o_t, gy)

    back = gemb[1]
    for k in list(range(2, band)) + [0]:
        back = shift(back, 1, band) + gemb[k]
    back = back[:vis_count]
    embed_grad = jnp.einsum("ve,vd->ed", visible, back, preferred_element_type=F32).astype(BF)
    visible_grad = jnp.einsum(
        "vd,ed->ve", back, embed_weight, preferred_element_type=F32
    ).astype(BF)

    sums_f = jnp.sum(sums_f, axis=0)
    sums_b = jnp.sum(sums_b, axis=0)
    small = jnp.concatenate(
        [
            sums_f[0:2],
            sums_b[0:6],
            jnp.sum(cotangent, axis=0, dtype=F32)[None],
            jnp.sum(back, axis=0, dtype=F32)[None],
            fc1b_grad.reshape(hidden // features, features),
        ],
        axis=0,
    )
    small = reduce_small(small, bits, dp, band)

    outs = []
    for grad in (fc2_grad, fc1_grad_t, qkv_grad_t, proj_grad, embed_grad):
        share = reduce_rows(grad, bits, dp, band)
        outs.append(gather_rows(share, bits, dp, band))
    fc2_grad, fc1_grad_t, qkv_grad_t, proj_grad, embed_grad = outs

    return (
        block_out,
        visible_grad,
        embed_grad.astype(F32),
        small[9],
        small[7],
        small[5],
        small[6],
        qkv_grad_t.T.astype(F32),
        jnp.stack([small[3], small[4]]),
        proj_grad.astype(F32),
        small[2],
        small[0],
        small[1],
        fc1_grad_t.T.astype(F32),
        small[10:].reshape(hidden),
        fc2_grad.astype(F32),
        small[8],
    )


def solution(mesh):
    split = P(("dp", "band"), None)
    in_specs = (split, P(("dp", "band")), split) + (P(),) * 15 + (split,)
    out_specs = (split, split) + (P(),) * 15
    return jax.shard_map(
        functools.partial(body, mesh.shape["dp"], mesh.shape["band"]),
        mesh=mesh,
        in_specs=in_specs,
        out_specs=out_specs,
        check_vma=False,
    )
```

```python
import functools

import jax
import jax.numpy as jnp
from jax import lax
from jax.experimental import pallas as pl
from jax.experimental.pallas import tpu as pltpu
from jax.sharding import PartitionSpec as P

HEADS = 16
FREQ = 8
WIN = 4
EPS = 1e-06
BF = jnp.bfloat16
F32 = jnp.float32
LANES = 128
MIB = 1024 * 1024
SCALE = 1.0
PARAMS = pltpu.CompilerParams(vmem_limit_bytes=60 * MIB)


def takes(microseconds):
    return pl.CostEstimate(
        flops=0, bytes_accessed=int(SCALE * microseconds * 3.3e6), transcendentals=0
    )


def row_layout(is_long, rowid, row_count):
    quarter = row_count // 4
    span = row_count // (2 * FREQ)
    halfspan = span // 2
    target = rowid // quarter
    inner = rowid % quarter
    column = target // 2 * WIN + inner % WIN
    local = inner // WIN
    halves = target % 2
    if is_long:
        frame_time = halves * span + local
        frame = frame_time
    else:
        frame_time = halves * halfspan + local % halfspan
        frame = local // halfspan * span + frame_time
    return frame * FREQ + column, frame_time, column


def sincos_rows(places, features):
    halfway = features // 2
    omega = 1.0 / 10000.0 ** (jnp.arange(halfway, dtype=F32) / halfway)
    angles = omega[:, None] * places.astype(F32)[None, :]
    return jnp.concatenate([jnp.sin(angles), jnp.cos(angles)], axis=0)


def positions_t(frame_time, column, features):
    return jnp.concatenate(
        [sincos_rows(frame_time, features // 2), sincos_rows(column, features // 2)], axis=0
    )


def mm(a, b):
    return lax.dot_general(a, b, (((1,), (0,)), ((), ())), preferred_element_type=F32)


def mm_nt(a, b):
    return lax.dot_general(a, b, (((1,), (1,)), ((), ())), preferred_element_type=F32)


def window_of_lane(rows, columns):
    lane = lax.broadcasted_iota(jnp.int32, (rows, columns), 1)
    return (lane % LANES) // (WIN * WIN)


def compact(square, win):
    size = WIN * WIN
    out = square[0:size]
    for w in range(1, LANES // size):
        out = jnp.where(win == w, square[w * size : (w + 1) * size], out)
    return out


def expand(rows, win):
    size = WIN * WIN
    return jnp.concatenate(
        [jnp.where(win == w, rows, 0.0).astype(BF) for w in range(LANES // size)], axis=0
    )


def stacked(wide):
    return jnp.concatenate(
        [wide[:, j * LANES : (j + 1) * LANES] for j in range(wide.shape[1] // LANES)], axis=0
    )


def heads_apart(group, width):
    count = LANES // width
    blocks = []
    for j in range(count):
        parts = []
        if j:
            parts.append(jnp.zeros((j * width, LANES), BF))
        parts.append(group[j * width : (j + 1) * width])
        if j < count - 1:
            parts.append(jnp.zeros(((count - 1 - j) * width, LANES), BF))
        blocks.append(jnp.concatenate(parts, axis=0))
    return jnp.concatenate(blocks, axis=1)


def heads_of(wide, width):
    return jnp.concatenate(
        [
            wide[j * width : (j + 1) * width, j * LANES : (j + 1) * LANES]
            for j in range(LANES // width)
        ],
        axis=0,
    )


def normalize_t(x):
    count = x.shape[0]
    center = x - jnp.sum(x, axis=0, keepdims=True) * (1.0 / count)
    var = jnp.sum(center * center, axis=0, keepdims=True) * (1.0 / count)
    scale = lax.rsqrt(var + EPS)
    return center * scale, scale


def normalize_back_t(grad, unit, scale, gain):
    count = grad.shape[0]
    inner = grad * gain
    mean = jnp.sum(inner, axis=0, keepdims=True) * (1.0 / count)
    mixed = jnp.sum(inner * unit, axis=0, keepdims=True) * (1.0 / count)
    return scale * (inner - mean - unit * mixed)


def mm_tn(a, b):
    return lax.dot_general(a, b, (((0,), (0,)), ((), ())), preferred_element_type=F32)


def mm_tt(a, b):
    return lax.dot_general(a, b, (((0,), (1,)), ((), ())), preferred_element_type=F32)


def lane_sums(acc):
    return jnp.sum(acc.T, axis=0, keepdims=True)


def lanes(t):
    return slice(t * LANES, (t + 1) * LANES)


def copies(pairs, sems, start=True):
    made = [pltpu.make_async_copy(a, b, sems.at[i]) for i, (a, b) in enumerate(pairs)]
    if start:
        for copy in made:
            copy.start()
    return made


C_MASK, C_G1, C_B1, C_QB, C_VB, C_PB, C_G2, C_B2, C_F2B, C_EB, C_F1B = range(11)
N_COLS = 16
N_SAVED = 10
NOTE = 8


class Block:
    def __init__(self, features, rows):
        self.features, self.rows = features, rows
        self.tiles = rows // LANES
        self.half = rows // 2
        self.per_half = self.tiles // 2
        self.groups = features // LANES
        self.width = features // HEADS
        self.factor = self.width ** (-0.5)
        self.chunk = features // 2

    def of_half(self, h):
        return range(h * self.per_half, (h + 1) * self.per_half)

    def part(self, h):
        return slice(h * self.half, (h + 1) * self.half)

    def chunks(self, size):
        return [slice(i, i + self.chunk) for i in range(0, size, self.chunk)]

    def group(self, base, g):
        return slice(base + g * LANES, base + (g + 1) * LANES)


def forward_kernel(vis_count, aliased, sk, *refs):
    (v, places, cols, cot_hbm, *w_hbm) = refs[:11]
    refs = refs[11 + (N_SAVED if aliased else 0) :]
    out_hbm, refs = refs[:N_SAVED], refs[N_SAVED:]
    sums, refs = refs[0], refs[1:]
    saved, refs = refs[:N_SAVED], refs[N_SAVED:]
    (x_t, a_t, qkv_t, probs, o_t, act_t, gh_t, c_t, x1_t, ch_t) = saved
    held, refs = refs[:7], refs[7:]
    (wemb, pos_long, pos_short, wqkv, wproj, w1, w2) = held
    (v_pad, colb, e_t, wide, fill, cot, cot_t, scores, acc, in_sems, out_sems, half_sems, cot_sem) = refs
    features, rows = x_t.shape
    k = Block(features, rows)
    source = sk[0]
    always = source >= 0
    row_at = pl.ds(pl.multiple_of(source * rows, rows), rows)

    loads = copies(zip(w_hbm, held), in_sems, start=False)
    loads[0].start()
    cot_load = pltpu.make_async_copy(cot_hbm.at[row_at, :], cot, cot_sem.at[0])
    cot_load.start()
    for copy in loads[1:]:
        copy.start()
    views = [ref.at[source] if i == 3 else ref.at[:, row_at] for i, ref in enumerate(out_hbm)]
    stores = [
        None if i in (5, 6) else pltpu.make_async_copy(a, b, out_sems.at[i])
        for i, (a, b) in enumerate(zip(saved, views))
    ]
    halves = []
    for h in range(2):
        at = pl.ds(pl.multiple_of(source * rows + h * k.half, k.half), k.half)
        pairs = [(saved[i].at[:, k.part(h)], out_hbm[i].at[:, at]) for i in (5, 6)]
        halves.append(copies(pairs, half_sems.at[h], start=False))

    count = v.shape[0]
    note = v[count - 16 : count, 0:rows].astype(F32)
    is_long = note[NOTE + 2 : NOTE + 3, :] > 0.5
    loads[0].wait()

    @pl.when(always)
    def _():
        columns = cols[...].T
        for i in range(C_F1B + 4):
            colb[i] = jnp.broadcast_to(columns[:, i : i + 1], (features, LANES))
        v_pad[0:count, :] = v[...]
        v_pad[count:, :] = jnp.zeros((v_pad.shape[0] - count, v_pad.shape[1]), BF)
        embedded = mm_tt(wemb[...], v_pad[...])
        note_t = note.T
        index = lax.broadcasted_iota(jnp.int32, (rows, 1), 0)
        patch = note_t[:, NOTE : NOTE + 1] * 64.0 + note_t[:, NOTE + 1 : NOTE + 2]
        patch = jnp.where(index < vis_count, patch.astype(jnp.int32), -1)
        place = jnp.where(is_long, places[0:1, :], places[1:2, :])
        for t in range(k.tiles):
            chosen = jnp.where(patch == place[:, lanes(t)], 1.0, 0.0)
            ch_t[:, lanes(t)] = chosen.astype(BF)
            fill[:, lanes(t)] = jnp.sum(chosen, axis=0, keepdims=True)
        for t in range(k.tiles):
            e_t[:, lanes(t)] = (embedded[:, lanes(t)] + colb[C_EB]).astype(BF)
        for h in range(2):
            wide[:, k.part(h)] = mm(e_t[...], ch_t[:, k.part(h)])

    stores[9].start()
    cot_load.wait()
    for copy in loads[1:4]:
        copy.wait()

    @pl.when(always)
    def _():
        def entry(t):
            pos = jnp.where(is_long[:, lanes(t)], pos_long[:, lanes(t)], pos_short[:, lanes(t)])
            start = (wide[:, lanes(t)] + (1.0 - fill[:, lanes(t)]) * colb[C_MASK]) + pos
            start = start.astype(BF)
            x_t[:, lanes(t)] = start
            unit, _scale = normalize_t(start.astype(F32))
            a_t[:, lanes(t)] = (unit * colb[C_G1] + colb[C_B1]).astype(BF)
            cot_t[:, lanes(t)] = cot[t * LANES : (t + 1) * LANES, :].T

        def project(h):
            for n, chunk in enumerate(k.chunks(3 * features)):
                prod = mm_tn(wqkv[:, chunk], a_t[:, k.part(h)])
                bias = (C_QB, None, C_VB)[n // 2]
                for u, t in enumerate(k.of_half(h)):
                    piece = prod[:, lanes(u)]
                    if bias is not None:
                        piece = piece + colb[bias, slice((n % 2) * k.chunk, (n % 2 + 1) * k.chunk)]
                    qkv_t[chunk, lanes(t)] = piece.astype(BF)

        for t in k.of_half(0):
            entry(t)
        project(0)
        for t in k.of_half(1):
            entry(t)
        project(1)

    for i in range(3):
        stores[i].start()

    @pl.when(always)
    def _():
        win = window_of_lane(WIN * WIN, 4 * LANES)

        def score(t):
            for g in range(k.groups):
                q_g = qkv_t[k.group(0, g), lanes(t)]
                k_g = qkv_t[k.group(features, g), lanes(t)]
                scores[t * k.groups + g] = compact(mm(k_g.T, heads_apart(q_g, k.width)), win)

        def soften(t):
            for g in range(k.groups):
                logits = scores[t * k.groups + g] * k.factor
                shifted = jnp.exp(logits - jnp.max(logits, axis=0, keepdims=True))
                prob = shifted / jnp.sum(shifted, axis=0, keepdims=True)
                probs[t, :, g * 4 * LANES : (g + 1) * 4 * LANES] = prob

        def mix(t):
            for g in range(k.groups):
                prob = probs[t, :, g * 4 * LANES : (g + 1) * 4 * LANES]
                mixed = mm(qkv_t[k.group(2 * features, g), lanes(t)], expand(prob, win))
                o_t[k.group(0, g), lanes(t)] = heads_of(mixed, k.width).astype(BF)

        score(0)
        for t in range(k.tiles):
            if t + 1 < k.tiles:
                score(t + 1)
            soften(t)
            mix(t)

    stores[3].start()
    stores[4].start()
    loads[4].wait()

    @pl.when(always)
    def _():
        def norm2(t, grown):
            x1 = x_t[:, lanes(t)].astype(F32) + (grown + colb[C_PB])
            x1_t[:, lanes(t)] = x1
            unit, _scale = normalize_t(x1)
            c_t[:, lanes(t)] = (unit * colb[C_G2] + colb[C_B2]).astype(BF)

        grown = [mm_tn(wproj[...], o_t[:, k.part(h)]) for h in range(2)]
        for h in range(2):
            for u, t in enumerate(k.of_half(h)):
                norm2(t, grown[h][:, lanes(u)])

    stores[7].start()
    stores[8].start()
    loads[5].wait()
    loads[6].wait()

    for h in range(2):

        @pl.when(always)
        def _():
            for n, chunk in enumerate(k.chunks(w1.shape[1])):
                hidden = mm_tn(w1[:, chunk], c_t[:, k.part(h)])
                gact = mm(w2[chunk, :], cot_t[:, k.part(h)])
                rows_of = slice((n % 2) * k.chunk, (n % 2 + 1) * k.chunk)
                for u, t in enumerate(k.of_half(h)):
                    own = hidden[:, lanes(u)] + colb[C_F1B + n // 2, rows_of]
                    cumulative = 0.5 * (1.0 + lax.erf(own * 0.7071067811865476))
                    act_t[chunk, lanes(t)] = (own * cumulative).astype(BF)
                    slope = cumulative + own * jnp.exp(-0.5 * own * own) * 0.3989422804014327
                    gh_t[chunk, lanes(t)] = (gact[:, lanes(u)] * slope).astype(BF)

        for copy in halves[h]:
            copy.start()

    for t in range(k.tiles):
        own = cot_t[:, lanes(t)].astype(F32)
        if t == 0:
            acc[...] = own
        else:
            acc[...] += own
    sums[...] = jnp.zeros_like(sums)
    sums[0:1, :] = lane_sums(acc[...])
    sums[1:2, :] = fill[...]
    for copy in stores:
        if copy is not None:
            copy.wait()
    for copy in halves[0] + halves[1]:
        copy.wait()


def backward_kernel(aliased, sk, *refs):
    (kept, cols, *in_hbm) = refs[:9]
    w_hbm = refs[9:12]
    refs = refs[12 + (2 if aliased else 0) :]
    gqkv_hbm, gy_hbm, gemb, sums = refs[:4]
    (gh_t, x1_t, cot, qkv_t, probs, x_t, ch_t) = refs[4:11]
    (w1, wproj, wqkv) = refs[11:14]
    (gqkv_t, gy_t, colb, gx1_t, go_t, gx_t, hot, acc, in_sems, w_sems, out_sems) = refs[14:]
    features, rows = x_t.shape
    k = Block(features, rows)
    source = sk[0]
    always = source >= 0
    row_at = pl.ds(pl.multiple_of(source * rows, rows), rows)
    views = []
    for i, ref in enumerate(in_hbm):
        views.append(ref.at[row_at, :] if i == 2 else ref.at[source] if i == 4 else ref.at[:, row_at])
    pairs = list(zip(views, refs[4:11]))
    wanted = list(zip(w_hbm, refs[11:14]))
    loads = copies(pairs, in_sems, start=False)
    w_loads = copies(wanted, w_sems, start=False)
    for copy in (loads[0], w_loads[0], *loads[1:3], w_loads[1], *loads[3:], w_loads[2]):
        copy.start()
    stores = copies(
        [(gqkv_t, gqkv_hbm.at[:, row_at]), (gy_t, gy_hbm.at[:, row_at])], out_sems, start=False
    )

    def add(i, at, value, begin):
        if begin:
            acc[i, at] = value
        else:
            acc[i, at] += value

    everything = slice(0, features)
    for i in range(3):
        loads[i].wait()
    w_loads[0].wait()
    w_loads[1].wait()

    @pl.when(always)
    def _():
        columns = cols[...].T
        for n, i in enumerate((C_G1, C_G2)):
            colb[n] = jnp.broadcast_to(columns[:, i : i + 1], (features, LANES))

        def norm2_back(t, gc):
            unit, scale = normalize_t(x1_t[:, lanes(t)])
            add(7, everything, gc * unit, t == 0)
            add(8, everything, gc, t == 0)
            own = cot[t * LANES : (t + 1) * LANES, :].T.astype(F32)
            gx1 = own + normalize_back_t(gc, unit, scale, colb[1])
            gx1_t[:, lanes(t)] = gx1
            low = gx1.astype(BF)
            gy_t[:, lanes(t)] = low
            add(0, everything, low.astype(F32), t == 0)

        gc = [mm(w1[...], gh_t[:, k.part(h)]) for h in range(2)]
        for h in range(2):
            for u, t in enumerate(k.of_half(h)):
                norm2_back(t, gc[h][:, lanes(u)])
        for h in range(2):
            go_t[:, k.part(h)] = mm(wproj[...], gy_t[:, k.part(h)]).astype(BF)

    stores[1].start()
    loads[3].wait()
    loads[4].wait()

    @pl.when(always)
    def _():
        win = window_of_lane(WIN * WIN, 4 * LANES)

        def probs_grad(t):
            for g in range(k.groups):
                v_g = qkv_t[k.group(2 * features, g), lanes(t)]
                go_g = go_t[k.group(0, g), lanes(t)]
                hot[t * k.groups + g] = compact(mm(v_g.T, heads_apart(go_g, k.width)), win)

        def score_grad(t):
            for g in range(k.groups):
                gp = hot[t * k.groups + g]
                prob = probs[t, :, g * 4 * LANES : (g + 1) * 4 * LANES]
                hot[t * k.groups + g] = prob * (gp - jnp.sum(gp * prob, axis=0, keepdims=True))

        def row_grads(t):
            products = []
            for g in range(k.groups):
                q_g = qkv_t[k.group(0, g), lanes(t)]
                k_g = qkv_t[k.group(features, g), lanes(t)]
                go_g = go_t[k.group(0, g), lanes(t)]
                gs = expand(hot[t * k.groups + g], win)
                prob = expand(probs[t, :, g * 4 * LANES : (g + 1) * 4 * LANES], win)
                products.append(
                    (mm(k_g, gs), mm_nt(q_g, stacked(gs)), mm_nt(go_g, stacked(prob)))
                )
            for g, (gq, gk, gv) in enumerate(products):
                gq = (heads_of(gq, k.width) * k.factor).astype(BF)
                gk = (heads_of(gk, k.width) * k.factor).astype(BF)
                gv = heads_of(gv, k.width).astype(BF)
                gqkv_t[k.group(0, g), lanes(t)] = gq
                gqkv_t[k.group(features, g), lanes(t)] = gk
                gqkv_t[k.group(2 * features, g), lanes(t)] = gv
                add(1, k.group(0, g), gq.astype(F32), t == 0)
                add(2, k.group(0, g), gv.astype(F32), t == 0)

        probs_grad(0)
        for t in range(k.tiles):
            if t + 1 < k.tiles:
                probs_grad(t + 1)
            score_grad(t)
            row_grads(t)

    stores[0].start()
    loads[5].wait()
    loads[6].wait()
    w_loads[2].wait()

    @pl.when(always)
    def _():
        def norm1_back(t, ga):
            unit, scale = normalize_t(x_t[:, lanes(t)].astype(F32))
            add(3, everything, ga * unit, t == 0)
            add(4, everything, ga, t == 0)
            low = (gx1_t[:, lanes(t)] + normalize_back_t(ga, unit, scale, colb[0])).astype(BF)
            gx_t[:, lanes(t)] = low
            own = low.astype(F32)
            filled = kept[1:2, lanes(t)]
            add(5, everything, own * (1.0 - filled), t == 0)
            add(6, everything, own * filled, t == 0)

        ga = [mm(wqkv[...], gqkv_t[:, k.part(h)]) for h in range(2)]
        for h in range(2):
            for u, t in enumerate(k.of_half(h)):
                norm1_back(t, ga[h][:, lanes(u)])

    @pl.when(always)
    def _():
        chosen = mm_nt(ch_t[...], gx_t[...]).astype(BF)
        gemb[...] = chosen[0 : gemb.shape[0]]
        sums[...] = jnp.zeros_like(sums)
        for i in range(9):
            sums[i : i + 1, :] = lane_sums(acc[i])

    for copy in stores:
        copy.wait()


def whole(shape):
    zeros = (0,) * len(shape)
    return pl.BlockSpec(shape, lambda *_: zeros)


FAR = pl.BlockSpec(memory_space=pltpu.HBM)


def forward(sk, v, places, cols, cot, weights, vis_count, old):
    rows = places.shape[1]
    features = cols.shape[1]
    total = cot.shape[0]
    hidden = weights[-1].shape[0]
    tiles = rows // LANES
    wide_probs = HEADS * LANES
    s = jax.ShapeDtypeStruct
    saved = [
        ((features,), BF),
        ((features,), BF),
        ((3 * features,), BF),
        None,
        ((features,), BF),
        ((hidden,), BF),
        ((hidden,), BF),
        ((features,), BF),
        ((features,), F32),
        ((rows,), BF),
    ]
    probs = (tiles, WIN * WIN, wide_probs)
    out_shape = [
        s((total // rows,) + probs, F32) if x is None else s(x[0] + (total,), x[1]) for x in saved
    ] + [s((8, features), F32)]
    scratch = [
        pltpu.VMEM(probs, F32) if x is None else pltpu.VMEM(x[0] + (rows,), x[1]) for x in saved
    ] + [
        *[pltpu.VMEM(w.shape, w.dtype) for w in weights],
        pltpu.VMEM((rows, v.shape[1]), BF),
        pltpu.VMEM((C_F1B + 4, features, LANES), F32),
        pltpu.VMEM((features, rows), BF),
        pltpu.VMEM((features, rows), F32),
        pltpu.VMEM((1, rows), F32),
        pltpu.VMEM((rows, features), BF),
        pltpu.VMEM((features, rows), BF),
        pltpu.VMEM((tiles * features // LANES, WIN * WIN, 4 * LANES), F32),
        pltpu.VMEM((features, LANES), F32),
        pltpu.SemaphoreType.DMA((len(weights),)),
        pltpu.SemaphoreType.DMA((N_SAVED,)),
        pltpu.SemaphoreType.DMA((2, 2)),
        pltpu.SemaphoreType.DMA((1,)),
    ]
    old = list(old or ())
    ins = [v, places, cols, cot, *weights]
    return pl.pallas_call(
        functools.partial(forward_kernel, vis_count, bool(old)),
        grid_spec=pltpu.PrefetchScalarGridSpec(
            num_scalar_prefetch=1,
            grid=(1,),
            in_specs=[whole(v.shape), whole(places.shape), whole(cols.shape)]
            + [FAR] * (1 + len(weights) + len(old)),
            out_specs=[FAR] * N_SAVED + [whole((8, features))],
            scratch_shapes=scratch,
        ),
        out_shape=out_shape,
        input_output_aliases={1 + len(ins) + i: i for i in range(len(old))},
        cost_estimate=takes(13.5),
        compiler_params=PARAMS,
    )(sk, *ins, *old)


def backward(sk, count, kept, cols, saved, weights, old):
    gh_t, x1_t, cot, qkv_t, probs, x_t, ch_t = saved
    features, total = x_t.shape
    rows = ch_t.shape[0]
    hidden = gh_t.shape[0]
    tiles = rows // LANES
    s = jax.ShapeDtypeStruct
    old = list(old or ())
    ins = [kept, cols, *saved, *weights]
    return pl.pallas_call(
        functools.partial(backward_kernel, bool(old)),
        grid_spec=pltpu.PrefetchScalarGridSpec(
            num_scalar_prefetch=1,
            grid=(1,),
            in_specs=[whole(kept.shape), whole(cols.shape)]
            + [FAR] * (len(saved) + len(weights) + len(old)),
            out_specs=[FAR, FAR, whole((count, features)), whole((16, features))],
            scratch_shapes=[
            pltpu.VMEM((hidden, rows), BF),
            pltpu.VMEM((features, rows), F32),
            pltpu.VMEM((rows, features), BF),
            pltpu.VMEM((3 * features, rows), BF),
            pltpu.VMEM(probs.shape[1:], F32),
            pltpu.VMEM((features, rows), BF),
            pltpu.VMEM((rows, rows), BF),
        ]
        + [pltpu.VMEM(w.shape, BF) for w in weights]
        + [
            pltpu.VMEM((3 * features, rows), BF),
            pltpu.VMEM((features, rows), BF),
            pltpu.VMEM((2, features, LANES), F32),
            pltpu.VMEM((features, rows), F32),
            pltpu.VMEM((features, rows), BF),
            pltpu.VMEM((features, rows), BF),
            pltpu.VMEM((tiles * features // LANES, WIN * WIN, 4 * LANES), F32),
            pltpu.VMEM((9, features, LANES), F32),
            pltpu.SemaphoreType.DMA((len(saved),)),
            pltpu.SemaphoreType.DMA((len(weights),)),
            pltpu.SemaphoreType.DMA((2,)),
        ],
        ),
        out_shape=[
            s((3 * features, total), BF),
            s((features, total), BF),
            s((count, features), BF),
            s((16, features), F32),
        ],
        input_output_aliases={1 + len(ins) + i: i for i in range(len(old))},
        cost_estimate=takes(12.0),
        compiler_params=PARAMS,
    )(sk, *ins, *old)


def output_kernel(x1_t, act_t, w2, bias, out):
    for t in range(x1_t.shape[1] // LANES):
        if t % 2 == 0:
            grown = mm_tn(w2[...], act_t[:, t * LANES : (t + 2) * LANES])
        total = x1_t[:, lanes(t)] + (grown[:, lanes(t % 2)] + bias[...])
        out[t * LANES : (t + 1) * LANES, :] = total.astype(BF).T


def output(x1_t, act_t, w2, bias):
    features, total = x1_t.shape
    hidden = act_t.shape[0]
    rows = features
    return pl.pallas_call(
        output_kernel,
        grid=(total // rows,),
        in_specs=[
            pl.BlockSpec((features, rows), lambda i: (0, i)),
            pl.BlockSpec((hidden, rows), lambda i: (0, i)),
            whole(w2.shape),
            whole((features, 1)),
        ],
        out_specs=pl.BlockSpec((rows, features), lambda i: (i, 0)),
        out_shape=jax.ShapeDtypeStruct((total, features), BF),
        cost_estimate=takes(11.0),
        compiler_params=PARAMS,
    )(x1_t, act_t, w2, bias)


def to_halves(core, low, send, keep, at=slice(None)):
    cut = low.shape[1] // 2
    left, right = low[:, :cut], low[:, cut:]
    send[at, :] = jnp.where(core == 0, right, left)
    keep[at, :] = jnp.where(core == 0, left, right)


def ff_kernel(steps, core, act, cot, c, gh, send, keep, bias):
    i = pl.program_id(0)

    @pl.when(i < steps)
    def _():
        to_halves(core[0], mm(act[...], cot[...]).astype(BF), send, keep)

    @pl.when(i >= steps)
    def _():
        to_halves(core[0], mm_nt(c[...], gh[...]).astype(BF), send, keep)
        total = gh[:, 0:LANES].astype(F32)
        for t in range(1, gh.shape[1] // LANES):
            total += gh[:, lanes(t)].astype(F32)
        bias[...] = jnp.sum(total.T, axis=0, keepdims=True)


def ff_gradients(core, act_t, cot, c_t, gh_t):
    hidden, total = act_t.shape
    features = cot.shape[1]
    steps = hidden // features
    out = pl.BlockSpec((features, features // 2), lambda i, _: (i, 0))
    first = lambda i, _: (jnp.minimum(i, steps - 1), 0)
    second = lambda i, _: (jnp.maximum(i - steps, 0), 0)
    s = jax.ShapeDtypeStruct
    return pl.pallas_call(
        functools.partial(ff_kernel, steps),
        grid_spec=pltpu.PrefetchScalarGridSpec(
            num_scalar_prefetch=1,
            grid=(2 * steps,),
            in_specs=[
                pl.BlockSpec((features, total), first),
                whole(cot.shape),
                whole(c_t.shape),
                pl.BlockSpec((features, total), second),
            ],
            out_specs=[
                out,
                out,
                pl.BlockSpec((None, 1, features), lambda i, _: (jnp.maximum(i - steps, 0), 0, 0)),
            ],
        ),
        out_shape=[
            s((2 * hidden, features // 2), BF),
            s((2 * hidden, features // 2), BF),
            s((steps, 1, features), F32),
        ],
        cost_estimate=takes(16.0),
        compiler_params=PARAMS,
    )(core, act_t, cot, c_t, gh_t)


def rest_kernel(band, blocks, core, a, gqkv, o, gy, bias, *refs):
    visible, emb, kept, sums = (refs[n * band : (n + 1) * band] for n in range(4))
    send, keep = refs[4 * band :]
    i = pl.program_id(0)
    size = send.shape[0]

    def embed(at):
        total = mm_tn(visible[0][:, at], emb[0][...])
        for n in range(1, band):
            total = total + mm_tn(visible[n][:, at], emb[n][...])
        return total.astype(BF)

    @pl.when(i < blocks)
    def _():
        to_halves(core[0], mm_nt(a[...], gqkv[...]).astype(BF), send, keep)

    @pl.when(i == blocks)
    def _():
        to_halves(core[0], mm_nt(o[...], gy[...]).astype(BF), send, keep)

    @pl.when(i == blocks + 1)
    def _():
        to_halves(core[0], embed(slice(0, size)), send, keep)

    @pl.when(i == blocks + 2)
    def _():
        over = visible[0].shape[1] - size
        to_halves(core[0], embed(slice(size, size + over)), send, keep, slice(0, over))
        ours, cots = sums[0][0:9, :], kept[0][0:1, :]
        for n in range(1, band):
            ours = ours + sums[n][0:9, :]
            cots = cots + kept[n][0:1, :]
        hidden = [bias[n] for n in range(bias.shape[0])]
        used = 10 + bias.shape[0]
        rest = jnp.zeros((size - over - used, send.shape[1] * 2), F32)
        small = jnp.concatenate([ours, cots, *hidden, rest], axis=0)
        to_halves(core[0], small.astype(BF), send, keep, slice(over, size))


def rest_gradients(core, a_t, gqkv_t, o_t, gy_t, bias, visible, emb, kept, sums):
    features, total = a_t.shape
    blocks = gqkv_t.shape[0] // features
    steps = blocks + 3
    out = pl.BlockSpec((features, features // 2), lambda i, _: (i, 0))
    s = jax.ShapeDtypeStruct((steps * features, features // 2), BF)
    lists = (*visible, *emb, *kept, *sums)
    return pl.pallas_call(
        functools.partial(rest_kernel, len(emb), blocks),
        grid_spec=pltpu.PrefetchScalarGridSpec(
            num_scalar_prefetch=1,
            grid=(steps,),
            in_specs=[
                whole(a_t.shape),
                pl.BlockSpec((features, total), lambda i, _: (jnp.minimum(i, blocks - 1), 0)),
                whole(o_t.shape),
                whole(gy_t.shape),
                whole(bias.shape),
            ]
            + [whole(x.shape) for x in lists],
            out_specs=[out, out],
        ),
        out_shape=[s, s],
        cost_estimate=takes(13.0),
        compiler_params=PARAMS,
    )(core, a_t, gqkv_t, o_t, gy_t, bias, *lists)


def done_kernel(count, sides, own, got, own2, got2, *refs):
    outs, held, sems = refs[:-2], refs[-2], refs[-1]
    size = held.shape[1]
    per_half = count // 2
    for b in range(count):
        at = slice((b % per_half) * size, (b % per_half + 1) * size)
        mine = jnp.where(sides[1] == b // per_half, own[at, :], got[at, :])
        theirs = jnp.where(sides[2] == b // per_half, own2[at, :], got2[at, :])
        left = jnp.where(sides[0] == 0, mine, theirs)
        right = jnp.where(sides[0] == 0, theirs, mine)
        held[b, :, : size // 2] = left.astype(F32)
        held[b, :, size // 2 :] = right.astype(F32)
        for copy in done_copies(b, outs, held, sems):
            copy.start()
    for b in range(count):
        for copy in done_copies(b, outs, held, sems):
            copy.wait()


def done_copies(b, outs, held, sems):
    size = held.shape[1]
    row, place = 0, []
    for n, out in enumerate(outs):
        high, wide = out.shape
        for j in range(wide // size):
            for i in range(0, high, size):
                place.append((row, n, i, j * size, min(size, high - i)))
                row += min(size, high - i)
    made = []
    for n, (row, which, i, j, high) in enumerate(place):
        if row // size == b:
            made.append(
                pltpu.make_async_copy(
                    held.at[b, pl.ds(row % size, high), :],
                    outs[which].at[pl.ds(i, high), pl.ds(j, size)],
                    sems.at[n],
                )
            )
    return made


def done(sides, own, got, own2, got2, shapes):
    size = 2 * own.shape[1]
    count = 2 * own.shape[0] // size
    return pl.pallas_call(
        functools.partial(done_kernel, count),
        grid_spec=pltpu.PrefetchScalarGridSpec(
            num_scalar_prefetch=1,
            grid=(1,),
            in_specs=[whole(own.shape)] * 4,
            out_specs=[FAR] * len(shapes),
            scratch_shapes=[
                pltpu.VMEM((count, size, size), F32),
                pltpu.SemaphoreType.DMA((count + 2,)),
            ],
        ),
        out_shape=[jax.ShapeDtypeStruct(x, F32) for x in shapes],
        cost_estimate=takes(6.0),
        compiler_params=PARAMS,
    )(sides, own, got, own2, got2)


def add_rows(terms, starts, size):
    total = 0.0
    for term, start in zip(terms, starts):
        total = total + lax.dynamic_slice_in_dim(term, start, size, 0).astype(F32)
    return total.astype(BF)


def join_rows(side, own, got):
    return jnp.where(
        side == 0, jnp.concatenate([own, got], axis=0), jnp.concatenate([got, own], axis=0)
    )


def shift(x, by, size):
    return lax.ppermute(x, "band", [(i, (i + by) % size) for i in range(size)])


def after(x, *others):
    return lax.optimization_barrier((x, *others))[0]


class Ring:
    def __init__(self, dp, band):
        me, z = lax.axis_index("dp"), lax.axis_index("band")
        self.dp = dp
        bits = []
        while (2 << len(bits)) < dp:
            bits.append(len(bits) + 1)
        self.stages = []
        sides = []
        for up, down in zip(bits, reversed(bits)):
            pairs = [(i, i ^ (1 << (down if i & 1 else up))) for i in range(dp)]
            both = ((me >> up) & 1, (me >> down) & 1)
            sides.append(both)
            self.stages.append(("dp", pairs, jnp.where(me & 1 == 1, both[1], both[0])))
        step = 1
        while step < band:
            pairs = [(i, i ^ step) for i in range(band)]
            side = (z // step) & 1
            sides.append((side, side))
            self.stages.append(("band", pairs, side))
            step *= 2
        core = me & 1
        self.core = core.astype(jnp.int32)[None]
        first = sides[0]
        mine = jnp.where(core == 1, first[1], first[0])
        theirs = jnp.where(core == 1, first[0], first[1])
        self.sides = jnp.stack([core, mine, theirs]).astype(jnp.int32)

    def swap_cores(self, x):
        return lax.ppermute(x, "dp", [(i, i ^ 1) for i in range(self.dp)])

    def swap(self, x, i):
        axis, pairs, _side = self.stages[i]
        return lax.ppermute(x, axis, pairs)


class Sum:
    def __init__(self, ring, keep, send):
        self.ring = ring
        zero = jnp.int32(0)
        self.terms, self.starts = [keep], [zero, zero]
        self.base, self.size = zero, keep.shape[0]
        self.stage = 0
        self.last = len(ring.stages)
        self.flight = [ring.swap_cores(send)]

    def rows(self, start):
        return add_rows(self.terms, [start - x for x in self.starts], self.size)

    def down(self):
        self.terms += self.flight
        side = self.ring.stages[self.stage][2].astype(jnp.int32)
        self.size //= 2
        send = self.rows(self.base + (1 - side) * self.size)
        self.base = self.base + side * self.size
        self.flight = [self.ring.swap(send, self.stage)]
        self.starts.append(self.base)
        self.stage += 1
        return send

    def turn(self):
        self.terms += self.flight
        self.own = self.rows(self.base)
        self.stage = self.last - 1
        self.flight = [self.ring.swap(self.own, self.stage)]
        return self.own

    def up(self):
        side = self.ring.stages[self.stage][2]
        self.own = join_rows(side, self.own, self.flight[0])
        self.stage -= 1
        self.flight = [self.ring.swap(self.own, self.stage)]
        return self.own

    def swap_cores(self):
        self.halves = (self.own, self.flight[0])
        self.flight = [self.ring.swap_cores(x) for x in self.halves]
        return self.halves[1]

    def done(self, shapes):
        return done(self.ring.sides, *self.halves, *self.flight, shapes)


class Trip:
    def __init__(self, x, band):
        self.band = band
        self.flight = [shift(x, 1, band)]

    def on(self, own):
        going = self.flight[0] + own
        self.flight = [shift(going, 1, self.band)]
        return going


def meet(flights, *others):
    arrays = [x for f in flights for x in f.flight]
    out = lax.optimization_barrier((*arrays, *others))
    at = 0
    for f in flights:
        f.flight = list(out[at : at + len(f.flight)])
        at += len(f.flight)
    return out[at:]


def body(
    dp, band,
    visible, clip_long, patch_order, embed_weight, embed_bias, mask_token,
    norm1_gain, norm1_bias, qkv_weight, qv_bias, proj_weight, proj_bias,
    norm2_gain, norm2_bias, fc1_weight, fc1_bias, fc2_weight, fc2_bias, cotangent,
):
    features = embed_weight.shape[1]
    hidden = fc1_weight.shape[1]
    total = patch_order.shape[1]
    rows = total // band
    vis_count, enc = visible.shape
    z = lax.axis_index("band")
    ring = Ring(dp, band)
    stages = len(ring.stages)

    order = patch_order[0]
    half = vis_count // 2
    middle = total // 2
    visible_at = jnp.where(
        clip_long[0] == 1,
        order[:vis_count],
        jnp.concatenate([order[:half], order[middle : middle + vis_count - half]]),
    )
    notes = jnp.stack(
        [visible_at // 64, visible_at % 64, jnp.broadcast_to(clip_long, (vis_count,))]
    ).astype(BF)
    notes = jnp.pad(notes, ((0, NOTE - 3), (0, enc - vis_count)), mode="edge")
    block = jnp.concatenate([visible, notes], axis=0)
    sources = [((z - k) % band).astype(jnp.int32)[None] for k in range(band)]
    moving = shift(block, 1, band)

    rowid = z * rows + jnp.arange(rows, dtype=jnp.int32)
    place_long, time_long, column = row_layout(True, rowid, total)
    place_short, time_short, _ = row_layout(False, rowid, total)
    places = jnp.stack([place_long, place_short])
    pos_long = positions_t(time_long, column, features)
    pos_short = positions_t(time_short, column, features)

    cols = jnp.concatenate(
        [
            x.reshape(-1, features)
            for x in (
                mask_token, norm1_gain, norm1_bias, qv_bias, proj_bias,
                norm2_gain, norm2_bias, fc2_bias, embed_bias, fc1_bias, jnp.zeros_like(fc2_bias),
            )
        ],
        axis=0,
    )
    cols = jnp.concatenate([cols, jnp.zeros((N_COLS - cols.shape[0], features), F32)], axis=0)
    weights = (embed_weight, pos_long, pos_short, qkv_weight, proj_weight, fc1_weight, fc2_weight)

    saved, kept, blocks = None, [], [block]
    for k in range(band):
        *saved, sums = forward(
            sources[k], blocks[k], places, cols, cotangent, weights, vis_count, saved
        )
        kept.append(sums)
        if k + 1 < band:
            blocks.append(after(moving, sums))
        if k + 2 < band:
            moving = shift(blocks[-1], 1, band)
    (x_t, a_t, qkv_t, probs, o_t, act_t, gh_t, c_t, x1_t, ch_t) = saved

    send, keep, fc1b_grad = ff_gradients(ring.core, act_t, cotangent, c_t, gh_t)
    ff = Sum(ring, keep, send)
    flights = [ff]

    old, emb, sums_b, trip = None, [None] * band, [None] * band, None
    back_order = list(range(1, band)) + [0]
    ready = [send]
    for k in back_order:
        args = [after(gh_t, *ready), x1_t, cotangent, qkv_t, probs, x_t, ch_t]
        *old, emb[k], sums_b[k] = backward(
            sources[k], block.shape[0], kept[k], cols, args,
            (fc1_weight, proj_weight, qkv_weight), old,
        )
        emb[k], sums_b[k] = meet(flights, emb[k], sums_b[k])
        ready = []
        if ff.stage < stages:
            ready.append(ff.down())
        if trip is None:
            trip = Trip(emb[k], band)
            flights.append(trip)
        elif k:
            ready.append(trip.on(emb[k]))
    gqkv_t, gy_t = old

    send, keep = rest_gradients(
        ring.core, after(a_t, *ready), gqkv_t, o_t, gy_t, fc1b_grad, blocks, emb, kept, sums_b
    )
    send, keep = meet(flights, send, keep)
    rest = Sum(ring, keep, send)
    while ff.stage < stages:
        ff.down()
        meet([ff])
    ready = [ff.turn()]
    back = after(trip.flight[0] + emb[0], *ready)
    visible_grad = jnp.einsum(
        "vd,ed->ve", back[:vis_count], embed_weight, preferred_element_type=F32
    ).astype(BF)
    (visible_grad,) = meet([rest], visible_grad)
    ready = [rest.down()]
    block_out = output(after(x1_t, *ready), act_t, fc2_weight, fc2_bias[:, None])
    (block_out,) = meet([ff, rest], block_out)
    for _ in range(1, stages):
        flights = [rest]
        if ff.stage > 0:
            ff.up()
            if ff.stage > 0:
                flights.append(ff)
        rest.down()
        meet(flights)
    while ff.stage > 0:
        ff.up()
    rest.turn()
    meet([rest])
    rest.up()
    meet([rest, ff])
    ready = [rest.up(), ff.swap_cores()]
    while rest.stage > 1:
        meet([rest])
        ready.append(rest.up())
    meet([rest, ff])
    ready.append(rest.up())
    ff.flight[0] = after(ff.flight[0], *ready)
    fc2_grad, fc1_grad = ff.done([(hidden, features), (features, hidden)])
    (fc2_grad, fc1_grad) = meet([rest], fc2_grad, fc1_grad)
    rest.swap_cores()
    small_rows = rest.own.shape[0] * 2 - 4 * features - enc
    qkv_grad, proj_grad, embed_grad, small = rest.done(
        [(features, 3 * features), (features, features), (enc, features), (small_rows, features)]
    )
    return (
        block_out,
        visible_grad,
        embed_grad,
        small[6],
        small[5],
        small[3],
        small[4],
        qkv_grad,
        small[1:3],
        proj_grad,
        small[0],
        small[7],
        small[8],
        fc1_grad,
        small[10 : 10 + hidden // features].reshape(hidden),
        fc2_grad,
        small[9],
    )


def solution(mesh):
    split = P(("dp", "band"), None)
    in_specs = (split, P(("dp", "band")), split) + (P(),) * 15 + (split,)
    out_specs = (split, split) + (P(),) * 15
    return jax.shard_map(
        functools.partial(body, mesh.shape["dp"], mesh.shape["band"]),
        mesh=mesh,
        in_specs=in_specs,
        out_specs=out_specs,
        check_vma=False,
    )
```

```python
import functools

import jax
import jax.numpy as jnp
from jax import lax
from jax.experimental import pallas as pl
from jax.experimental.pallas import tpu as pltpu
from jax.sharding import PartitionSpec as P

HEADS = 16
FREQ = 8
WIN = 4
EPS = 1e-06
BF = jnp.bfloat16
F32 = jnp.float32
LANES = 128
MIB = 1024 * 1024
SCALE = 1.0
PARAMS = pltpu.CompilerParams(vmem_limit_bytes=60 * MIB)


def takes(microseconds):
    return pl.CostEstimate(
        flops=0, bytes_accessed=int(SCALE * microseconds * 3.3e6), transcendentals=0
    )


def row_layout(is_long, rowid, row_count):
    quarter = row_count // 4
    span = row_count // (2 * FREQ)
    halfspan = span // 2
    target = rowid // quarter
    inner = rowid % quarter
    column = target // 2 * WIN + inner % WIN
    local = inner // WIN
    halves = target % 2
    if is_long:
        frame_time = halves * span + local
        frame = frame_time
    else:
        frame_time = halves * halfspan + local % halfspan
        frame = local // halfspan * span + frame_time
    return frame * FREQ + column, frame_time, column


def sincos_rows(places, features):
    halfway = features // 2
    omega = 1.0 / 10000.0 ** (jnp.arange(halfway, dtype=F32) / halfway)
    angles = omega[:, None] * places.astype(F32)[None, :]
    return jnp.sin(angles), jnp.cos(angles)


def mm(a, b):
    return lax.dot_general(a, b, (((1,), (0,)), ((), ())), preferred_element_type=F32)


def mm_nt(a, b):
    return lax.dot_general(a, b, (((1,), (1,)), ((), ())), preferred_element_type=F32)


def window_of_lane(rows, columns):
    lane = lax.broadcasted_iota(jnp.int32, (rows, columns), 1)
    return (lane % LANES) // (WIN * WIN)


def compact(square, win):
    size = WIN * WIN
    out = square[0:size]
    for w in range(1, LANES // size):
        out = jnp.where(win == w, square[w * size : (w + 1) * size], out)
    return out


def expand(rows, win):
    size = WIN * WIN
    return jnp.concatenate(
        [jnp.where(win == w, rows, 0.0).astype(BF) for w in range(LANES // size)], axis=0
    )


def stacked(wide):
    return jnp.concatenate(
        [wide[:, j * LANES : (j + 1) * LANES] for j in range(wide.shape[1] // LANES)], axis=0
    )


def heads_apart(group, width):
    count = LANES // width
    blocks = []
    for j in range(count):
        parts = []
        if j:
            parts.append(jnp.zeros((j * width, LANES), BF))
        parts.append(group[j * width : (j + 1) * width])
        if j < count - 1:
            parts.append(jnp.zeros(((count - 1 - j) * width, LANES), BF))
        blocks.append(jnp.concatenate(parts, axis=0))
    return jnp.concatenate(blocks, axis=1)


def heads_of(wide, width):
    return jnp.concatenate(
        [
            wide[j * width : (j + 1) * width, j * LANES : (j + 1) * LANES]
            for j in range(LANES // width)
        ],
        axis=0,
    )


def normalize_t(x):
    count = x.shape[0]
    center = x - jnp.sum(x, axis=0, keepdims=True) * (1.0 / count)
    var = jnp.sum(center * center, axis=0, keepdims=True) * (1.0 / count)
    scale = lax.rsqrt(var + EPS)
    return center * scale, scale


def normalize_back_t(grad, unit, scale, gain):
    count = grad.shape[0]
    inner = grad * gain
    mean = jnp.sum(inner, axis=0, keepdims=True) * (1.0 / count)
    mixed = jnp.sum(inner * unit, axis=0, keepdims=True) * (1.0 / count)
    return scale * (inner - mean - unit * mixed)


def mm_tn(a, b):
    return lax.dot_general(a, b, (((0,), (0,)), ((), ())), preferred_element_type=F32)


def mm_tt(a, b):
    return lax.dot_general(a, b, (((0,), (1,)), ((), ())), preferred_element_type=F32)


def columns_kernel(*refs):
    vectors, out = refs[:-1], refs[-1]
    width = out.shape[1]
    out[...] = jnp.zeros_like(out)
    row = 0
    for ref in vectors:
        for i in range(ref.shape[0]):
            for j in range(ref.shape[1] // width):
                out[row : row + 1, :] = ref[i : i + 1, j * width : (j + 1) * width]
                row += 1


def stack_columns(vectors, width):
    return pl.pallas_call(
        columns_kernel,
        out_shape=jax.ShapeDtypeStruct((N_COLS, width), F32),
        cost_estimate=takes(2.0),
    )(*vectors)


def lane_sums(acc):
    return jnp.sum(acc.T, axis=0, keepdims=True)


def lanes(t):
    return slice(t * LANES, (t + 1) * LANES)


def copies(pairs, sems, start=True):
    made = [pltpu.make_async_copy(a, b, sems.at[i]) for i, (a, b) in enumerate(pairs)]
    if start:
        for copy in made:
            copy.start()
    return made


C_MASK, C_G1, C_B1, C_QB, C_VB, C_PB, C_G2, C_B2, C_F2B, C_EB, C_F1B = range(11)
N_COLS = 16
N_WEIGHTS = 11
N_SAVED = 11
NOTE = 8


class Block:
    def __init__(self, features, rows):
        self.features, self.rows = features, rows
        self.tiles = rows // LANES
        self.half = rows // 2
        self.per_half = self.tiles // 2
        self.groups = features // LANES
        self.width = features // HEADS
        self.factor = self.width ** (-0.5)
        self.chunk = features // 2

    def of_half(self, h):
        return range(h * self.per_half, (h + 1) * self.per_half)

    def part(self, h):
        return slice(h * self.half, (h + 1) * self.half)

    def chunks(self, size):
        return [slice(i, i + self.chunk) for i in range(0, size, self.chunk)]

    def group(self, base, g):
        return slice(base + g * LANES, base + (g + 1) * LANES)


def forward_kernel(vis_count, aliased, sk, *refs):
    (cols_hbm, places_hbm, v_hbm, cot_hbm, *w_hbm) = refs[: 4 + N_WEIGHTS]
    refs = refs[4 + N_WEIGHTS + (N_SAVED if aliased else 0) :]
    out_hbm, sums_hbm, refs = refs[:N_SAVED], refs[N_SAVED], refs[N_SAVED + 1 :]
    saved, refs = refs[:N_SAVED], refs[N_SAVED:]
    (x_t, a_t, qkv_t, probs, o_t, act_t, gh_t, c_t, x1_t, ch_t, gc_t) = saved
    held, refs = refs[:7], refs[7:]
    (wemb, wqkv, wproj, w1, w2, pos_long, pos_short) = held
    (places, cols, sums, v_pad, colb, e_t, wide, cot, cot_t, scores) = refs[:10]
    (in_sems, first_sems, out_sems, half_sems) = refs[10:]
    features, rows = x_t.shape
    k = Block(features, rows)
    source = sk[0]
    always = source >= 0
    row_at = pl.ds(pl.multiple_of(source * rows, rows), rows)

    count = v_hbm.shape[0]
    first = copies(
        [
            (cols_hbm, cols),
            (places_hbm, places),
            (v_hbm, v_pad.at[pl.ds(0, count), :]),
            (cot_hbm.at[row_at, :], cot),
        ],
        first_sems,
        start=False,
    )
    pairs = list(zip(w_hbm, held))[:5]
    quarter = features // 4
    for i, ref in enumerate(w_hbm[5:7]):
        pairs.append((ref, pos_long.at[pl.ds(i * quarter, quarter), :]))
    for i, ref in enumerate(w_hbm[7:9]):
        pairs.append((ref, pos_short.at[pl.ds(i * quarter, quarter), :]))
    for pos in (pos_long, pos_short):
        for i, ref in enumerate(w_hbm[9:11], 2):
            pairs.append((ref, pos.at[pl.ds(i * quarter, quarter), :]))
    loads = copies(pairs, in_sems, start=False)
    loads = [loads[0], *loads[5:], *loads[1:5]]
    for copy in (*first[:3], loads[0], first[3], *loads[1:]):
        copy.start()
    views = [ref.at[source] if i == 3 else ref.at[:, row_at] for i, ref in enumerate(out_hbm)]
    stores = [
        None if i in (5, 6) else pltpu.make_async_copy(a, b, out_sems.at[i])
        for i, (a, b) in enumerate(zip(saved, views))
    ]
    sums_store = pltpu.make_async_copy(sums, sums_hbm, out_sems.at[N_SAVED])
    halves = []
    for h in range(2):
        at = pl.ds(pl.multiple_of(source * rows + h * k.half, k.half), k.half)
        pairs = [(saved[i].at[:, k.part(h)], out_hbm[i].at[:, at]) for i in (5, 6)]
        halves.append(copies(pairs, half_sems.at[h], start=False))

    v_pad[count:, :] = jnp.zeros((v_pad.shape[0] - count, v_pad.shape[1]), BF)
    sums[...] = jnp.zeros_like(sums)
    first[0].wait()
    columns = cols[...].T
    for i in range(C_F1B + 4):
        colb[i] = jnp.broadcast_to(columns[:, i : i + 1], (features, LANES))
    first[1].wait()
    first[2].wait()
    note = v_pad[count - 16 : count, 0:rows].astype(F32)
    is_long = note[NOTE + 2 : NOTE + 3, :] > 0.5
    loads[0].wait()

    @pl.when(always)
    def _():
        embedded = mm_tt(wemb[...], v_pad[...])
        note_t = note.T
        index = lax.broadcasted_iota(jnp.int32, (rows, 1), 0)
        patch = note_t[:, NOTE : NOTE + 1] * 64.0 + note_t[:, NOTE + 1 : NOTE + 2]
        patch = jnp.where(index < vis_count, patch.astype(jnp.int32), -1)
        place = jnp.where(is_long, places[0:1, :], places[1:2, :])
        for t in range(k.tiles):
            chosen = jnp.where(patch == place[:, lanes(t)], 1.0, 0.0)
            ch_t[:, lanes(t)] = chosen.astype(BF)
            sums[1:2, lanes(t)] = jnp.sum(chosen, axis=0, keepdims=True)
        for t in range(k.tiles):
            e_t[:, lanes(t)] = (embedded[:, lanes(t)] + colb[C_EB]).astype(BF)
        for h in range(2):
            wide[:, k.part(h)] = mm(e_t[...], ch_t[:, k.part(h)])

    stores[9].start()
    first[3].wait()
    for copy in loads[1:9]:
        copy.wait()
    win = window_of_lane(WIN * WIN, 4 * LANES)

    def entry(t):
        pos = jnp.where(is_long[:, lanes(t)], pos_long[:, lanes(t)], pos_short[:, lanes(t)])
        start = (wide[:, lanes(t)] + (1.0 - sums[1:2, lanes(t)]) * colb[C_MASK]) + pos
        start = start.astype(BF)
        x_t[:, lanes(t)] = start
        unit, _scale = normalize_t(start.astype(F32))
        a_t[:, lanes(t)] = (unit * colb[C_G1] + colb[C_B1]).astype(BF)
        cot_t[:, lanes(t)] = cot[t * LANES : (t + 1) * LANES, :].T

    def project(h, parts):
        for n in parts:
            chunk = slice(n * k.chunk, (n + 1) * k.chunk)
            prod = mm_tn(wqkv[:, chunk], a_t[:, k.part(h)])
            bias = (C_QB, None, C_VB)[n // 2]
            for u, t in enumerate(k.of_half(h)):
                piece = prod[:, lanes(u)]
                if bias is not None:
                    piece = piece + colb[bias, slice((n % 2) * k.chunk, (n % 2 + 1) * k.chunk)]
                qkv_t[chunk, lanes(t)] = piece.astype(BF)

    def score(t):
        for g in range(k.groups):
            q_g = qkv_t[k.group(0, g), lanes(t)]
            k_g = qkv_t[k.group(features, g), lanes(t)]
            scores[t * k.groups + g] = compact(mm(k_g.T, heads_apart(q_g, k.width)), win)

    def soften(t):
        for g in range(k.groups):
            logits = scores[t * k.groups + g] * k.factor
            shifted = jnp.exp(logits - jnp.max(logits, axis=0, keepdims=True))
            prob = shifted / jnp.sum(shifted, axis=0, keepdims=True)
            probs[t, :, g * 4 * LANES : (g + 1) * 4 * LANES] = prob

    def mix(t):
        for g in range(k.groups):
            prob = probs[t, :, g * 4 * LANES : (g + 1) * 4 * LANES]
            mixed = mm(qkv_t[k.group(2 * features, g), lanes(t)], expand(prob, win))
            o_t[k.group(0, g), lanes(t)] = heads_of(mixed, k.width).astype(BF)

    def grow(h):
        wide[:, k.part(h)] = mm_tn(wproj[...], o_t[:, k.part(h)])

    def norm2(t):
        x1 = x_t[:, lanes(t)].astype(F32) + (wide[:, lanes(t)] + colb[C_PB])
        x1_t[:, lanes(t)] = x1
        unit, _scale = normalize_t(x1)
        c_t[:, lanes(t)] = (unit * colb[C_G2] + colb[C_B2]).astype(BF)

    def hidden(h, parts):
        for n in parts:
            chunk = slice(n * k.chunk, (n + 1) * k.chunk)
            grown = mm_tn(w1[:, chunk], c_t[:, k.part(h)])
            gact = mm(w2[chunk, :], cot_t[:, k.part(h)])
            rows_of = slice((n % 2) * k.chunk, (n % 2 + 1) * k.chunk)
            for u, t in enumerate(k.of_half(h)):
                own = grown[:, lanes(u)] + colb[C_F1B + n // 2, rows_of]
                cumulative = 0.5 * (1.0 + lax.erf(own * 0.7071067811865476))
                act_t[chunk, lanes(t)] = (own * cumulative).astype(BF)
                slope = cumulative + own * jnp.exp(-0.5 * own * own) * 0.3989422804014327
                gh_t[chunk, lanes(t)] = (gact[:, lanes(u)] * slope).astype(BF)

    def hidden_back(h):
        gc_t[:, k.part(h)] = mm(w1[...], gh_t[:, k.part(h)])

    @pl.when(always)
    def _():
        entry(0)
        entry(1)

    loads[9].wait()

    @pl.when(always)
    def _():
        project(0, range(6))
        entry(2)
        entry(3)
        total = cot_t[:, 0:LANES].astype(F32)
        for t in range(1, k.tiles):
            total += cot_t[:, lanes(t)].astype(F32)
        sums[0:1, :] = lane_sums(total)

    sums_store.start()
    stores[0].start()
    stores[1].start()

    @pl.when(always)
    def _():
        score(0)
        score(1)
        project(1, range(0, 3))
        soften(0)
        mix(0)
        project(1, range(3, 6))
        soften(1)
        mix(1)

    stores[2].start()
    loads[10].wait()

    @pl.when(always)
    def _():
        score(2)
        score(3)
        grow(0)
        soften(2)
        mix(2)
        norm2(0)
        soften(3)
        mix(3)
        norm2(1)

    stores[3].start()
    stores[4].start()
    loads[11].wait()
    loads[12].wait()

    @pl.when(always)
    def _():
        grow(1)
        hidden(0, range(0, 4))
        norm2(2)
        norm2(3)
        hidden(0, range(4, 8))

    stores[7].start()
    stores[8].start()
    for copy in halves[0]:
        copy.start()

    @pl.when(always)
    def _():
        hidden(1, range(0, 4))
        hidden_back(0)
        hidden(1, range(4, 8))

    for copy in halves[1]:
        copy.start()

    @pl.when(always)
    def _():
        hidden_back(1)

    stores[10].start()
    for copy in stores:
        if copy is not None:
            copy.wait()
    for copy in (*halves[0], *halves[1], sums_store):
        copy.wait()


def backward_kernel(aliased, sk, *refs):
    (cols_hbm, kept_hbm, *in_hbm) = refs[:9]
    w_hbm = refs[9:11]
    refs = refs[11 + (2 if aliased else 0) :]
    gqkv_hbm, gy_hbm, gemb_hbm, sums_hbm = refs[:4]
    (gc_t, x1_t, cot, qkv_t, probs, x_t, ch_t) = refs[4:11]
    (wproj, wqkv) = refs[11:13]
    (kept, cols, gemb, sums, gqkv_t, gy_t, colb, gx1_t, go_t, gx_t, hot, wide, acc) = refs[13:26]
    (in_sems, w_sems, out_sems) = refs[26:]
    features, rows = x_t.shape
    k = Block(features, rows)
    source = sk[0]
    always = source >= 0
    row_at = pl.ds(pl.multiple_of(source * rows, rows), rows)
    views = []
    for i, ref in enumerate(in_hbm):
        views.append(ref.at[row_at, :] if i == 2 else ref.at[source] if i == 4 else ref.at[:, row_at])
    pairs = [*zip(views, refs[4:11]), (kept_hbm, kept)]
    pairs.append((cols_hbm, cols))
    loads = copies(pairs, in_sems, start=False)
    w_loads = copies(zip(w_hbm, refs[11:13]), w_sems, start=False)
    for copy in (*loads[8:], *loads[:3], w_loads[0], *loads[3:8], w_loads[1]):
        copy.start()
    stores = copies(
        [
            (gqkv_t, gqkv_hbm.at[:, row_at]),
            (gy_t, gy_hbm.at[:, row_at]),
            (gemb, gemb_hbm),
            (sums, sums_hbm),
        ],
        out_sems,
        start=False,
    )

    def add(i, at, value, begin):
        if begin:
            acc[i, at] = value
        else:
            acc[i, at] += value

    everything = slice(0, features)
    sums[...] = jnp.zeros_like(sums)
    loads[8].wait()
    columns = cols[...].T
    for n, i in enumerate((C_G1, C_G2)):
        colb[n] = jnp.broadcast_to(columns[:, i : i + 1], (features, LANES))
    for copy in loads[:3]:
        copy.wait()
    win = window_of_lane(WIN * WIN, 4 * LANES)

    def norm2_back(t):
        gc = gc_t[:, lanes(t)]
        unit, scale = normalize_t(x1_t[:, lanes(t)])
        add(7, everything, gc * unit, t == 0)
        add(8, everything, gc, t == 0)
        own = cot[t * LANES : (t + 1) * LANES, :].T.astype(F32)
        gx1 = own + normalize_back_t(gc, unit, scale, colb[1])
        gx1_t[:, lanes(t)] = gx1
        low = gx1.astype(BF)
        gy_t[:, lanes(t)] = low
        add(0, everything, low.astype(F32), t == 0)

    def branch(h):
        go_t[:, k.part(h)] = mm(wproj[...], gy_t[:, k.part(h)]).astype(BF)

    def probs_grad(t):
        for g in range(k.groups):
            v_g = qkv_t[k.group(2 * features, g), lanes(t)]
            go_g = go_t[k.group(0, g), lanes(t)]
            hot[t * k.groups + g] = compact(mm(v_g.T, heads_apart(go_g, k.width)), win)

    def score_grad(t):
        for g in range(k.groups):
            gp = hot[t * k.groups + g]
            prob = probs[t, :, g * 4 * LANES : (g + 1) * 4 * LANES]
            hot[t * k.groups + g] = prob * (gp - jnp.sum(gp * prob, axis=0, keepdims=True))

    def row_grads(t):
        products = []
        for g in range(k.groups):
            q_g = qkv_t[k.group(0, g), lanes(t)]
            k_g = qkv_t[k.group(features, g), lanes(t)]
            go_g = go_t[k.group(0, g), lanes(t)]
            gs = expand(hot[t * k.groups + g], win)
            prob = expand(probs[t, :, g * 4 * LANES : (g + 1) * 4 * LANES], win)
            products.append((mm(k_g, gs), mm_nt(q_g, stacked(gs)), mm_nt(go_g, stacked(prob))))
        for g, (gq, gk, gv) in enumerate(products):
            gq = (heads_of(gq, k.width) * k.factor).astype(BF)
            gk = (heads_of(gk, k.width) * k.factor).astype(BF)
            gv = heads_of(gv, k.width).astype(BF)
            gqkv_t[k.group(0, g), lanes(t)] = gq
            gqkv_t[k.group(features, g), lanes(t)] = gk
            gqkv_t[k.group(2 * features, g), lanes(t)] = gv
            add(1, k.group(0, g), gq.astype(F32), t == 0)
            add(2, k.group(0, g), gv.astype(F32), t == 0)

    def project_back(h):
        wide[:, k.part(h)] = mm(wqkv[...], gqkv_t[:, k.part(h)])

    def norm1_back(t):
        ga = wide[:, lanes(t)]
        unit, scale = normalize_t(x_t[:, lanes(t)].astype(F32))
        add(3, everything, ga * unit, t == 0)
        add(4, everything, ga, t == 0)
        low = (gx1_t[:, lanes(t)] + normalize_back_t(ga, unit, scale, colb[0])).astype(BF)
        gx_t[:, lanes(t)] = low
        own = low.astype(F32)
        filled = kept[1:2, lanes(t)]
        add(5, everything, own * (1.0 - filled), t == 0)
        add(6, everything, own * filled, t == 0)

    @pl.when(always)
    def _():
        norm2_back(0)
        norm2_back(1)

    w_loads[0].wait()
    loads[3].wait()
    loads[4].wait()

    @pl.when(always)
    def _():
        branch(0)
        norm2_back(2)
        norm2_back(3)
        for i in (0, 7, 8):
            sums[i : i + 1, :] = lane_sums(acc[i])

    stores[1].start()

    @pl.when(always)
    def _():
        probs_grad(0)
        probs_grad(1)
        branch(1)
        score_grad(0)
        row_grads(0)
        score_grad(1)
        row_grads(1)

    loads[5].wait()
    loads[6].wait()
    loads[7].wait()
    w_loads[1].wait()

    @pl.when(always)
    def _():
        probs_grad(2)
        probs_grad(3)
        project_back(0)
        score_grad(2)
        row_grads(2)
        norm1_back(0)
        score_grad(3)
        row_grads(3)
        norm1_back(1)

    stores[0].start()

    @pl.when(always)
    def _():
        project_back(1)
        for i in (1, 2):
            sums[i : i + 1, :] = lane_sums(acc[i])
        norm1_back(2)
        norm1_back(3)

    @pl.when(always)
    def _():
        chosen = mm_nt(ch_t[...], gx_t[...]).astype(BF)
        for i in (3, 4, 5, 6):
            sums[i : i + 1, :] = lane_sums(acc[i])
        gemb[...] = chosen[0 : gemb.shape[0]]

    stores[2].start()
    stores[3].start()
    for copy in stores:
        copy.wait()


def whole(shape):
    zeros = (0,) * len(shape)
    return pl.BlockSpec(shape, lambda *_: zeros)


FAR = pl.BlockSpec(memory_space=pltpu.HBM)
ANYWHERE = pl.BlockSpec(memory_space=pl.ANY)


def forward(sk, v, places, cols, cot, weights, vis_count, old):
    rows = places.shape[1]
    features = cols.shape[1]
    total = cot.shape[0]
    hidden = weights[4].shape[0]
    tiles = rows // LANES
    wide_probs = HEADS * LANES
    s = jax.ShapeDtypeStruct
    saved = [
        ((features,), BF),
        ((features,), BF),
        ((3 * features,), BF),
        None,
        ((features,), BF),
        ((hidden,), BF),
        ((hidden,), BF),
        ((features,), BF),
        ((features,), F32),
        ((rows,), BF),
        ((features,), F32),
    ]
    probs = (tiles, WIN * WIN, wide_probs)
    out_shape = [
        s((total // rows,) + probs, F32) if x is None else s(x[0] + (total,), x[1]) for x in saved
    ] + [s((8, features), F32)]
    scratch = [
        pltpu.VMEM(probs, F32) if x is None else pltpu.VMEM(x[0] + (rows,), x[1]) for x in saved
    ] + [
        *[pltpu.VMEM(w.shape, w.dtype) for w in weights[:5]],
        pltpu.VMEM((features, rows), F32),
        pltpu.VMEM((features, rows), F32),
        pltpu.VMEM(places.shape, places.dtype),
        pltpu.VMEM((N_COLS, features), F32),
        pltpu.VMEM((8, features), F32),
        pltpu.VMEM((rows, v.shape[1]), BF),
        pltpu.VMEM((C_F1B + 4, features, LANES), F32),
        pltpu.VMEM((features, rows), BF),
        pltpu.VMEM((features, rows), F32),
        pltpu.VMEM((rows, features), BF),
        pltpu.VMEM((features, rows), BF),
        pltpu.VMEM((tiles * features // LANES, WIN * WIN, 4 * LANES), F32),
        pltpu.SemaphoreType.DMA((13,)),
        pltpu.SemaphoreType.DMA((4,)),
        pltpu.SemaphoreType.DMA((N_SAVED + 1,)),
        pltpu.SemaphoreType.DMA((2, 2)),
    ]
    old = list(old or ())
    ins = [cols, places, v, cot, *weights]
    return pl.pallas_call(
        functools.partial(forward_kernel, vis_count, bool(old)),
        grid_spec=pltpu.PrefetchScalarGridSpec(
            num_scalar_prefetch=1,
            grid=(1,),
            in_specs=[ANYWHERE] * 3 + [FAR] * (len(ins) - 3 + len(old)),
            out_specs=[FAR] * (N_SAVED + 1),
            scratch_shapes=scratch,
        ),
        out_shape=out_shape,
        input_output_aliases={1 + len(ins) + i: i for i in range(len(old))},
        cost_estimate=takes(13.5),
        compiler_params=PARAMS,
    )(sk, *ins, *old)


def backward(sk, count, kept, cols, saved, weights, old):
    gc_t, x1_t, cot, qkv_t, probs, x_t, ch_t = saved
    features, total = x_t.shape
    rows = ch_t.shape[0]
    tiles = rows // LANES
    s = jax.ShapeDtypeStruct
    old = list(old or ())
    ins = [cols, kept, *saved, *weights]
    return pl.pallas_call(
        functools.partial(backward_kernel, bool(old)),
        grid_spec=pltpu.PrefetchScalarGridSpec(
            num_scalar_prefetch=1,
            grid=(1,),
            in_specs=[ANYWHERE] * 2 + [FAR] * (len(ins) - 2 + len(old)),
            out_specs=[FAR] * 4,
            scratch_shapes=[
            pltpu.VMEM((features, rows), F32),
            pltpu.VMEM((features, rows), F32),
            pltpu.VMEM((rows, features), BF),
            pltpu.VMEM((3 * features, rows), BF),
            pltpu.VMEM(probs.shape[1:], F32),
            pltpu.VMEM((features, rows), BF),
            pltpu.VMEM((rows, rows), BF),
        ]
        + [pltpu.VMEM(w.shape, BF) for w in weights]
        + [
            pltpu.VMEM(kept.shape, F32),
            pltpu.VMEM(cols.shape, F32),
            pltpu.VMEM((count, features), BF),
            pltpu.VMEM((16, features), F32),
            pltpu.VMEM((3 * features, rows), BF),
            pltpu.VMEM((features, rows), BF),
            pltpu.VMEM((2, features, LANES), F32),
            pltpu.VMEM((features, rows), F32),
            pltpu.VMEM((features, rows), BF),
            pltpu.VMEM((features, rows), BF),
            pltpu.VMEM((tiles * features // LANES, WIN * WIN, 4 * LANES), F32),
            pltpu.VMEM((features, rows), F32),
            pltpu.VMEM((9, features, LANES), F32),
            pltpu.SemaphoreType.DMA((len(saved) + 2,)),
            pltpu.SemaphoreType.DMA((len(weights),)),
            pltpu.SemaphoreType.DMA((4,)),
        ],
        ),
        out_shape=[
            s((3 * features, total), BF),
            s((features, total), BF),
            s((count, features), BF),
            s((16, features), F32),
        ],
        input_output_aliases={1 + len(ins) + i: i for i in range(len(old))},
        cost_estimate=takes(12.0),
        compiler_params=PARAMS,
    )(sk, *ins, *old)


def output_kernel(aliased, x1_t, act_t, w2, bias, *refs):
    out = refs[-1]
    column = jnp.broadcast_to(bias[...], (8, bias.shape[1])).T[:, 0:1]
    for t in range(x1_t.shape[1] // LANES):
        if t % 2 == 0:
            grown = mm_tn(w2[...], act_t[:, t * LANES : (t + 2) * LANES])
        total = x1_t[:, lanes(t)] + (grown[:, lanes(t % 2)] + column)
        out[t * LANES : (t + 1) * LANES, :] = total.astype(BF).T


def output(x1_t, act_t, w2, bias, part, old):
    features, total = x1_t.shape
    hidden = act_t.shape[0]
    rows = features
    steps = total // rows // 2
    old = [] if old is None else [old]
    return pl.pallas_call(
        functools.partial(output_kernel, bool(old)),
        grid=(steps,),
        in_specs=[
            pl.BlockSpec((features, rows), lambda i: (0, i + part * steps)),
            pl.BlockSpec((hidden, rows), lambda i: (0, i + part * steps)),
            whole(w2.shape),
            whole((1, features)),
        ]
        + [FAR] * len(old),
        out_specs=pl.BlockSpec((rows, features), lambda i: (i + part * steps, 0)),
        out_shape=jax.ShapeDtypeStruct((total, features), BF),
        input_output_aliases={4: 0} if old else {},
        cost_estimate=takes(6.0),
        compiler_params=PARAMS,
    )(x1_t, act_t, w2, bias, *old)


def to_halves(core, low, send, keep, at=slice(None)):
    cut = low.shape[1] // 2
    left, right = low[:, :cut], low[:, cut:]
    send[at, :] = jnp.where(core == 0, right, left)
    keep[at, :] = jnp.where(core == 0, left, right)


def ff_kernel(steps, core, act, cot_hbm, c_hbm, gh, send, keep, bias, left, cot, c, out, sems, out_sems):
    size = out.shape[2]

    def load(i):
        source = act if i < steps else gh
        at = pl.ds((i % steps) * size, size)
        return pltpu.make_async_copy(source.at[at, :], left.at[i], sems.at[i])

    def stored(i):
        at = pl.ds(pl.multiple_of(i * size, size), size)
        return [
            pltpu.make_async_copy(out.at[i, n], ref.at[at, :], out_sems.at[i, n])
            for n, ref in enumerate((send, keep))
        ]

    def finish(i, product):
        to_halves(core[0], product.astype(BF), out.at[i, 0], out.at[i, 1])
        for copy in stored(i):
            copy.start()

    cot_load = pltpu.make_async_copy(cot_hbm, cot, sems.at[2 * steps])
    c_load = pltpu.make_async_copy(c_hbm, c, sems.at[2 * steps + 1])
    cot_load.start()
    for i in range(2 * steps):
        load(i).start()
        if i == steps - 1:
            c_load.start()
    cot_load.wait()
    always = core[0] >= 0
    for i in range(2 * steps):
        load(i).wait()
        if i == steps:
            c_load.wait()

        @pl.when(always)
        def _():
            if i < steps:
                finish(i, mm(left[i], cot[...]))
            else:
                finish(i, mm_nt(c[...], left[i]))
                total = left[i, :, 0:LANES].astype(F32)
                for t in range(1, left.shape[2] // LANES):
                    total += left[i, :, lanes(t)].astype(F32)
                bias[i - steps] = jnp.sum(total.T, axis=0, keepdims=True)

    for i in range(2 * steps):
        for copy in stored(i):
            copy.wait()


def ff_gradients(core, act_t, cot, c_t, gh_t):
    hidden, total = act_t.shape
    features = cot.shape[1]
    steps = hidden // features
    s = jax.ShapeDtypeStruct
    return pl.pallas_call(
        functools.partial(ff_kernel, steps),
        grid_spec=pltpu.PrefetchScalarGridSpec(
            num_scalar_prefetch=1,
            grid=(1,),
            in_specs=[FAR] * 4,
            out_specs=[FAR, FAR, whole((steps, 1, features))],
            scratch_shapes=[
                pltpu.VMEM((2 * steps, features, total), BF),
                pltpu.VMEM(cot.shape, BF),
                pltpu.VMEM(c_t.shape, BF),
                pltpu.VMEM((2 * steps, 2, features, features // 2), BF),
                pltpu.SemaphoreType.DMA((2 * steps + 2,)),
                pltpu.SemaphoreType.DMA((2 * steps, 2)),
            ],
        ),
        out_shape=[
            s((2 * hidden, features // 2), BF),
            s((2 * hidden, features // 2), BF),
            s((steps, 1, features), F32),
        ],
        cost_estimate=takes(11.0),
        compiler_params=PARAMS,
    )(core, act_t, cot, c_t, gh_t)


def rest_kernel(band, blocks, core, *refs):
    (kept, sums), refs = (refs[:band], refs[band : 2 * band]), refs[2 * band :]
    (bias, a_hbm, gqkv_hbm, o_hbm, gy_hbm), refs = refs[:5], refs[5:]
    v_hbm, emb_hbm, refs = refs[:band], refs[band : 2 * band], refs[2 * band :]
    (send, keep, a, gqkv, o, gy, visible, emb, out, sems, out_sems) = refs
    size = out.shape[2]
    pairs = [(a_hbm, a)]
    for i in range(blocks):
        pairs.append((gqkv_hbm.at[pl.ds(i * size, size), :], gqkv.at[i]))
    pairs += [(o_hbm, o), (gy_hbm, gy)]
    for n in range(band):
        pairs += [(v_hbm[n], visible.at[n]), (emb_hbm[n], emb.at[n])]
    loads = copies(pairs, sems, start=False)
    for copy in loads:
        copy.start()
    always = core[0] >= 0

    def stored(i):
        at = pl.ds(i * size, size)
        return [
            pltpu.make_async_copy(out.at[i, n], ref.at[at, :], out_sems.at[i, n])
            for n, ref in enumerate((send, keep))
        ]

    def finish(i, low, at=slice(None)):
        to_halves(core[0], low, out.at[i, 0], out.at[i, 1], at)

    loads[0].wait()
    for i in range(blocks):
        loads[1 + i].wait()

        @pl.when(always)
        def _():
            finish(i, mm_nt(a[...], gqkv[i]).astype(BF))

        for copy in stored(i):
            copy.start()
    for copy in loads[1 + blocks :]:
        copy.wait()

    @pl.when(always)
    def _():
        finish(blocks, mm_nt(o[...], gy[...]).astype(BF))

    for copy in stored(blocks):
        copy.start()

    def embed(at):
        total = mm_tn(visible[0, :, at], emb[0])
        for n in range(1, band):
            total = total + mm_tn(visible[n, :, at], emb[n])
        return total.astype(BF)

    @pl.when(always)
    def _():
        over = visible.shape[2] - size
        finish(blocks + 1, embed(slice(0, size)))
        finish(blocks + 2, embed(slice(size, size + over)), slice(0, over))
        ours, cots = sums[0][0:9, :], kept[0][0:1, :]
        for n in range(1, band):
            ours = ours + sums[n][0:9, :]
            cots = cots + kept[n][0:1, :]
        hidden = [bias[n] for n in range(bias.shape[0])]
        rest = jnp.zeros((size - over - 10 - bias.shape[0], size), F32)
        small = jnp.concatenate([ours, cots, *hidden, rest], axis=0)
        finish(blocks + 2, small.astype(BF), slice(over, size))

    for i in range(blocks + 1, blocks + 3):
        for copy in stored(i):
            copy.start()
    for i in range(blocks + 3):
        for copy in stored(i):
            copy.wait()


def rest_gradients(core, a_t, gqkv_t, o_t, gy_t, bias, visible, emb, kept, sums):
    features, total = a_t.shape
    blocks = gqkv_t.shape[0] // features
    band = len(emb)
    steps = blocks + 3
    s = jax.ShapeDtypeStruct((steps * features, features // 2), BF)
    return pl.pallas_call(
        functools.partial(rest_kernel, band, blocks),
        grid_spec=pltpu.PrefetchScalarGridSpec(
            num_scalar_prefetch=1,
            grid=(1,),
            in_specs=[whole(x.shape) for x in (*kept, *sums, bias)]
            + [FAR] * 4
            + [ANYWHERE] * (2 * band),
            out_specs=[FAR, FAR],
            scratch_shapes=[
                pltpu.VMEM((features, total), BF),
                pltpu.VMEM((blocks, features, total), BF),
                pltpu.VMEM((features, total), BF),
                pltpu.VMEM((features, total), BF),
                pltpu.VMEM((band,) + visible[0].shape, BF),
                pltpu.VMEM((band,) + emb[0].shape, BF),
                pltpu.VMEM((steps, 2, features, features // 2), BF),
                pltpu.SemaphoreType.DMA((3 + blocks + 2 * band,)),
                pltpu.SemaphoreType.DMA((steps, 2)),
            ],
        ),
        out_shape=[s, s],
        cost_estimate=takes(8.0),
        compiler_params=PARAMS,
    )(core, *kept, *sums, bias, a_t, gqkv_t, o_t, gy_t, *visible, *emb)


def done_kernel(count, n_vectors, aliased, sides, own, got, *refs):
    last = aliased > 0 and n_vectors > 0
    if last:
        other, refs = refs[0], refs[1:]
    refs, held, sems = refs[aliased:-2], refs[-2], refs[-1]
    count_small = (n_vectors if last else 1) if n_vectors else 0
    cut_at = len(refs) - count_small
    outs, vectors = refs[:cut_at], refs[cut_at:]
    size, cut = held.shape[1:]
    per_half = count // 2
    side, columns = sides[0], sides[1]
    at_columns = pl.multiple_of(columns * cut, cut)
    places = done_places(size, [out.shape for out in outs])
    made = []
    for n, (row, which, i, j, high) in enumerate(places):
        made.append(
            pltpu.make_async_copy(
                held.at[row // size, pl.ds(row % size, high), :],
                outs[which].at[pl.ds(i, high), pl.ds(j + at_columns, cut)],
                sems.at[n],
            )
        )
    for b in range(count):
        at = slice((b % per_half) * size, (b % per_half + 1) * size)
        held[b] = jnp.where(side == b // per_half, own[at, :], got[at, :]).astype(F32)
        for copy, place in zip(made, places):
            if place[0] // size == b:
                copy.start()
    if n_vectors:
        row = (places[-1][0] + places[-1][4]) % size
        small = held[count - 1, row : row + 16, :]
        if last:
            left = jnp.where(columns == 0, small, other[...])
            right = jnp.where(columns == 0, other[...], small)
            small = jnp.concatenate([left, right], axis=1)
            row = 0
            for ref in vectors:
                for j in range(ref.shape[1] // size):
                    for i in range(ref.shape[0]):
                        ref[i : i + 1, j * size : (j + 1) * size] = small[row : row + 1, :]
                        row += 1
        else:
            vectors[0][...] = small
    for copy in made:
        copy.wait()


def done_places(size, shapes):
    row, places = 0, []
    for n, (high, wide) in enumerate(shapes):
        for j in range(wide // size):
            for i in range(0, high, size):
                places.append((row, n, i, j * size, min(size, high - i)))
                row += min(size, high - i)
    return places


def done(sides, own, got, shapes, vectors=(), old=(), small=None):
    cut = own.shape[1]
    size = 2 * cut
    count = 2 * own.shape[0] // size
    ins = [own, got] + ([] if small is None else [small])
    ends = list(vectors) if small is not None or not vectors else [(16, cut)]
    return pl.pallas_call(
        functools.partial(done_kernel, count, len(vectors), len(old)),
        grid_spec=pltpu.PrefetchScalarGridSpec(
            num_scalar_prefetch=1,
            grid=(1,),
            in_specs=[whole(x.shape) for x in ins] + [FAR] * len(old),
            out_specs=[FAR] * len(shapes) + [whole(x) for x in ends],
            scratch_shapes=[
                pltpu.VMEM((count, size, cut), F32),
                pltpu.SemaphoreType.DMA((len(done_places(size, shapes)),)),
            ],
        ),
        out_shape=[jax.ShapeDtypeStruct(x, F32) for x in (*shapes, *ends)],
        input_output_aliases={1 + len(ins) + i: i for i in range(len(old))},
        cost_estimate=takes(3.0),
        compiler_params=PARAMS,
    )(sides, *ins, *old)


def add_rows(terms, starts, size):
    total = 0.0
    for term, start in zip(terms, starts):
        total = total + lax.dynamic_slice_in_dim(term, start, size, 0).astype(F32)
    return total.astype(BF)


def join_rows(side, own, got):
    return jnp.where(
        side == 0, jnp.concatenate([own, got], axis=0), jnp.concatenate([got, own], axis=0)
    )


def shift(x, by, size):
    return lax.ppermute(x, "band", [(i, (i + by) % size) for i in range(size)])


def after(x, *others):
    return lax.optimization_barrier((x, *others))[0]


class Ring:
    def __init__(self, dp, band):
        me, z = lax.axis_index("dp"), lax.axis_index("band")
        self.dp = dp
        bits = []
        while (2 << len(bits)) < dp:
            bits.append(len(bits) + 1)
        self.stages = []
        sides = []
        for up, down in zip(bits, reversed(bits)):
            pairs = [(i, i ^ (1 << (down if i & 1 else up))) for i in range(dp)]
            both = ((me >> up) & 1, (me >> down) & 1)
            sides.append(both)
            self.stages.append(("dp", pairs, jnp.where(me & 1 == 1, both[1], both[0])))
        step = 1
        while step < band:
            pairs = [(i, i ^ step) for i in range(band)]
            side = (z // step) & 1
            sides.append((side, side))
            self.stages.append(("band", pairs, side))
            step *= 2
        core = me & 1
        self.core = core.astype(jnp.int32)[None]
        first = sides[0]
        mine = jnp.where(core == 1, first[1], first[0])
        theirs = jnp.where(core == 1, first[0], first[1])
        self.mine = jnp.stack([mine, core]).astype(jnp.int32)
        self.theirs = jnp.stack([theirs, 1 - core]).astype(jnp.int32)

    def swap_cores(self, x):
        return lax.ppermute(x, "dp", [(i, i ^ 1) for i in range(self.dp)])

    def swap(self, x, i):
        axis, pairs, _side = self.stages[i]
        return lax.ppermute(x, axis, pairs)


class Sum:
    def __init__(self, ring, keep, send):
        self.ring = ring
        zero = jnp.int32(0)
        self.terms, self.starts = [keep], [zero, zero]
        self.base, self.size = zero, keep.shape[0]
        self.stage = 0
        self.last = len(ring.stages)
        self.flight = [ring.swap_cores(send)]

    def rows(self, start):
        return add_rows(self.terms, [start - x for x in self.starts], self.size)

    def left(self):
        return self.stage < 2 * self.last

    def step(self):
        n, last = self.stage, self.last - 1
        self.stage += 1
        if n < last:
            self.terms += self.flight
            side = self.ring.stages[n][2].astype(jnp.int32)
            self.size //= 2
            send = self.rows(self.base + (1 - side) * self.size)
            self.base = self.base + side * self.size
            self.starts.append(self.base)
        elif n == last:
            self.terms += self.flight
            send = self.own = self.rows(self.base)
        elif n <= 2 * last:
            got = self.flight[0]
            if n == last + 1:
                self.own = (self.own.astype(F32) + got.astype(F32)).astype(BF)
            else:
                side = self.ring.stages[2 * last - n + 1][2]
                self.own = join_rows(side, self.own, got)
            send = self.own
        else:
            return self.swap_cores()
        self.flight = [self.ring.swap(send, min(n, 2 * last - n))]
        return send

    def swap_cores(self):
        self.halves = (self.own, self.flight[0])
        self.flight = [self.ring.swap_cores(x) for x in self.halves]
        return self.halves[1]

    def done_own(self, shapes, vectors=()):
        self.shapes, self.vectors = shapes, vectors
        self.out = done(self.ring.mine, *self.halves, shapes, vectors)
        return self.out

    def done(self):
        count = len(self.shapes)
        small = self.out[count] if self.vectors else None
        old = self.out[:count]
        return done(self.ring.theirs, *self.flight, self.shapes, self.vectors, old, small)


class Trip:
    def __init__(self, x, band):
        self.band = band
        self.flight = [shift(x, 1, band)]

    def on(self, own):
        going = self.flight[0] + own
        self.flight = [shift(going, 1, self.band)]
        return going


def meet(flights, *others):
    arrays = [x for f in flights for x in f.flight]
    out = lax.optimization_barrier((*arrays, *others))
    at = 0
    for f in flights:
        f.flight = list(out[at : at + len(f.flight)])
        at += len(f.flight)
    return out[at:]


def body(
    dp, band,
    visible, clip_long, patch_order, embed_weight, embed_bias, mask_token,
    norm1_gain, norm1_bias, qkv_weight, qv_bias, proj_weight, proj_bias,
    norm2_gain, norm2_bias, fc1_weight, fc1_bias, fc2_weight, fc2_bias, cotangent,
):
    features = embed_weight.shape[1]
    hidden = fc1_weight.shape[1]
    total = patch_order.shape[1]
    rows = total // band
    vis_count, enc = visible.shape
    z = lax.axis_index("band")
    ring = Ring(dp, band)
    stages = len(ring.stages)

    order = patch_order[0]
    half = vis_count // 2
    middle = total // 2
    visible_at = jnp.where(
        clip_long[0] == 1,
        order[:vis_count],
        jnp.concatenate([order[:half], order[middle : middle + vis_count - half]]),
    )
    notes = jnp.stack(
        [visible_at // 64, visible_at % 64, jnp.broadcast_to(clip_long, (vis_count,))]
    ).astype(BF)
    notes = jnp.pad(notes, ((0, NOTE - 3), (0, enc - vis_count)), mode="edge")
    block = jnp.concatenate([visible, notes], axis=0)
    sources = [((z - k) % band).astype(jnp.int32)[None] for k in range(band)]
    moving = shift(block, 1, band)

    rowid = z * rows + jnp.arange(rows, dtype=jnp.int32)
    place_long, time_long, column = row_layout(True, rowid, total)
    place_short, time_short, _ = row_layout(False, rowid, total)
    places = jnp.stack([place_long, place_short])
    positions = []
    for place in (time_long, time_short, column):
        positions += sincos_rows(place, features // 2)

    vectors = (
        mask_token, norm1_gain, norm1_bias, qv_bias, proj_bias, norm2_gain, norm2_bias, fc2_bias,
        embed_bias, fc1_bias,
    )
    cols = stack_columns([x if x.ndim == 2 else x[None] for x in vectors], features)
    weights = (embed_weight, qkv_weight, proj_weight, fc1_weight, fc2_weight, *positions)

    saved, kept, blocks = None, [], [block]
    for k in range(band):
        *saved, sums = forward(
            sources[k], blocks[k], places, cols, cotangent, weights, vis_count, saved
        )
        kept.append(sums)
        if k + 1 < band:
            blocks.append(after(moving, sums))
        if k + 2 < band:
            moving = shift(blocks[-1], 1, band)
    (x_t, a_t, qkv_t, probs, o_t, act_t, gh_t, c_t, x1_t, ch_t, gc_t) = saved

    send, keep, fc1b_grad = ff_gradients(ring.core, act_t, cotangent, c_t, gh_t)
    ff = Sum(ring, keep, send)
    old, emb, sums_b, trip = None, [None] * band, [None] * band, None
    back_order = list(range(1, band)) + [0]
    ready = [send]
    for n, k in enumerate(back_order):
        args = [after(gc_t, *ready), x1_t, cotangent, qkv_t, probs, x_t, ch_t]
        *old, emb[k], sums_b[k] = backward(
            sources[k], block.shape[0], kept[k], cols, args, (proj_weight, qkv_weight), old
        )
        flights = [] if n == 1 else [ff, trip] if n == 2 else [ff]
        emb[k], sums_b[k] = meet(flights, emb[k], sums_b[k])
        ready = [ff.step()] if ff in flights else []
        if n == 0:
            trip = Trip(emb[k], band)
        elif trip in flights:
            ready.append(trip.on(emb[back_order[1]]))
    gqkv_t, gy_t = old

    send, keep = rest_gradients(
        ring.core, after(a_t, *ready), gqkv_t, o_t, gy_t, fc1b_grad, blocks, emb, kept, sums_b
    )
    send, keep = meet([ff, trip], send, keep)
    rest = Sum(ring, keep, send)
    ready = [ff.step()]
    meet([rest], *ready)
    block_out, waits, ff_grads, ff_shapes = None, 0, None, [(hidden, features), (features, hidden)]
    ends = 2 * stages - 1
    for n in range(2 * stages):
        ready = [rest.step()]
        if n and ff.left() and not waits:
            ready.append(ff.step())
            waits = 1 if ff.stage == ends else 0
        else:
            waits = max(waits - 1, 0)
        flights = [rest] if waits or n == 0 else [rest, ff]
        if n < 2:
            block_out = output(
                after(x1_t, *ready), act_t, fc2_weight, fc2_bias[None], n, block_out
            )
            (block_out,) = meet(flights, block_out)
        elif n == ends - 2:
            for k in back_order[2:-1]:
                going = trip.on(emb[k])
            if not ff.left():
                ff.halves = (after(ff.halves[0], going, *ready), ff.halves[1])
                ff.out = meet([ff, rest], *ff.done_own(ff_shapes))
            else:
                meet([rest, ff], going)
        elif n == ends - 1:
            if not ff.left():
                ff.flight = [after(ff.flight[0], *ready), ff.flight[1]]
                ff_grads = ff.done()
                ff_grads = meet([trip], *ff_grads)
                ready = ff_grads
            back = after(trip.flight[0], *ready) + emb[0]
            visible_grad = jnp.einsum(
                "vd,ed->ve", back[:vis_count], embed_weight, preferred_element_type=F32
            ).astype(BF)
            (visible_grad,) = meet([rest], visible_grad)
        elif n < ends:
            meet(flights)
    if ff_grads is None:
        while ff.left():
            ff.step()
        ff.out = ff.done_own(ff_shapes)
        ff_grads = ff.done()
    fc2_grad, fc1_grad = ff_grads
    row = (1, features)
    rest.out = meet(
        [rest],
        *rest.done_own(
            [(features, 3 * features), (features, features), (enc, features)],
            [row, (2, features)] + [row] * 7 + [(1, hidden)],
        ),
    )
    (
        qkv_grad, proj_grad, embed_grad,
        projb, qvb, gain1, bias1, mask, embb, gain2, bias2, fc2b, fc1b,
    ) = rest.done()
    return (
        block_out,
        visible_grad,
        embed_grad,
        embb[0],
        mask[0],
        gain1[0],
        bias1[0],
        qkv_grad,
        qvb,
        proj_grad,
        projb[0],
        gain2[0],
        bias2[0],
        fc1_grad,
        fc1b[0],
        fc2_grad,
        fc2b[0],
    )


def solution(mesh):
    split = P(("dp", "band"), None)
    in_specs = (split, P(("dp", "band")), split) + (P(),) * 15 + (split,)
    out_specs = (split, split) + (P(),) * 15
    return jax.shard_map(
        functools.partial(body, mesh.shape["dp"], mesh.shape["band"]),
        mesh=mesh,
        in_specs=in_specs,
        out_specs=out_specs,
        check_vma=False,
    )
```

```python
import functools

import jax
import jax.numpy as jnp
from jax import lax
from jax.experimental import pallas as pl
from jax.experimental.pallas import tpu as pltpu
from jax.sharding import PartitionSpec as P

HEADS = 16
FREQ = 8
WIN = 4
EPS = 1e-06
BF = jnp.bfloat16
F32 = jnp.float32
LANES = 128
MIB = 1024 * 1024
SCALE = 1.0
PARAMS = pltpu.CompilerParams(vmem_limit_bytes=60 * MIB)
SMALL_PARAMS = pltpu.CompilerParams(vmem_limit_bytes=28 * MIB)


def takes(microseconds):
    return pl.CostEstimate(
        flops=0, bytes_accessed=int(SCALE * microseconds * 3.3e6), transcendentals=0
    )


def row_layout(is_long, rowid, row_count):
    quarter = row_count // 4
    span = row_count // (2 * FREQ)
    halfspan = span // 2
    target = rowid // quarter
    inner = rowid % quarter
    column = target // 2 * WIN + inner % WIN
    local = inner // WIN
    halves = target % 2
    if is_long:
        frame_time = halves * span + local
        frame = frame_time
    else:
        frame_time = halves * halfspan + local % halfspan
        frame = local // halfspan * span + frame_time
    return frame * FREQ + column, frame_time, column


def sincos_rows(places, features):
    halfway = features // 2
    omega = 1.0 / 10000.0 ** (jnp.arange(halfway, dtype=F32) / halfway)
    angles = omega[:, None] * places.astype(F32)[None, :]
    return jnp.sin(angles), jnp.cos(angles)


def mm(a, b):
    return lax.dot_general(a, b, (((1,), (0,)), ((), ())), preferred_element_type=F32)


def mm_nt(a, b):
    return lax.dot_general(a, b, (((1,), (1,)), ((), ())), preferred_element_type=F32)


def window_of_lane(rows, columns):
    lane = lax.broadcasted_iota(jnp.int32, (rows, columns), 1)
    return (lane % LANES) // (WIN * WIN)


def compact(square, win):
    size = WIN * WIN
    out = square[0:size]
    for w in range(1, LANES // size):
        out = jnp.where(win == w, square[w * size : (w + 1) * size], out)
    return out


def expand(rows, win):
    size = WIN * WIN
    return jnp.concatenate(
        [jnp.where(win == w, rows, 0.0).astype(BF) for w in range(LANES // size)], axis=0
    )


def stacked(wide):
    return jnp.concatenate(
        [wide[:, j * LANES : (j + 1) * LANES] for j in range(wide.shape[1] // LANES)], axis=0
    )


def heads_apart(group, width):
    count = LANES // width
    blocks = []
    for j in range(count):
        parts = []
        if j:
            parts.append(jnp.zeros((j * width, LANES), BF))
        parts.append(group[j * width : (j + 1) * width])
        if j < count - 1:
            parts.append(jnp.zeros(((count - 1 - j) * width, LANES), BF))
        blocks.append(jnp.concatenate(parts, axis=0))
    return jnp.concatenate(blocks, axis=1)


def heads_of(wide, width):
    return jnp.concatenate(
        [
            wide[j * width : (j + 1) * width, j * LANES : (j + 1) * LANES]
            for j in range(LANES // width)
        ],
        axis=0,
    )


def normalize_t(x):
    count = x.shape[0]
    center = x - jnp.sum(x, axis=0, keepdims=True) * (1.0 / count)
    var = jnp.sum(center * center, axis=0, keepdims=True) * (1.0 / count)
    scale = lax.rsqrt(var + EPS)
    return center * scale, scale


def normalize_back_t(grad, unit, scale, gain):
    count = grad.shape[0]
    inner = grad * gain
    mean = jnp.sum(inner, axis=0, keepdims=True) * (1.0 / count)
    mixed = jnp.sum(inner * unit, axis=0, keepdims=True) * (1.0 / count)
    return scale * (inner - mean - unit * mixed)


def mm_tn(a, b):
    return lax.dot_general(a, b, (((0,), (0,)), ((), ())), preferred_element_type=F32)


def mm_tt(a, b):
    return lax.dot_general(a, b, (((0,), (1,)), ((), ())), preferred_element_type=F32)


def columns_kernel(*refs):
    vectors, out = refs[:-1], refs[-1]
    width = out.shape[1]
    out[...] = jnp.zeros_like(out)
    row = 0
    for ref in vectors:
        for i in range(ref.shape[0]):
            for j in range(ref.shape[1] // width):
                out[row : row + 1, :] = ref[i : i + 1, j * width : (j + 1) * width]
                row += 1


def stack_columns(vectors, width):
    return pl.pallas_call(
        columns_kernel,
        out_shape=jax.ShapeDtypeStruct((N_COLS, width), F32),
        cost_estimate=takes(2.0),
    )(*vectors)


def expand_exactly(table, ones):
    high = table.astype(BF)
    rest = table - high.astype(F32)
    middle = rest.astype(BF)
    low = (rest - middle.astype(F32)).astype(BF)
    return mm(high, ones) + (mm(middle, ones) + mm(low, ones))


def lane_sums(acc):
    return jnp.sum(acc.T, axis=0, keepdims=True)


def lanes(t):
    return slice(t * LANES, (t + 1) * LANES)


def copies(pairs, sems, start=True):
    made = [pltpu.make_async_copy(a, b, sems.at[i]) for i, (a, b) in enumerate(pairs)]
    if start:
        for copy in made:
            copy.start()
    return made


C_MASK, C_G1, C_B1, C_QB, C_VB, C_PB, C_G2, C_B2, C_F2B, C_EB, C_F1B = range(11)
N_COLS = 16
N_WEIGHTS = 11
N_SAVED = 11
NOTE = 8


class Block:
    def __init__(self, features, rows):
        self.features, self.rows = features, rows
        self.tiles = rows // LANES
        self.half = rows // 2
        self.per_half = self.tiles // 2
        self.groups = features // LANES
        self.width = features // HEADS
        self.factor = self.width ** (-0.5)
        self.chunk = features // 2

    def of_half(self, h):
        return range(h * self.per_half, (h + 1) * self.per_half)

    def part(self, h):
        return slice(h * self.half, (h + 1) * self.half)

    def chunks(self, size):
        return [slice(i, i + self.chunk) for i in range(0, size, self.chunk)]

    def group(self, base, g):
        return slice(base + g * LANES, base + (g + 1) * LANES)


def forward_kernel(vis_count, aliased, sk, *refs):
    (cols_hbm, places_hbm, v_hbm, cot_hbm, *w_hbm) = refs[: 4 + N_WEIGHTS]
    refs = refs[4 + N_WEIGHTS + (N_SAVED if aliased else 0) :]
    out_hbm, sums_hbm, refs = refs[:N_SAVED], refs[N_SAVED], refs[N_SAVED + 1 :]
    saved, refs = refs[:N_SAVED], refs[N_SAVED:]
    (x_t, a_t, qkv_t, probs, o_t, act_t, gh_t, c_t, x1_t, ch_t, gc_t) = saved
    held, refs = refs[:7], refs[7:]
    (wemb, wqkv, wproj, w1, w2, tables, pos) = held
    (places, cols, sums, v_pad, colb, e_t, wide, cot, cot_t, scores) = refs[:10]
    (in_sems, first_sems, out_sems, half_sems) = refs[10:]
    features, rows = x_t.shape
    k = Block(features, rows)
    source = sk[0]
    always = source >= 0
    row_at = pl.ds(pl.multiple_of(source * rows, rows), rows)

    count = v_hbm.shape[0]
    first = copies(
        [
            (cols_hbm, cols),
            (places_hbm, places),
            (v_hbm, v_pad.at[pl.ds(0, count), :]),
            (cot_hbm.at[row_at, :], cot),
        ],
        first_sems,
        start=False,
    )
    pairs = list(zip(w_hbm, held))[:5]
    quarter = features // 4
    for i, ref in enumerate(w_hbm[5:]):
        pairs.append((ref, tables.at[i // 2, pl.ds(i % 2 * quarter, quarter), :]))
    loads = copies(pairs, in_sems, start=False)
    loads = [loads[0], *loads[5:], *loads[1:5]]
    for copy in (*first[:3], loads[0], first[3], *loads[1:]):
        copy.start()
    views = [ref.at[source] if i == 3 else ref.at[:, row_at] for i, ref in enumerate(out_hbm)]
    stores = [
        None if i in (5, 6) else pltpu.make_async_copy(a, b, out_sems.at[i])
        for i, (a, b) in enumerate(zip(saved, views))
    ]
    sums_store = pltpu.make_async_copy(sums, sums_hbm, out_sems.at[N_SAVED])
    halves = []
    for h in range(2):
        at = pl.ds(pl.multiple_of(source * rows + h * k.half, k.half), k.half)
        pairs = [(saved[i].at[:, k.part(h)], out_hbm[i].at[:, at]) for i in (5, 6)]
        halves.append(copies(pairs, half_sems.at[h], start=False))

    v_pad[count:, :] = jnp.zeros((v_pad.shape[0] - count, v_pad.shape[1]), BF)
    sums[...] = jnp.zeros_like(sums)
    first[0].wait()
    columns = cols[...].T
    for i in range(C_F1B + 4):
        colb[i] = jnp.broadcast_to(columns[:, i : i + 1], (features, LANES))
    first[1].wait()
    first[2].wait()
    note = v_pad[count - 16 : count, 0:rows].astype(F32)
    is_long = note[NOTE + 2 : NOTE + 3, :] > 0.5
    for copy in loads[:7]:
        copy.wait()

    @pl.when(always)
    def _():
        embedded = mm_tt(wemb[...], v_pad[...])
        at = lax.broadcasted_iota(jnp.int32, (LANES, rows), 0)
        row = lax.broadcasted_iota(jnp.int32, (LANES, rows), 1)
        times = jnp.where(is_long[:, 0:LANES], tables[0], tables[1])
        spread = (jnp.where(row // WIN == at, 1.0, 0.0), jnp.where(row % WIN == at, 1.0, 0.0))
        for i, (table, ones) in enumerate(zip((times, tables[2]), spread)):
            place = slice(i * features // 2, (i + 1) * features // 2)
            pos[place, :] = expand_exactly(table, ones.astype(BF))
        note_t = note.T
        index = lax.broadcasted_iota(jnp.int32, (rows, 1), 0)
        patch = note_t[:, NOTE : NOTE + 1] * 64.0 + note_t[:, NOTE + 1 : NOTE + 2]
        patch = jnp.where(index < vis_count, patch.astype(jnp.int32), -1)
        place = jnp.where(is_long, places[0:1, :], places[1:2, :])
        for t in range(k.tiles):
            chosen = jnp.where(patch == place[:, lanes(t)], 1.0, 0.0)
            ch_t[:, lanes(t)] = chosen.astype(BF)
            sums[1:2, lanes(t)] = jnp.sum(chosen, axis=0, keepdims=True)
        for t in range(k.tiles):
            e_t[:, lanes(t)] = (embedded[:, lanes(t)] + colb[C_EB]).astype(BF)
        for h in range(2):
            wide[:, k.part(h)] = mm(e_t[...], ch_t[:, k.part(h)])

    stores[9].start()
    first[3].wait()
    win = window_of_lane(WIN * WIN, 4 * LANES)

    def entry(t):
        start = (wide[:, lanes(t)] + (1.0 - sums[1:2, lanes(t)]) * colb[C_MASK]) + pos[:, lanes(t)]
        start = start.astype(BF)
        x_t[:, lanes(t)] = start
        unit, _scale = normalize_t(start.astype(F32))
        a_t[:, lanes(t)] = (unit * colb[C_G1] + colb[C_B1]).astype(BF)
        cot_t[:, lanes(t)] = cot[t * LANES : (t + 1) * LANES, :].T

    def project(h, parts):
        for n in parts:
            chunk = slice(n * k.chunk, (n + 1) * k.chunk)
            prod = mm_tn(wqkv[:, chunk], a_t[:, k.part(h)])
            bias = (C_QB, None, C_VB)[n // 2]
            for u, t in enumerate(k.of_half(h)):
                piece = prod[:, lanes(u)]
                if bias is not None:
                    piece = piece + colb[bias, slice((n % 2) * k.chunk, (n % 2 + 1) * k.chunk)]
                qkv_t[chunk, lanes(t)] = piece.astype(BF)

    def score(t):
        for g in range(k.groups):
            q_g = qkv_t[k.group(0, g), lanes(t)]
            k_g = qkv_t[k.group(features, g), lanes(t)]
            scores[t * k.groups + g] = compact(mm(k_g.T, heads_apart(q_g, k.width)), win)

    def soften(t):
        for g in range(k.groups):
            logits = scores[t * k.groups + g] * k.factor
            shifted = jnp.exp(logits - jnp.max(logits, axis=0, keepdims=True))
            prob = shifted / jnp.sum(shifted, axis=0, keepdims=True)
            probs[t, :, g * 4 * LANES : (g + 1) * 4 * LANES] = prob

    def mix(t):
        for g in range(k.groups):
            prob = probs[t, :, g * 4 * LANES : (g + 1) * 4 * LANES]
            mixed = mm(qkv_t[k.group(2 * features, g), lanes(t)], expand(prob, win))
            o_t[k.group(0, g), lanes(t)] = heads_of(mixed, k.width).astype(BF)

    def grow(h):
        wide[:, k.part(h)] = mm_tn(wproj[...], o_t[:, k.part(h)])

    def norm2(t):
        x1 = x_t[:, lanes(t)].astype(F32) + (wide[:, lanes(t)] + colb[C_PB])
        x1_t[:, lanes(t)] = x1
        unit, _scale = normalize_t(x1)
        c_t[:, lanes(t)] = (unit * colb[C_G2] + colb[C_B2]).astype(BF)

    def hidden(h, parts):
        for n in parts:
            chunk = slice(n * k.chunk, (n + 1) * k.chunk)
            grown = mm_tn(w1[:, chunk], c_t[:, k.part(h)])
            gact = mm(w2[chunk, :], cot_t[:, k.part(h)])
            rows_of = slice((n % 2) * k.chunk, (n % 2 + 1) * k.chunk)
            for u, t in enumerate(k.of_half(h)):
                own = grown[:, lanes(u)] + colb[C_F1B + n // 2, rows_of]
                cumulative = 0.5 * (1.0 + lax.erf(own * 0.7071067811865476))
                act_t[chunk, lanes(t)] = (own * cumulative).astype(BF)
                slope = cumulative + own * jnp.exp(-0.5 * own * own) * 0.3989422804014327
                gh_t[chunk, lanes(t)] = (gact[:, lanes(u)] * slope).astype(BF)

    def hidden_back(h):
        gc_t[:, k.part(h)] = mm(w1[...], gh_t[:, k.part(h)])

    @pl.when(always)
    def _():
        entry(0)
        entry(1)

    loads[7].wait()

    @pl.when(always)
    def _():
        project(0, range(6))
        entry(2)
        entry(3)
        total = cot_t[:, 0:LANES].astype(F32)
        for t in range(1, k.tiles):
            total += cot_t[:, lanes(t)].astype(F32)
        sums[0:1, :] = lane_sums(total)

    sums_store.start()
    stores[0].start()
    stores[1].start()

    @pl.when(always)
    def _():
        score(0)
        score(1)
        project(1, range(0, 3))
        soften(0)
        mix(0)
        project(1, range(3, 6))
        soften(1)
        mix(1)

    stores[2].start()
    loads[8].wait()

    @pl.when(always)
    def _():
        score(2)
        score(3)
        grow(0)
        soften(2)
        mix(2)
        norm2(0)
        soften(3)
        mix(3)
        norm2(1)

    stores[3].start()
    stores[4].start()
    loads[9].wait()
    loads[10].wait()

    @pl.when(always)
    def _():
        grow(1)
        hidden(0, range(0, 4))
        norm2(2)
        norm2(3)
        hidden(0, range(4, 8))

    stores[7].start()
    stores[8].start()
    for copy in halves[0]:
        copy.start()

    @pl.when(always)
    def _():
        hidden(1, range(0, 4))
        hidden_back(0)
        hidden(1, range(4, 8))

    for copy in halves[1]:
        copy.start()

    @pl.when(always)
    def _():
        hidden_back(1)

    stores[10].start()
    for copy in stores:
        if copy is not None:
            copy.wait()
    for copy in (*halves[0], *halves[1], sums_store):
        copy.wait()


def backward_kernel(aliased, sk, *refs):
    (cols_hbm, kept_hbm, *in_hbm) = refs[:9]
    w_hbm = refs[9:11]
    refs = refs[11 + (2 if aliased else 0) :]
    gqkv_hbm, gy_hbm, gemb_hbm, sums_hbm = refs[:4]
    (gc_t, x1_t, cot, qkv_t, probs, x_t, ch_t) = refs[4:11]
    (wproj, wqkv) = refs[11:13]
    (kept, cols, gemb, sums, gqkv_t, gy_t, colb, gx1_t, go_t, gx_t, hot, wide, acc) = refs[13:26]
    (in_sems, w_sems, out_sems) = refs[26:]
    features, rows = x_t.shape
    k = Block(features, rows)
    source = sk[0]
    always = source >= 0
    row_at = pl.ds(pl.multiple_of(source * rows, rows), rows)
    views = []
    for i, ref in enumerate(in_hbm):
        views.append(ref.at[row_at, :] if i == 2 else ref.at[source] if i == 4 else ref.at[:, row_at])
    pairs = [*zip(views, refs[4:11]), (kept_hbm, kept)]
    pairs.append((cols_hbm, cols))
    loads = copies(pairs, in_sems, start=False)
    w_loads = copies(zip(w_hbm, refs[11:13]), w_sems, start=False)
    for copy in (*loads[8:], *loads[:3], w_loads[0], *loads[3:8], w_loads[1]):
        copy.start()
    stores = copies(
        [
            (gqkv_t, gqkv_hbm.at[:, row_at]),
            (gy_t, gy_hbm.at[:, row_at]),
            (gemb, gemb_hbm),
            (sums, sums_hbm),
        ],
        out_sems,
        start=False,
    )

    def add(i, at, value, begin):
        if begin:
            acc[i, at] = value
        else:
            acc[i, at] += value

    everything = slice(0, features)
    sums[...] = jnp.zeros_like(sums)
    loads[8].wait()
    columns = cols[...].T
    for n, i in enumerate((C_G1, C_G2)):
        colb[n] = jnp.broadcast_to(columns[:, i : i + 1], (features, LANES))
    for copy in loads[:3]:
        copy.wait()
    win = window_of_lane(WIN * WIN, 4 * LANES)

    def norm2_back(t):
        gc = gc_t[:, lanes(t)]
        unit, scale = normalize_t(x1_t[:, lanes(t)])
        add(7, everything, gc * unit, t == 0)
        add(8, everything, gc, t == 0)
        own = cot[t * LANES : (t + 1) * LANES, :].T.astype(F32)
        gx1 = own + normalize_back_t(gc, unit, scale, colb[1])
        gx1_t[:, lanes(t)] = gx1
        low = gx1.astype(BF)
        gy_t[:, lanes(t)] = low
        add(0, everything, low.astype(F32), t == 0)

    def branch(h):
        go_t[:, k.part(h)] = mm(wproj[...], gy_t[:, k.part(h)]).astype(BF)

    def probs_grad(t):
        for g in range(k.groups):
            v_g = qkv_t[k.group(2 * features, g), lanes(t)]
            go_g = go_t[k.group(0, g), lanes(t)]
            hot[t * k.groups + g] = compact(mm(v_g.T, heads_apart(go_g, k.width)), win)

    def score_grad(t):
        for g in range(k.groups):
            gp = hot[t * k.groups + g]
            prob = probs[t, :, g * 4 * LANES : (g + 1) * 4 * LANES]
            hot[t * k.groups + g] = prob * (gp - jnp.sum(gp * prob, axis=0, keepdims=True))

    def row_grads(t):
        products = []
        for g in range(k.groups):
            q_g = qkv_t[k.group(0, g), lanes(t)]
            k_g = qkv_t[k.group(features, g), lanes(t)]
            go_g = go_t[k.group(0, g), lanes(t)]
            gs = expand(hot[t * k.groups + g], win)
            prob = expand(probs[t, :, g * 4 * LANES : (g + 1) * 4 * LANES], win)
            products.append((mm(k_g, gs), mm_nt(q_g, stacked(gs)), mm_nt(go_g, stacked(prob))))
        for g, (gq, gk, gv) in enumerate(products):
            gq = (heads_of(gq, k.width) * k.factor).astype(BF)
            gk = (heads_of(gk, k.width) * k.factor).astype(BF)
            gv = heads_of(gv, k.width).astype(BF)
            gqkv_t[k.group(0, g), lanes(t)] = gq
            gqkv_t[k.group(features, g), lanes(t)] = gk
            gqkv_t[k.group(2 * features, g), lanes(t)] = gv
            add(1, k.group(0, g), gq.astype(F32), t == 0)
            add(2, k.group(0, g), gv.astype(F32), t == 0)

    def project_back(h):
        wide[:, k.part(h)] = mm(wqkv[...], gqkv_t[:, k.part(h)])

    def norm1_back(t):
        ga = wide[:, lanes(t)]
        unit, scale = normalize_t(x_t[:, lanes(t)].astype(F32))
        add(3, everything, ga * unit, t == 0)
        add(4, everything, ga, t == 0)
        low = (gx1_t[:, lanes(t)] + normalize_back_t(ga, unit, scale, colb[0])).astype(BF)
        gx_t[:, lanes(t)] = low
        own = low.astype(F32)
        filled = kept[1:2, lanes(t)]
        add(5, everything, own * (1.0 - filled), t == 0)
        add(6, everything, own * filled, t == 0)

    @pl.when(always)
    def _():
        norm2_back(0)
        norm2_back(1)

    w_loads[0].wait()
    loads[3].wait()
    loads[4].wait()

    @pl.when(always)
    def _():
        branch(0)
        norm2_back(2)
        norm2_back(3)
        for i in (0, 7, 8):
            sums[i : i + 1, :] = lane_sums(acc[i])

    stores[1].start()

    @pl.when(always)
    def _():
        probs_grad(0)
        probs_grad(1)
        branch(1)
        score_grad(0)
        row_grads(0)
        score_grad(1)
        row_grads(1)

    loads[5].wait()
    loads[6].wait()
    loads[7].wait()
    w_loads[1].wait()

    @pl.when(always)
    def _():
        probs_grad(2)
        probs_grad(3)
        project_back(0)
        score_grad(2)
        row_grads(2)
        norm1_back(0)
        score_grad(3)
        row_grads(3)
        norm1_back(1)

    stores[0].start()

    @pl.when(always)
    def _():
        project_back(1)
        for i in (1, 2):
            sums[i : i + 1, :] = lane_sums(acc[i])
        norm1_back(2)
        norm1_back(3)

    @pl.when(always)
    def _():
        chosen = mm_nt(ch_t[...], gx_t[...]).astype(BF)
        for i in (3, 4, 5, 6):
            sums[i : i + 1, :] = lane_sums(acc[i])
        gemb[...] = chosen[0 : gemb.shape[0]]

    stores[2].start()
    stores[3].start()
    for copy in stores:
        copy.wait()


def whole(shape):
    zeros = (0,) * len(shape)
    return pl.BlockSpec(shape, lambda *_: zeros)


FAR = pl.BlockSpec(memory_space=pltpu.HBM)
ANYWHERE = pl.BlockSpec(memory_space=pl.ANY)


def forward(sk, v, places, cols, cot, weights, vis_count, old):
    rows = places.shape[1]
    features = cols.shape[1]
    total = cot.shape[0]
    hidden = weights[4].shape[0]
    tiles = rows // LANES
    wide_probs = HEADS * LANES
    s = jax.ShapeDtypeStruct
    saved = [
        ((features,), BF),
        ((features,), BF),
        ((3 * features,), BF),
        None,
        ((features,), BF),
        ((hidden,), BF),
        ((hidden,), BF),
        ((features,), BF),
        ((features,), F32),
        ((rows,), BF),
        ((features,), F32),
    ]
    probs = (tiles, WIN * WIN, wide_probs)
    out_shape = [
        s((total // rows,) + probs, F32) if x is None else s(x[0] + (total,), x[1]) for x in saved
    ] + [s((8, features), F32)]
    scratch = [
        pltpu.VMEM(probs, F32) if x is None else pltpu.VMEM(x[0] + (rows,), x[1]) for x in saved
    ] + [
        *[pltpu.VMEM(w.shape, w.dtype) for w in weights[:5]],
        pltpu.VMEM((3, features // 2, LANES), F32),
        pltpu.VMEM((features, rows), F32),
        pltpu.VMEM(places.shape, places.dtype),
        pltpu.VMEM((N_COLS, features), F32),
        pltpu.VMEM((8, features), F32),
        pltpu.VMEM((rows, v.shape[1]), BF),
        pltpu.VMEM((C_F1B + 4, features, LANES), F32),
        pltpu.VMEM((features, rows), BF),
        pltpu.VMEM((features, rows), F32),
        pltpu.VMEM((rows, features), BF),
        pltpu.VMEM((features, rows), BF),
        pltpu.VMEM((tiles * features // LANES, WIN * WIN, 4 * LANES), F32),
        pltpu.SemaphoreType.DMA((N_WEIGHTS,)),
        pltpu.SemaphoreType.DMA((4,)),
        pltpu.SemaphoreType.DMA((N_SAVED + 1,)),
        pltpu.SemaphoreType.DMA((2, 2)),
    ]
    old = list(old or ())
    ins = [cols, places, v, cot, *weights]
    return pl.pallas_call(
        functools.partial(forward_kernel, vis_count, bool(old)),
        grid_spec=pltpu.PrefetchScalarGridSpec(
            num_scalar_prefetch=1,
            grid=(1,),
            in_specs=[ANYWHERE] * 3 + [FAR] * (len(ins) - 3 + len(old)),
            out_specs=[FAR] * (N_SAVED + 1),
            scratch_shapes=scratch,
        ),
        out_shape=out_shape,
        input_output_aliases={1 + len(ins) + i: i for i in range(len(old))},
        cost_estimate=takes(13.5),
        compiler_params=PARAMS,
    )(sk, *ins, *old)


def backward(sk, count, kept, cols, saved, weights, old):
    gc_t, x1_t, cot, qkv_t, probs, x_t, ch_t = saved
    features, total = x_t.shape
    rows = ch_t.shape[0]
    tiles = rows // LANES
    s = jax.ShapeDtypeStruct
    old = list(old or ())
    ins = [cols, kept, *saved, *weights]
    return pl.pallas_call(
        functools.partial(backward_kernel, bool(old)),
        grid_spec=pltpu.PrefetchScalarGridSpec(
            num_scalar_prefetch=1,
            grid=(1,),
            in_specs=[ANYWHERE] * 2 + [FAR] * (len(ins) - 2 + len(old)),
            out_specs=[FAR] * 4,
            scratch_shapes=[
            pltpu.VMEM((features, rows), F32),
            pltpu.VMEM((features, rows), F32),
            pltpu.VMEM((rows, features), BF),
            pltpu.VMEM((3 * features, rows), BF),
            pltpu.VMEM(probs.shape[1:], F32),
            pltpu.VMEM((features, rows), BF),
            pltpu.VMEM((rows, rows), BF),
        ]
        + [pltpu.VMEM(w.shape, BF) for w in weights]
        + [
            pltpu.VMEM(kept.shape, F32),
            pltpu.VMEM(cols.shape, F32),
            pltpu.VMEM((count, features), BF),
            pltpu.VMEM((16, features), F32),
            pltpu.VMEM((3 * features, rows), BF),
            pltpu.VMEM((features, rows), BF),
            pltpu.VMEM((2, features, LANES), F32),
            pltpu.VMEM((features, rows), F32),
            pltpu.VMEM((features, rows), BF),
            pltpu.VMEM((features, rows), BF),
            pltpu.VMEM((tiles * features // LANES, WIN * WIN, 4 * LANES), F32),
            pltpu.VMEM((features, rows), F32),
            pltpu.VMEM((9, features, LANES), F32),
            pltpu.SemaphoreType.DMA((len(saved) + 2,)),
            pltpu.SemaphoreType.DMA((len(weights),)),
            pltpu.SemaphoreType.DMA((4,)),
        ],
        ),
        out_shape=[
            s((3 * features, total), BF),
            s((features, total), BF),
            s((count, features), BF),
            s((16, features), F32),
        ],
        input_output_aliases={1 + len(ins) + i: i for i in range(len(old))},
        cost_estimate=takes(12.0),
        compiler_params=PARAMS,
    )(sk, *ins, *old)


def output_kernel(aliased, x1_t, act_t, w2, bias, *refs):
    out = refs[-1]
    column = jnp.broadcast_to(bias[...], (8, bias.shape[1])).T[:, 0:1]
    for t in range(x1_t.shape[1] // LANES):
        if t % 2 == 0:
            grown = mm_tn(w2[...], act_t[:, t * LANES : (t + 2) * LANES])
        total = x1_t[:, lanes(t)] + (grown[:, lanes(t % 2)] + column)
        out[t * LANES : (t + 1) * LANES, :] = total.astype(BF).T


def output(x1_t, act_t, w2, bias, first, steps, old):
    features, total = x1_t.shape
    hidden = act_t.shape[0]
    rows = features
    old = [] if old is None else [old]
    return pl.pallas_call(
        functools.partial(output_kernel, bool(old)),
        grid=(steps,),
        in_specs=[
            pl.BlockSpec((features, rows), lambda i: (0, i + first)),
            pl.BlockSpec((hidden, rows), lambda i: (0, i + first)),
            whole(w2.shape),
            whole((1, features)),
        ]
        + [FAR] * len(old),
        out_specs=pl.BlockSpec((rows, features), lambda i: (i + first, 0)),
        out_shape=jax.ShapeDtypeStruct((total, features), BF),
        input_output_aliases={4: 0} if old else {},
        cost_estimate=takes(3.0 * steps),
        compiler_params=PARAMS,
    )(x1_t, act_t, w2, bias, *old)


def to_halves(core, low, send, keep, at=slice(None)):
    cut = low.shape[1] // 2
    left, right = low[:, :cut], low[:, cut:]
    send[at, :] = jnp.where(core == 0, right, left)
    keep[at, :] = jnp.where(core == 0, left, right)


def ff_kernel(steps, core, act, cot_hbm, c_hbm, gh, send, keep, bias, left, cot, c, out, sems, out_sems):
    size = out.shape[2]

    def load(i):
        source = act if i < steps else gh
        at = pl.ds((i % steps) * size, size)
        return pltpu.make_async_copy(source.at[at, :], left.at[i], sems.at[i])

    def stored(i):
        at = pl.ds(pl.multiple_of(i * size, size), size)
        return [
            pltpu.make_async_copy(out.at[i, n], ref.at[at, :], out_sems.at[i, n])
            for n, ref in enumerate((send, keep))
        ]

    def finish(i, product):
        to_halves(core[0], product.astype(BF), out.at[i, 0], out.at[i, 1])
        for copy in stored(i):
            copy.start()

    cot_load = pltpu.make_async_copy(cot_hbm, cot, sems.at[2 * steps])
    c_load = pltpu.make_async_copy(c_hbm, c, sems.at[2 * steps + 1])
    cot_load.start()
    for i in range(2 * steps):
        load(i).start()
        if i == steps - 1:
            c_load.start()
    cot_load.wait()
    always = core[0] >= 0
    for i in range(2 * steps):
        load(i).wait()
        if i == steps:
            c_load.wait()

        @pl.when(always)
        def _():
            if i < steps:
                finish(i, mm(left[i], cot[...]))
            else:
                finish(i, mm_nt(c[...], left[i]))
                total = left[i, :, 0:LANES].astype(F32)
                for t in range(1, left.shape[2] // LANES):
                    total += left[i, :, lanes(t)].astype(F32)
                bias[i - steps] = jnp.sum(total.T, axis=0, keepdims=True)

    for i in range(2 * steps):
        for copy in stored(i):
            copy.wait()


def ff_gradients(core, act_t, cot, c_t, gh_t):
    hidden, total = act_t.shape
    features = cot.shape[1]
    steps = hidden // features
    s = jax.ShapeDtypeStruct
    return pl.pallas_call(
        functools.partial(ff_kernel, steps),
        grid_spec=pltpu.PrefetchScalarGridSpec(
            num_scalar_prefetch=1,
            grid=(1,),
            in_specs=[FAR] * 4,
            out_specs=[FAR, FAR, whole((steps, 1, features))],
            scratch_shapes=[
                pltpu.VMEM((2 * steps, features, total), BF),
                pltpu.VMEM(cot.shape, BF),
                pltpu.VMEM(c_t.shape, BF),
                pltpu.VMEM((2 * steps, 2, features, features // 2), BF),
                pltpu.SemaphoreType.DMA((2 * steps + 2,)),
                pltpu.SemaphoreType.DMA((2 * steps, 2)),
            ],
        ),
        out_shape=[
            s((2 * hidden, features // 2), BF),
            s((2 * hidden, features // 2), BF),
            s((steps, 1, features), F32),
        ],
        cost_estimate=takes(11.0),
        compiler_params=PARAMS,
    )(core, act_t, cot, c_t, gh_t)


def rest_kernel(band, blocks, core, *refs):
    (kept, sums), refs = (refs[:band], refs[band : 2 * band]), refs[2 * band :]
    (bias, a_hbm, gqkv_hbm, o_hbm, gy_hbm), refs = refs[:5], refs[5:]
    v_hbm, emb_hbm, refs = refs[:band], refs[band : 2 * band], refs[2 * band :]
    (send, keep, a, gqkv, o, gy, visible, emb, out, sems, out_sems) = refs
    size = out.shape[2]
    pairs = [(a_hbm, a)]
    for i in range(blocks):
        pairs.append((gqkv_hbm.at[pl.ds(i * size, size), :], gqkv.at[i]))
    pairs += [(o_hbm, o), (gy_hbm, gy)]
    for n in range(band):
        pairs += [(v_hbm[n], visible.at[n]), (emb_hbm[n], emb.at[n])]
    loads = copies(pairs, sems, start=False)
    for copy in loads:
        copy.start()
    always = core[0] >= 0

    def stored(i):
        at = pl.ds(i * size, size)
        return [
            pltpu.make_async_copy(out.at[i, n], ref.at[at, :], out_sems.at[i, n])
            for n, ref in enumerate((send, keep))
        ]

    def finish(i, low, at=slice(None)):
        to_halves(core[0], low, out.at[i, 0], out.at[i, 1], at)

    loads[0].wait()
    for i in range(blocks):
        loads[1 + i].wait()

        @pl.when(always)
        def _():
            finish(i, mm_nt(a[...], gqkv[i]).astype(BF))

        for copy in stored(i):
            copy.start()
    for copy in loads[1 + blocks :]:
        copy.wait()

    @pl.when(always)
    def _():
        finish(blocks, mm_nt(o[...], gy[...]).astype(BF))

    for copy in stored(blocks):
        copy.start()

    def embed(at):
        total = mm_tn(visible[0, :, at], emb[0])
        for n in range(1, band):
            total = total + mm_tn(visible[n, :, at], emb[n])
        return total.astype(BF)

    @pl.when(always)
    def _():
        over = visible.shape[2] - size
        finish(blocks + 1, embed(slice(0, size)))
        finish(blocks + 2, embed(slice(size, size + over)), slice(0, over))
        ours, cots = sums[0][0:9, :], kept[0][0:1, :]
        for n in range(1, band):
            ours = ours + sums[n][0:9, :]
            cots = cots + kept[n][0:1, :]
        hidden = [bias[n] for n in range(bias.shape[0])]
        rest = jnp.zeros((size - over - 10 - bias.shape[0], size), F32)
        small = jnp.concatenate([ours, cots, *hidden, rest], axis=0)
        finish(blocks + 2, small.astype(BF), slice(over, size))

    for i in range(blocks + 1, blocks + 3):
        for copy in stored(i):
            copy.start()
    for i in range(blocks + 3):
        for copy in stored(i):
            copy.wait()


def rest_gradients(core, a_t, gqkv_t, o_t, gy_t, bias, visible, emb, kept, sums):
    features, total = a_t.shape
    blocks = gqkv_t.shape[0] // features
    band = len(emb)
    steps = blocks + 3
    s = jax.ShapeDtypeStruct((steps * features, features // 2), BF)
    return pl.pallas_call(
        functools.partial(rest_kernel, band, blocks),
        grid_spec=pltpu.PrefetchScalarGridSpec(
            num_scalar_prefetch=1,
            grid=(1,),
            in_specs=[whole(x.shape) for x in (*kept, *sums, bias)]
            + [FAR] * 4
            + [ANYWHERE] * (2 * band),
            out_specs=[FAR, FAR],
            scratch_shapes=[
                pltpu.VMEM((features, total), BF),
                pltpu.VMEM((blocks, features, total), BF),
                pltpu.VMEM((features, total), BF),
                pltpu.VMEM((features, total), BF),
                pltpu.VMEM((band,) + visible[0].shape, BF),
                pltpu.VMEM((band,) + emb[0].shape, BF),
                pltpu.VMEM((steps, 2, features, features // 2), BF),
                pltpu.SemaphoreType.DMA((3 + blocks + 2 * band,)),
                pltpu.SemaphoreType.DMA((steps, 2)),
            ],
        ),
        out_shape=[s, s],
        cost_estimate=takes(8.0),
        compiler_params=PARAMS,
    )(core, *kept, *sums, bias, a_t, gqkv_t, o_t, gy_t, *visible, *emb)


def done_kernel(count, n_vectors, sides, *refs):
    parts_hbm, refs = refs[:4], refs[4:]
    outs, vectors = refs[: -4 - n_vectors], refs[-4 - n_vectors : -4]
    parts, held, in_sems, sems = refs[-4:]
    size = held.shape[1]
    cut = size // 2
    per_half = count // 2
    loads = []
    for i in range(per_half):
        at = pl.ds(i * size, size)
        pairs = [(ref.at[at, :], parts.at[n, at, :]) for n, ref in enumerate(parts_hbm)]
        loads.append(copies(pairs, in_sems.at[i]))
    places = done_places(size, [out.shape for out in outs])
    made = []
    for n, (row, which, i, j, high) in enumerate(places):
        made.append(
            pltpu.make_async_copy(
                held.at[row // size, pl.ds(row % size, high), :],
                outs[which].at[pl.ds(i, high), pl.ds(j, size)],
                sems.at[n],
            )
        )
    for b in [i + j for i in range(per_half) for j in (0, per_half)]:
        at = slice((b % per_half) * size, (b % per_half + 1) * size)
        if b < per_half:
            for copy in loads[b]:
                copy.wait()
        mine = jnp.where(sides[1] == b // per_half, parts[0, at, :], parts[1, at, :])
        theirs = jnp.where(sides[2] == b // per_half, parts[2, at, :], parts[3, at, :])
        held[b, :, :cut] = jnp.where(sides[0] == 0, mine, theirs).astype(F32)
        held[b, :, cut:] = jnp.where(sides[0] == 0, theirs, mine).astype(F32)
        for copy, place in zip(made, places):
            if place[0] // size == b:
                copy.start()
    row = (places[-1][0] + places[-1][4]) % size
    for ref in vectors:
        for j in range(ref.shape[1] // size):
            for i in range(ref.shape[0]):
                ref[i : i + 1, j * size : (j + 1) * size] = held[count - 1, row : row + 1, :]
                row += 1
    for copy in made:
        copy.wait()


def done_places(size, shapes):
    row, places = 0, []
    for n, (high, wide) in enumerate(shapes):
        for j in range(wide // size):
            for i in range(0, high, size):
                places.append((row, n, i, j * size, min(size, high - i)))
                row += min(size, high - i)
    return places


def done(sides, parts, shapes, vectors=()):
    rows, cut = parts[0].shape
    size = 2 * cut
    count = 2 * rows // size
    return pl.pallas_call(
        functools.partial(done_kernel, count, len(vectors)),
        grid_spec=pltpu.PrefetchScalarGridSpec(
            num_scalar_prefetch=1,
            grid=(1,),
            in_specs=[ANYWHERE] * 4,
            out_specs=[FAR] * len(shapes) + [whole(x) for x in vectors],
            scratch_shapes=[
                pltpu.VMEM((4, rows, cut), BF),
                pltpu.VMEM((count, size, size), F32),
                pltpu.SemaphoreType.DMA((count // 2, 4)),
                pltpu.SemaphoreType.DMA((len(done_places(size, shapes)),)),
            ],
        ),
        out_shape=[jax.ShapeDtypeStruct(x, F32) for x in (*shapes, *vectors)],
        cost_estimate=takes(5.0),
        compiler_params=SMALL_PARAMS,
    )(sides, *parts)


def visible_kernel(moved, own, weight, out):
    back = moved[...] + own[...]
    out[...] = mm_nt(back[0 : out.shape[0]], weight[...]).astype(BF)


def visible_gradient(moved, own, weight, vis_count):
    ins = (moved, own, weight)
    return pl.pallas_call(
        visible_kernel,
        grid=(1,),
        in_specs=[whole(x.shape) for x in ins],
        out_specs=whole((vis_count, weight.shape[0])),
        out_shape=jax.ShapeDtypeStruct((vis_count, weight.shape[0]), BF),
        cost_estimate=takes(3.0),
        compiler_params=SMALL_PARAMS,
    )(*ins)


def add_rows(terms, starts, size):
    total = 0.0
    for term, start in zip(terms, starts):
        total = total + lax.dynamic_slice_in_dim(term, start, size, 0).astype(F32)
    return total.astype(BF)


def join_rows(side, own, got):
    return jnp.where(
        side == 0, jnp.concatenate([own, got], axis=0), jnp.concatenate([got, own], axis=0)
    )


def shift(x, by, size):
    return lax.ppermute(x, "band", [(i, (i + by) % size) for i in range(size)])


def after(x, *others):
    return lax.optimization_barrier((x, *others))[0]


class Ring:
    def __init__(self, dp, band):
        me, z = lax.axis_index("dp"), lax.axis_index("band")
        self.dp = dp
        bits = []
        while (2 << len(bits)) < dp:
            bits.append(len(bits) + 1)
        self.stages = []
        sides = []
        for up, down in zip(bits, reversed(bits)):
            pairs = [(i, i ^ (1 << (down if i & 1 else up))) for i in range(dp)]
            both = ((me >> up) & 1, (me >> down) & 1)
            sides.append(both)
            self.stages.append(("dp", pairs, jnp.where(me & 1 == 1, both[1], both[0])))
        step = 1
        while step < band:
            pairs = [(i, i ^ step) for i in range(band)]
            side = (z // step) & 1
            sides.append((side, side))
            self.stages.append(("band", pairs, side))
            step *= 2
        core = me & 1
        self.core = core.astype(jnp.int32)[None]
        first = sides[0]
        mine = jnp.where(core == 1, first[1], first[0])
        theirs = jnp.where(core == 1, first[0], first[1])
        self.sides = jnp.stack([core, mine, theirs]).astype(jnp.int32)

    def swap_cores(self, x):
        return lax.ppermute(x, "dp", [(i, i ^ 1) for i in range(self.dp)])

    def swap(self, x, i):
        axis, pairs, _side = self.stages[i]
        return lax.ppermute(x, axis, pairs)


class Sum:
    def __init__(self, ring, keep, send):
        self.ring = ring
        zero = jnp.int32(0)
        self.terms, self.starts = [keep], [zero, zero]
        self.base, self.size = zero, keep.shape[0]
        self.stage = 0
        self.last = len(ring.stages)
        self.flight = [ring.swap_cores(send)]

    def rows(self, start):
        return add_rows(self.terms, [start - x for x in self.starts], self.size)

    def left(self):
        return self.stage < 2 * self.last

    def step(self):
        n, last = self.stage, self.last - 1
        self.stage += 1
        if n < last:
            self.terms += self.flight
            side = self.ring.stages[n][2].astype(jnp.int32)
            self.size //= 2
            send = self.rows(self.base + (1 - side) * self.size)
            self.base = self.base + side * self.size
            self.starts.append(self.base)
        elif n == last:
            self.terms += self.flight
            send = self.own = self.rows(self.base)
        elif n <= 2 * last:
            got = self.flight[0]
            if n == last + 1:
                self.own = (self.own.astype(F32) + got.astype(F32)).astype(BF)
            else:
                side = self.ring.stages[2 * last - n + 1][2]
                self.own = join_rows(side, self.own, got)
            send = self.own
        else:
            return self.swap_cores()
        self.flight = [self.ring.swap(send, min(n, 2 * last - n))]
        return send

    def swap_cores(self):
        self.halves = (self.own, self.flight[0])
        self.flight = [self.ring.swap_cores(x) for x in self.halves]
        return self.halves[1]

    def done(self, shapes, vectors=()):
        return done(self.ring.sides, [*self.halves, *self.flight], shapes, vectors)


class Trip:
    def __init__(self, x, band):
        self.band = band
        self.flight = [shift(x, 1, band)]

    def on(self, own):
        going = self.flight[0] + own
        self.flight = [shift(going, 1, self.band)]
        return going


def meet(flights, *others):
    arrays = [x for f in flights for x in f.flight]
    out = lax.optimization_barrier((*arrays, *others))
    at = 0
    for f in flights:
        f.flight = list(out[at : at + len(f.flight)])
        at += len(f.flight)
    return out[at:]


def body(
    dp, band,
    visible, clip_long, patch_order, embed_weight, embed_bias, mask_token,
    norm1_gain, norm1_bias, qkv_weight, qv_bias, proj_weight, proj_bias,
    norm2_gain, norm2_bias, fc1_weight, fc1_bias, fc2_weight, fc2_bias, cotangent,
):
    features = embed_weight.shape[1]
    hidden = fc1_weight.shape[1]
    total = patch_order.shape[1]
    rows = total // band
    vis_count, enc = visible.shape
    z = lax.axis_index("band")
    ring = Ring(dp, band)
    stages = len(ring.stages)

    order = patch_order[0]
    half = vis_count // 2
    middle = total // 2
    visible_at = jnp.where(
        clip_long[0] == 1,
        order[:vis_count],
        jnp.concatenate([order[:half], order[middle : middle + vis_count - half]]),
    )
    notes = jnp.stack(
        [visible_at // 64, visible_at % 64, jnp.broadcast_to(clip_long, (vis_count,))]
    ).astype(BF)
    notes = jnp.pad(notes, ((0, NOTE - 3), (0, enc - vis_count)), mode="edge")
    block = jnp.concatenate([visible, notes], axis=0)
    sources = [((z - k) % band).astype(jnp.int32)[None] for k in range(band)]
    moving = shift(block, 1, band)

    rowid = z * rows + jnp.arange(rows, dtype=jnp.int32)
    places = jnp.stack([row_layout(x, rowid, total)[0] for x in (True, False)])
    quads = z * rows + WIN * jnp.arange(LANES, dtype=jnp.int32)
    positions = []
    for place in (
        row_layout(True, quads, total)[1],
        row_layout(False, quads, total)[1],
        row_layout(True, rowid[:LANES], total)[2],
    ):
        positions += sincos_rows(place, features // 2)
    vectors = (
        mask_token, norm1_gain, norm1_bias, qv_bias, proj_bias, norm2_gain, norm2_bias, fc2_bias,
        embed_bias, fc1_bias,
    )
    cols = stack_columns([x if x.ndim == 2 else x[None] for x in vectors], features)
    weights = (embed_weight, qkv_weight, proj_weight, fc1_weight, fc2_weight, *positions)

    saved, kept, blocks = None, [], [block]
    for k in range(band):
        *saved, sums = forward(
            sources[k], blocks[k], places, cols, cotangent, weights, vis_count, saved
        )
        kept.append(sums)
        if k + 1 < band:
            blocks.append(after(moving, sums))
        if k + 2 < band:
            moving = shift(blocks[-1], 1, band)
    (x_t, a_t, qkv_t, probs, o_t, act_t, gh_t, c_t, x1_t, ch_t, gc_t) = saved

    send, keep, fc1b_grad = ff_gradients(ring.core, act_t, cotangent, c_t, gh_t)
    ff = Sum(ring, keep, send)
    old, emb, sums_b, trip = None, [None] * band, [None] * band, None
    back_order = list(range(1, band)) + [0]
    ready = [send]
    for n, k in enumerate(back_order):
        args = [after(gc_t, *ready), x1_t, cotangent, qkv_t, probs, x_t, ch_t]
        *old, emb[k], sums_b[k] = backward(
            sources[k], block.shape[0], kept[k], cols, args, (proj_weight, qkv_weight), old
        )
        flights = [[ff], [], [ff, trip], [ff, trip]][n]
        emb[k], sums_b[k] = meet(flights, emb[k], sums_b[k])
        ready = [ff.step()] if ff in flights else []
        if n == 0:
            trip = Trip(emb[k], band)
        elif n == 2:
            ready.append(trip.on(emb[back_order[1]]))
    gqkv_t, gy_t = old

    send, keep = rest_gradients(
        ring.core, after(a_t, *ready), gqkv_t, o_t, gy_t, fc1b_grad, blocks, emb, kept, sums_b
    )
    send, keep = meet([ff], send, keep)
    rest = Sum(ring, keep, send)
    ready = [ff.step()]
    meet([rest], *ready)
    block_out, waits, ff_grads = None, 0, None
    ff_shapes = [(hidden, features), (features, hidden)]
    ends = 2 * stages - 1
    outputs = {0: (0, band - 2), 1: (band - 2, 1), ends - 2: (band - 1, 1)}
    for n in range(ends):
        ready = [rest.step()]
        if n and ff.left() and not waits:
            ff.flight[0] = after(ff.flight[0], *ready)
            ready.append(ff.step())
            waits = 1 if ff.stage == ends else 0
        else:
            waits = max(waits - 1, 0)
        flights = [rest] if waits or n == 0 else [rest, ff]
        if n == ends - 1:
            ready.append(trip.on(emb[back_order[2]]))
        if n in outputs:
            block_out = output(
                after(x1_t, *ready), act_t, fc2_weight, fc2_bias[None], *outputs[n], block_out
            )
            (block_out,) = meet(flights, block_out)
        elif n == ends - 1 and not ff.left():
            ff.flight[0] = after(ff.flight[0], *ready)
            ff_grads = meet([rest, trip], *ff.done(ff_shapes))
        elif n == ends - 1:
            meet([rest, trip, ff])
        else:
            meet(flights)
    ready = [rest.step()]
    visible_grad = visible_gradient(
        after(trip.flight[0], *ready), emb[0], embed_weight, vis_count
    )
    (visible_grad,) = meet([rest], visible_grad)
    if ff_grads is None:
        while ff.left():
            ff.step()
        ff_grads = ff.done(ff_shapes)
    fc2_grad, fc1_grad = ff_grads
    row = (1, features)
    (
        qkv_grad, proj_grad, embed_grad,
        projb, qvb, gain1, bias1, mask, embb, gain2, bias2, fc2b, fc1b,
    ) = rest.done(
        [(features, 3 * features), (features, features), (enc, features)],
        [row, (2, features)] + [row] * 7 + [(1, hidden)],
    )
    return (
        block_out,
        visible_grad,
        embed_grad,
        embb[0],
        mask[0],
        gain1[0],
        bias1[0],
        qkv_grad,
        qvb,
        proj_grad,
        projb[0],
        gain2[0],
        bias2[0],
        fc1_grad,
        fc1b[0],
        fc2_grad,
        fc2b[0],
    )


def solution(mesh):
    split = P(("dp", "band"), None)
    in_specs = (split, P(("dp", "band")), split) + (P(),) * 15 + (split,)
    out_specs = (split, split) + (P(),) * 15
    return jax.shard_map(
        functools.partial(body, mesh.shape["dp"], mesh.shape["band"]),
        mesh=mesh,
        in_specs=in_specs,
        out_specs=out_specs,
        check_vma=False,
    )
```

```python
import functools

import jax
import jax.numpy as jnp
from jax import lax
from jax.experimental import pallas as pl
from jax.experimental.pallas import tpu as pltpu
from jax.sharding import PartitionSpec as P

HEADS = 16
FREQ = 8
WIN = 4
EPS = 1e-06
BF = jnp.bfloat16
F32 = jnp.float32
LANES = 128
MIB = 1024 * 1024
SCALE = 1.0
PARAMS = pltpu.CompilerParams(vmem_limit_bytes=59 * MIB)
SMALL_PARAMS = pltpu.CompilerParams(vmem_limit_bytes=28 * MIB)


def takes(microseconds):
    return pl.CostEstimate(
        flops=0, bytes_accessed=int(SCALE * microseconds * 3.3e6), transcendentals=0
    )


def row_layout(is_long, rowid, row_count):
    quarter = row_count // 4
    span = row_count // (2 * FREQ)
    halfspan = span // 2
    target = rowid // quarter
    inner = rowid % quarter
    column = target // 2 * WIN + inner % WIN
    local = inner // WIN
    halves = target % 2
    if is_long:
        frame_time = halves * span + local
        frame = frame_time
    else:
        frame_time = halves * halfspan + local % halfspan
        frame = local // halfspan * span + frame_time
    return frame * FREQ + column, frame_time, column


def sincos_rows(places, features):
    halfway = features // 2
    omega = 1.0 / 10000.0 ** (jnp.arange(halfway, dtype=F32) / halfway)
    angles = omega[:, None] * places.astype(F32)[None, :]
    return jnp.sin(angles), jnp.cos(angles)


def mm(a, b):
    return lax.dot_general(a, b, (((1,), (0,)), ((), ())), preferred_element_type=F32)


def mm_nt(a, b):
    return lax.dot_general(a, b, (((1,), (1,)), ((), ())), preferred_element_type=F32)


def window_of_lane(rows, columns):
    lane = lax.broadcasted_iota(jnp.int32, (rows, columns), 1)
    return (lane % LANES) // (WIN * WIN)


def compact(square, win):
    size = WIN * WIN
    out = square[0:size]
    for w in range(1, LANES // size):
        out = jnp.where(win == w, square[w * size : (w + 1) * size], out)
    return out


def expand(rows, win):
    size = WIN * WIN
    return jnp.concatenate(
        [jnp.where(win == w, rows, 0.0).astype(BF) for w in range(LANES // size)], axis=0
    )


def stacked(wide):
    return jnp.concatenate(
        [wide[:, j * LANES : (j + 1) * LANES] for j in range(wide.shape[1] // LANES)], axis=0
    )


def heads_apart(group, width):
    count = LANES // width
    blocks = []
    for j in range(count):
        parts = []
        if j:
            parts.append(jnp.zeros((j * width, LANES), BF))
        parts.append(group[j * width : (j + 1) * width])
        if j < count - 1:
            parts.append(jnp.zeros(((count - 1 - j) * width, LANES), BF))
        blocks.append(jnp.concatenate(parts, axis=0))
    return jnp.concatenate(blocks, axis=1)


def heads_of(wide, width):
    return jnp.concatenate(
        [
            wide[j * width : (j + 1) * width, j * LANES : (j + 1) * LANES]
            for j in range(LANES // width)
        ],
        axis=0,
    )


def normalize_t(x):
    count = x.shape[0]
    center = x - jnp.sum(x, axis=0, keepdims=True) * (1.0 / count)
    var = jnp.sum(center * center, axis=0, keepdims=True) * (1.0 / count)
    scale = lax.rsqrt(var + EPS)
    return center * scale, scale


def normalize_back_t(grad, unit, scale, gain):
    count = grad.shape[0]
    inner = grad * gain
    mean = jnp.sum(inner, axis=0, keepdims=True) * (1.0 / count)
    mixed = jnp.sum(inner * unit, axis=0, keepdims=True) * (1.0 / count)
    return scale * (inner - mean - unit * mixed)


def mm_tn(a, b):
    return lax.dot_general(a, b, (((0,), (0,)), ((), ())), preferred_element_type=F32)


def mm_tt(a, b):
    return lax.dot_general(a, b, (((0,), (1,)), ((), ())), preferred_element_type=F32)


def columns_kernel(*refs):
    vectors, out = refs[:-1], refs[-1]
    width = out.shape[1]
    out[...] = jnp.zeros_like(out)
    row = 0
    for ref in vectors:
        for i in range(ref.shape[0]):
            for j in range(ref.shape[1] // width):
                out[row : row + 1, :] = ref[i : i + 1, j * width : (j + 1) * width]
                row += 1


def stack_columns(vectors, width):
    return pl.pallas_call(
        columns_kernel,
        out_shape=jax.ShapeDtypeStruct((N_COLS, width), F32),
        cost_estimate=takes(2.0),
    )(*vectors)


def expand_exactly(table, ones):
    high = table.astype(BF)
    rest = table - high.astype(F32)
    middle = rest.astype(BF)
    low = (rest - middle.astype(F32)).astype(BF)
    return mm(high, ones) + (mm(middle, ones) + mm(low, ones))


def lane_sums(acc):
    return jnp.sum(acc.T, axis=0, keepdims=True)


def lanes(t):
    return slice(t * LANES, (t + 1) * LANES)


def copies(pairs, sems, start=True):
    made = [pltpu.make_async_copy(a, b, sems.at[i]) for i, (a, b) in enumerate(pairs)]
    if start:
        for copy in made:
            copy.start()
    return made


C_MASK, C_G1, C_B1, C_QB, C_VB, C_PB, C_G2, C_B2, C_F2B, C_EB, C_F1B = range(11)
N_COLS = 16
N_WEIGHTS = 11
N_SAVED = 11
NOTE = 8


class Block:
    def __init__(self, features, rows):
        self.features, self.rows = features, rows
        self.tiles = rows // LANES
        self.half = rows // 2
        self.per_half = self.tiles // 2
        self.groups = features // LANES
        self.width = features // HEADS
        self.factor = self.width ** (-0.5)
        self.chunk = features // 2

    def of_half(self, h):
        return range(h * self.per_half, (h + 1) * self.per_half)

    def part(self, h):
        return slice(h * self.half, (h + 1) * self.half)

    def chunks(self, size):
        return [slice(i, i + self.chunk) for i in range(0, size, self.chunk)]

    def group(self, base, g):
        return slice(base + g * LANES, base + (g + 1) * LANES)


def forward_kernel(vis_count, aliased, sk, *refs):
    (cols_hbm, places_hbm, v_hbm, cot_hbm, *w_hbm) = refs[: 4 + N_WEIGHTS]
    refs = refs[4 + N_WEIGHTS + (N_SAVED if aliased else 0) :]
    out_hbm, sums_hbm, refs = refs[:N_SAVED], refs[N_SAVED], refs[N_SAVED + 1 :]
    saved, refs = refs[:N_SAVED], refs[N_SAVED:]
    (x_t, a_t, qkv_t, probs, o_t, act_t, gh_t, c_t, x1_t, ch_t, gc_t) = saved
    held, refs = refs[:7], refs[7:]
    (wemb, wqkv, wproj, w1, w2, tables, pos) = held
    (places, cols, sums, v_pad, colb, e_t, wide, cot, cot_t, scores) = refs[:10]
    (in_sems, first_sems, out_sems, half_sems) = refs[10:]
    features, rows = x_t.shape
    k = Block(features, rows)
    source = sk[0]
    always = source >= 0
    row_at = pl.ds(pl.multiple_of(source * rows, rows), rows)

    count = v_hbm.shape[0]
    first = copies(
        [
            (cols_hbm, cols),
            (places_hbm, places),
            (v_hbm, v_pad.at[pl.ds(0, count), :]),
            (cot_hbm.at[row_at, :], cot),
        ],
        first_sems,
        start=False,
    )
    pairs = list(zip(w_hbm, held))[:5]
    quarter = features // 4
    for i, ref in enumerate(w_hbm[5:]):
        pairs.append((ref, tables.at[i // 2, pl.ds(i % 2 * quarter, quarter), :]))
    loads = copies(pairs, in_sems, start=False)
    loads = [loads[0], *loads[5:], *loads[1:5]]
    for copy in (*first[:3], loads[0], first[3], *loads[1:]):
        copy.start()
    views = [ref.at[source] if i == 3 else ref.at[:, row_at] for i, ref in enumerate(out_hbm)]
    stores = [
        None if i in (5, 6) else pltpu.make_async_copy(a, b, out_sems.at[i])
        for i, (a, b) in enumerate(zip(saved, views))
    ]
    sums_store = pltpu.make_async_copy(sums, sums_hbm, out_sems.at[N_SAVED])
    halves = []
    for h in range(2):
        at = pl.ds(pl.multiple_of(source * rows + h * k.half, k.half), k.half)
        pairs = [(saved[i].at[:, k.part(h)], out_hbm[i].at[:, at]) for i in (5, 6)]
        halves.append(copies(pairs, half_sems.at[h], start=False))

    v_pad[count:, :] = jnp.zeros((v_pad.shape[0] - count, v_pad.shape[1]), BF)
    sums[...] = jnp.zeros_like(sums)
    first[0].wait()
    columns = cols[...].T
    for i in range(C_F1B + 4):
        colb[i] = jnp.broadcast_to(columns[:, i : i + 1], (features, LANES))
    first[1].wait()
    first[2].wait()
    note = v_pad[count - 16 : count, 0:rows].astype(F32)
    is_long = note[NOTE + 2 : NOTE + 3, :] > 0.5
    for copy in loads[:7]:
        copy.wait()

    @pl.when(always)
    def _():
        embedded = mm_tt(wemb[...], v_pad[...])
        at = lax.broadcasted_iota(jnp.int32, (LANES, rows), 0)
        row = lax.broadcasted_iota(jnp.int32, (LANES, rows), 1)
        times = jnp.where(is_long[:, 0:LANES], tables[0], tables[1])
        spread = (jnp.where(row // WIN == at, 1.0, 0.0), jnp.where(row % WIN == at, 1.0, 0.0))
        for i, (table, ones) in enumerate(zip((times, tables[2]), spread)):
            place = slice(i * features // 2, (i + 1) * features // 2)
            pos[place, :] = expand_exactly(table, ones.astype(BF))
        note_t = note.T
        index = lax.broadcasted_iota(jnp.int32, (rows, 1), 0)
        patch = note_t[:, NOTE : NOTE + 1] * 64.0 + note_t[:, NOTE + 1 : NOTE + 2]
        patch = jnp.where(index < vis_count, patch.astype(jnp.int32), -1)
        place = jnp.where(is_long, places[0:1, :], places[1:2, :])
        for t in range(k.tiles):
            chosen = jnp.where(patch == place[:, lanes(t)], 1.0, 0.0)
            ch_t[:, lanes(t)] = chosen.astype(BF)
            sums[1:2, lanes(t)] = jnp.sum(chosen, axis=0, keepdims=True)
        for t in range(k.tiles):
            e_t[:, lanes(t)] = (embedded[:, lanes(t)] + colb[C_EB]).astype(BF)
        for h in range(2):
            wide[:, k.part(h)] = mm(e_t[...], ch_t[:, k.part(h)])

    stores[9].start()
    first[3].wait()
    win = window_of_lane(WIN * WIN, 4 * LANES)

    def entry(t):
        start = (wide[:, lanes(t)] + (1.0 - sums[1:2, lanes(t)]) * colb[C_MASK]) + pos[:, lanes(t)]
        start = start.astype(BF)
        x_t[:, lanes(t)] = start
        unit, _scale = normalize_t(start.astype(F32))
        a_t[:, lanes(t)] = (unit * colb[C_G1] + colb[C_B1]).astype(BF)
        cot_t[:, lanes(t)] = cot[t * LANES : (t + 1) * LANES, :].T

    def project(h, parts):
        for n in parts:
            chunk = slice(n * k.chunk, (n + 1) * k.chunk)
            prod = mm_tn(wqkv[:, chunk], a_t[:, k.part(h)])
            bias = (C_QB, None, C_VB)[n // 2]
            for u, t in enumerate(k.of_half(h)):
                piece = prod[:, lanes(u)]
                if bias is not None:
                    piece = piece + colb[bias, slice((n % 2) * k.chunk, (n % 2 + 1) * k.chunk)]
                qkv_t[chunk, lanes(t)] = piece.astype(BF)

    def score(t):
        for g in range(k.groups):
            q_g = qkv_t[k.group(0, g), lanes(t)]
            k_g = qkv_t[k.group(features, g), lanes(t)]
            scores[t * k.groups + g] = compact(mm(k_g.T, heads_apart(q_g, k.width)), win)

    def soften(t):
        for g in range(k.groups):
            logits = scores[t * k.groups + g] * k.factor
            shifted = jnp.exp(logits - jnp.max(logits, axis=0, keepdims=True))
            prob = shifted / jnp.sum(shifted, axis=0, keepdims=True)
            probs[t, :, g * 4 * LANES : (g + 1) * 4 * LANES] = prob

    def mix(t):
        for g in range(k.groups):
            prob = probs[t, :, g * 4 * LANES : (g + 1) * 4 * LANES]
            mixed = mm(qkv_t[k.group(2 * features, g), lanes(t)], expand(prob, win))
            o_t[k.group(0, g), lanes(t)] = heads_of(mixed, k.width).astype(BF)

    def grow(h):
        wide[:, k.part(h)] = mm_tn(wproj[...], o_t[:, k.part(h)])

    def norm2(t):
        x1 = x_t[:, lanes(t)].astype(F32) + (wide[:, lanes(t)] + colb[C_PB])
        x1_t[:, lanes(t)] = x1
        unit, _scale = normalize_t(x1)
        c_t[:, lanes(t)] = (unit * colb[C_G2] + colb[C_B2]).astype(BF)

    def hidden(h, parts):
        for n in parts:
            chunk = slice(n * k.chunk, (n + 1) * k.chunk)
            grown = mm_tn(w1[:, chunk], c_t[:, k.part(h)])
            gact = mm(w2[chunk, :], cot_t[:, k.part(h)])
            rows_of = slice((n % 2) * k.chunk, (n % 2 + 1) * k.chunk)
            for u, t in enumerate(k.of_half(h)):
                own = grown[:, lanes(u)] + colb[C_F1B + n // 2, rows_of]
                cumulative = 0.5 * (1.0 + lax.erf(own * 0.7071067811865476))
                act_t[chunk, lanes(t)] = (own * cumulative).astype(BF)
                slope = cumulative + own * jnp.exp(-0.5 * own * own) * 0.3989422804014327
                gh_t[chunk, lanes(t)] = (gact[:, lanes(u)] * slope).astype(BF)

    def hidden_back(h):
        gc_t[:, k.part(h)] = mm(w1[...], gh_t[:, k.part(h)])

    @pl.when(always)
    def _():
        entry(0)
        entry(1)

    loads[7].wait()

    @pl.when(always)
    def _():
        project(0, range(6))
        entry(2)
        entry(3)
        total = cot_t[:, 0:LANES].astype(F32)
        for t in range(1, k.tiles):
            total += cot_t[:, lanes(t)].astype(F32)
        sums[0:1, :] = lane_sums(total)

    sums_store.start()
    stores[0].start()
    stores[1].start()

    @pl.when(always)
    def _():
        score(0)
        score(1)
        project(1, range(0, 3))
        soften(0)
        mix(0)
        project(1, range(3, 6))
        soften(1)
        mix(1)

    stores[2].start()
    loads[8].wait()

    @pl.when(always)
    def _():
        score(2)
        score(3)
        grow(0)
        soften(2)
        mix(2)
        norm2(0)
        soften(3)
        mix(3)
        norm2(1)

    stores[3].start()
    stores[4].start()
    loads[9].wait()
    loads[10].wait()

    @pl.when(always)
    def _():
        grow(1)
        hidden(0, range(0, 4))
        norm2(2)
        norm2(3)
        hidden(0, range(4, 8))

    stores[7].start()
    stores[8].start()
    for copy in halves[0]:
        copy.start()

    @pl.when(always)
    def _():
        hidden(1, range(0, 4))
        hidden_back(0)
        hidden(1, range(4, 8))

    for copy in halves[1]:
        copy.start()

    @pl.when(always)
    def _():
        hidden_back(1)

    stores[10].start()
    for copy in stores:
        if copy is not None:
            copy.wait()
    for copy in (*halves[0], *halves[1], sums_store):
        copy.wait()


def backward_kernel(aliased, sk, *refs):
    (cols_hbm, kept_hbm, *in_hbm) = refs[:9]
    w_hbm = refs[9:11]
    refs = refs[11 + (2 if aliased else 0) :]
    gqkv_hbm, gy_hbm, gemb_hbm, sums_hbm = refs[:4]
    (gc_t, x1_t, cot, qkv_t, probs, x_t, ch_t) = refs[4:11]
    (wproj, wqkv) = refs[11:13]
    (kept, cols, gemb, sums, gqkv_t, gy_t, colb, gx1_t, go_t, gx_t, hot, wide, acc) = refs[13:26]
    (in_sems, w_sems, out_sems) = refs[26:]
    features, rows = x_t.shape
    k = Block(features, rows)
    source = sk[0]
    always = source >= 0
    row_at = pl.ds(pl.multiple_of(source * rows, rows), rows)
    views = []
    for i, ref in enumerate(in_hbm):
        views.append(ref.at[row_at, :] if i == 2 else ref.at[source] if i == 4 else ref.at[:, row_at])
    pairs = [*zip(views, refs[4:11]), (kept_hbm, kept)]
    pairs.append((cols_hbm, cols))
    loads = copies(pairs, in_sems, start=False)
    w_loads = copies(zip(w_hbm, refs[11:13]), w_sems, start=False)
    for copy in (*loads[8:], *loads[:3], w_loads[0], *loads[3:8], w_loads[1]):
        copy.start()
    stores = copies(
        [
            (gqkv_t, gqkv_hbm.at[:, row_at]),
            (gy_t, gy_hbm.at[:, row_at]),
            (gemb, gemb_hbm),
            (sums, sums_hbm),
        ],
        out_sems,
        start=False,
    )

    def add(i, at, value, begin):
        if begin:
            acc[i, at] = value
        else:
            acc[i, at] += value

    everything = slice(0, features)
    sums[...] = jnp.zeros_like(sums)
    loads[8].wait()
    columns = cols[...].T
    for n, i in enumerate((C_G1, C_G2)):
        colb[n] = jnp.broadcast_to(columns[:, i : i + 1], (features, LANES))
    for copy in loads[:3]:
        copy.wait()
    win = window_of_lane(WIN * WIN, 4 * LANES)

    def norm2_back(t):
        gc = gc_t[:, lanes(t)]
        unit, scale = normalize_t(x1_t[:, lanes(t)])
        add(7, everything, gc * unit, t == 0)
        add(8, everything, gc, t == 0)
        own = cot[t * LANES : (t + 1) * LANES, :].T.astype(F32)
        gx1 = own + normalize_back_t(gc, unit, scale, colb[1])
        gx1_t[:, lanes(t)] = gx1
        low = gx1.astype(BF)
        gy_t[:, lanes(t)] = low
        add(0, everything, low.astype(F32), t == 0)

    def branch(h):
        go_t[:, k.part(h)] = mm(wproj[...], gy_t[:, k.part(h)]).astype(BF)

    def probs_grad(t):
        for g in range(k.groups):
            v_g = qkv_t[k.group(2 * features, g), lanes(t)]
            go_g = go_t[k.group(0, g), lanes(t)]
            hot[t * k.groups + g] = compact(mm(v_g.T, heads_apart(go_g, k.width)), win)

    def score_grad(t):
        for g in range(k.groups):
            gp = hot[t * k.groups + g]
            prob = probs[t, :, g * 4 * LANES : (g + 1) * 4 * LANES]
            hot[t * k.groups + g] = prob * (gp - jnp.sum(gp * prob, axis=0, keepdims=True))

    def row_grads(t):
        products = []
        for g in range(k.groups):
            q_g = qkv_t[k.group(0, g), lanes(t)]
            k_g = qkv_t[k.group(features, g), lanes(t)]
            go_g = go_t[k.group(0, g), lanes(t)]
            gs = expand(hot[t * k.groups + g], win)
            prob = expand(probs[t, :, g * 4 * LANES : (g + 1) * 4 * LANES], win)
            products.append((mm(k_g, gs), mm_nt(q_g, stacked(gs)), mm_nt(go_g, stacked(prob))))
        for g, (gq, gk, gv) in enumerate(products):
            gq = (heads_of(gq, k.width) * k.factor).astype(BF)
            gk = (heads_of(gk, k.width) * k.factor).astype(BF)
            gv = heads_of(gv, k.width).astype(BF)
            gqkv_t[k.group(0, g), lanes(t)] = gq
            gqkv_t[k.group(features, g), lanes(t)] = gk
            gqkv_t[k.group(2 * features, g), lanes(t)] = gv
            add(1, k.group(0, g), gq.astype(F32), t == 0)
            add(2, k.group(0, g), gv.astype(F32), t == 0)

    def project_back(h):
        wide[:, k.part(h)] = mm(wqkv[...], gqkv_t[:, k.part(h)])

    def norm1_back(t):
        ga = wide[:, lanes(t)]
        unit, scale = normalize_t(x_t[:, lanes(t)].astype(F32))
        add(3, everything, ga * unit, t == 0)
        add(4, everything, ga, t == 0)
        low = (gx1_t[:, lanes(t)] + normalize_back_t(ga, unit, scale, colb[0])).astype(BF)
        gx_t[:, lanes(t)] = low
        own = low.astype(F32)
        filled = kept[1:2, lanes(t)]
        add(5, everything, own * (1.0 - filled), t == 0)
        add(6, everything, own * filled, t == 0)

    @pl.when(always)
    def _():
        norm2_back(0)
        norm2_back(1)

    w_loads[0].wait()
    loads[3].wait()
    loads[4].wait()

    @pl.when(always)
    def _():
        branch(0)
        norm2_back(2)
        norm2_back(3)
        for i in (0, 7, 8):
            sums[i : i + 1, :] = lane_sums(acc[i])

    stores[1].start()

    @pl.when(always)
    def _():
        probs_grad(0)
        probs_grad(1)
        branch(1)
        score_grad(0)
        row_grads(0)
        score_grad(1)
        row_grads(1)

    loads[5].wait()
    loads[6].wait()
    loads[7].wait()
    w_loads[1].wait()

    @pl.when(always)
    def _():
        probs_grad(2)
        probs_grad(3)
        project_back(0)
        score_grad(2)
        row_grads(2)
        norm1_back(0)
        score_grad(3)
        row_grads(3)
        norm1_back(1)

    stores[0].start()

    @pl.when(always)
    def _():
        project_back(1)
        for i in (1, 2):
            sums[i : i + 1, :] = lane_sums(acc[i])
        norm1_back(2)
        norm1_back(3)

    @pl.when(always)
    def _():
        chosen = mm_nt(ch_t[...], gx_t[...]).astype(BF)
        for i in (3, 4, 5, 6):
            sums[i : i + 1, :] = lane_sums(acc[i])
        gemb[...] = chosen[0 : gemb.shape[0]]

    stores[2].start()
    stores[3].start()
    for copy in stores:
        copy.wait()


def whole(shape):
    zeros = (0,) * len(shape)
    return pl.BlockSpec(shape, lambda *_: zeros)


FAR = pl.BlockSpec(memory_space=pltpu.HBM)
ANYWHERE = pl.BlockSpec(memory_space=pl.ANY)


def forward(sk, v, places, cols, cot, weights, vis_count, old):
    rows = places.shape[1]
    features = cols.shape[1]
    total = cot.shape[0]
    hidden = weights[4].shape[0]
    tiles = rows // LANES
    wide_probs = HEADS * LANES
    s = jax.ShapeDtypeStruct
    saved = [
        ((features,), BF),
        ((features,), BF),
        ((3 * features,), BF),
        None,
        ((features,), BF),
        ((hidden,), BF),
        ((hidden,), BF),
        ((features,), BF),
        ((features,), F32),
        ((rows,), BF),
        ((features,), F32),
    ]
    probs = (tiles, WIN * WIN, wide_probs)
    out_shape = [
        s((total // rows,) + probs, F32) if x is None else s(x[0] + (total,), x[1]) for x in saved
    ] + [s((8, features), F32)]
    scratch = [
        pltpu.VMEM(probs, F32) if x is None else pltpu.VMEM(x[0] + (rows,), x[1]) for x in saved
    ] + [
        *[pltpu.VMEM(w.shape, w.dtype) for w in weights[:5]],
        pltpu.VMEM((3, features // 2, LANES), F32),
        pltpu.VMEM((features, rows), F32),
        pltpu.VMEM(places.shape, places.dtype),
        pltpu.VMEM((N_COLS, features), F32),
        pltpu.VMEM((8, features), F32),
        pltpu.VMEM((rows, v.shape[1]), BF),
        pltpu.VMEM((C_F1B + 4, features, LANES), F32),
        pltpu.VMEM((features, rows), BF),
        pltpu.VMEM((features, rows), F32),
        pltpu.VMEM((rows, features), BF),
        pltpu.VMEM((features, rows), BF),
        pltpu.VMEM((tiles * features // LANES, WIN * WIN, 4 * LANES), F32),
        pltpu.SemaphoreType.DMA((N_WEIGHTS,)),
        pltpu.SemaphoreType.DMA((4,)),
        pltpu.SemaphoreType.DMA((N_SAVED + 1,)),
        pltpu.SemaphoreType.DMA((2, 2)),
    ]
    old = list(old or ())
    ins = [cols, places, v, cot, *weights]
    return pl.pallas_call(
        functools.partial(forward_kernel, vis_count, bool(old)),
        grid_spec=pltpu.PrefetchScalarGridSpec(
            num_scalar_prefetch=1,
            grid=(1,),
            in_specs=[ANYWHERE] * 3 + [FAR] * (len(ins) - 3 + len(old)),
            out_specs=[FAR] * (N_SAVED + 1),
            scratch_shapes=scratch,
        ),
        out_shape=out_shape,
        input_output_aliases={1 + len(ins) + i: i for i in range(len(old))},
        cost_estimate=takes(13.5),
        compiler_params=PARAMS,
    )(sk, *ins, *old)


def backward(sk, count, kept, cols, saved, weights, old):
    gc_t, x1_t, cot, qkv_t, probs, x_t, ch_t = saved
    features, total = x_t.shape
    rows = ch_t.shape[0]
    tiles = rows // LANES
    s = jax.ShapeDtypeStruct
    old = list(old or ())
    ins = [cols, kept, *saved, *weights]
    return pl.pallas_call(
        functools.partial(backward_kernel, bool(old)),
        grid_spec=pltpu.PrefetchScalarGridSpec(
            num_scalar_prefetch=1,
            grid=(1,),
            in_specs=[ANYWHERE] * 2 + [FAR] * (len(ins) - 2 + len(old)),
            out_specs=[FAR] * 4,
            scratch_shapes=[
            pltpu.VMEM((features, rows), F32),
            pltpu.VMEM((features, rows), F32),
            pltpu.VMEM((rows, features), BF),
            pltpu.VMEM((3 * features, rows), BF),
            pltpu.VMEM(probs.shape[1:], F32),
            pltpu.VMEM((features, rows), BF),
            pltpu.VMEM((rows, rows), BF),
        ]
        + [pltpu.VMEM(w.shape, BF) for w in weights]
        + [
            pltpu.VMEM(kept.shape, F32),
            pltpu.VMEM(cols.shape, F32),
            pltpu.VMEM((count, features), BF),
            pltpu.VMEM((16, features), F32),
            pltpu.VMEM((3 * features, rows), BF),
            pltpu.VMEM((features, rows), BF),
            pltpu.VMEM((2, features, LANES), F32),
            pltpu.VMEM((features, rows), F32),
            pltpu.VMEM((features, rows), BF),
            pltpu.VMEM((features, rows), BF),
            pltpu.VMEM((tiles * features // LANES, WIN * WIN, 4 * LANES), F32),
            pltpu.VMEM((features, rows), F32),
            pltpu.VMEM((9, features, LANES), F32),
            pltpu.SemaphoreType.DMA((len(saved) + 2,)),
            pltpu.SemaphoreType.DMA((len(weights),)),
            pltpu.SemaphoreType.DMA((4,)),
        ],
        ),
        out_shape=[
            s((3 * features, total), BF),
            s((features, total), BF),
            s((count, features), BF),
            s((16, features), F32),
        ],
        input_output_aliases={1 + len(ins) + i: i for i in range(len(old))},
        cost_estimate=takes(12.0),
        compiler_params=PARAMS,
    )(sk, *ins, *old)


def output_kernel(aliased, x1_t, act_t, w2, bias, *refs):
    out = refs[-1]
    column = jnp.broadcast_to(bias[...], (8, bias.shape[1])).T[:, 0:1]
    for t in range(x1_t.shape[1] // LANES):
        if t % 2 == 0:
            grown = mm_tn(w2[...], act_t[:, t * LANES : (t + 2) * LANES])
        total = x1_t[:, lanes(t)] + (grown[:, lanes(t % 2)] + column)
        out[t * LANES : (t + 1) * LANES, :] = total.astype(BF).T


def output(x1_t, act_t, w2, bias, first, steps, old):
    features, total = x1_t.shape
    hidden = act_t.shape[0]
    rows = features
    old = [] if old is None else [old]
    return pl.pallas_call(
        functools.partial(output_kernel, bool(old)),
        grid=(steps,),
        in_specs=[
            pl.BlockSpec((features, rows), lambda i: (0, i + first)),
            pl.BlockSpec((hidden, rows), lambda i: (0, i + first)),
            whole(w2.shape),
            whole((1, features)),
        ]
        + [FAR] * len(old),
        out_specs=pl.BlockSpec((rows, features), lambda i: (i + first, 0)),
        out_shape=jax.ShapeDtypeStruct((total, features), BF),
        input_output_aliases={4: 0} if old else {},
        cost_estimate=takes(3.0 * steps),
        compiler_params=PARAMS,
    )(x1_t, act_t, w2, bias, *old)


def to_halves(core, low, send, keep, at=slice(None)):
    cut = low.shape[1] // 2
    left, right = low[:, :cut], low[:, cut:]
    send[at, :] = jnp.where(core == 0, right, left)
    keep[at, :] = jnp.where(core == 0, left, right)


def ff_kernel(steps, core, act, cot_hbm, c_hbm, gh, send, keep, bias, left, cot, c, out, sems, out_sems):
    size = out.shape[2]

    def load(i):
        source = act if i < steps else gh
        at = pl.ds((i % steps) * size, size)
        return pltpu.make_async_copy(source.at[at, :], left.at[i], sems.at[i])

    def stored(i):
        at = pl.ds(pl.multiple_of(i * size, size), size)
        return [
            pltpu.make_async_copy(out.at[i, n], ref.at[at, :], out_sems.at[i, n])
            for n, ref in enumerate((send, keep))
        ]

    def finish(i, product):
        to_halves(core[0], product.astype(BF), out.at[i, 0], out.at[i, 1])
        for copy in stored(i):
            copy.start()

    cot_load = pltpu.make_async_copy(cot_hbm, cot, sems.at[2 * steps])
    c_load = pltpu.make_async_copy(c_hbm, c, sems.at[2 * steps + 1])
    cot_load.start()
    for i in range(2 * steps):
        load(i).start()
        if i == steps - 1:
            c_load.start()
    cot_load.wait()
    always = core[0] >= 0
    for i in range(2 * steps):
        load(i).wait()
        if i == steps:
            c_load.wait()

        @pl.when(always)
        def _():
            if i < steps:
                finish(i, mm(left[i], cot[...]))
            else:
                finish(i, mm_nt(c[...], left[i]))
                total = left[i, :, 0:LANES].astype(F32)
                for t in range(1, left.shape[2] // LANES):
                    total += left[i, :, lanes(t)].astype(F32)
                bias[i - steps] = jnp.sum(total.T, axis=0, keepdims=True)

    for i in range(2 * steps):
        for copy in stored(i):
            copy.wait()


def ff_gradients(core, act_t, cot, c_t, gh_t):
    hidden, total = act_t.shape
    features = cot.shape[1]
    steps = hidden // features
    s = jax.ShapeDtypeStruct
    return pl.pallas_call(
        functools.partial(ff_kernel, steps),
        grid_spec=pltpu.PrefetchScalarGridSpec(
            num_scalar_prefetch=1,
            grid=(1,),
            in_specs=[FAR] * 4,
            out_specs=[FAR, FAR, whole((steps, 1, features))],
            scratch_shapes=[
                pltpu.VMEM((2 * steps, features, total), BF),
                pltpu.VMEM(cot.shape, BF),
                pltpu.VMEM(c_t.shape, BF),
                pltpu.VMEM((2 * steps, 2, features, features // 2), BF),
                pltpu.SemaphoreType.DMA((2 * steps + 2,)),
                pltpu.SemaphoreType.DMA((2 * steps, 2)),
            ],
        ),
        out_shape=[
            s((2 * hidden, features // 2), BF),
            s((2 * hidden, features // 2), BF),
            s((steps, 1, features), F32),
        ],
        cost_estimate=takes(11.0),
        compiler_params=PARAMS,
    )(core, act_t, cot, c_t, gh_t)


def rest_kernel(band, blocks, core, *refs):
    (kept, sums), refs = (refs[:band], refs[band : 2 * band]), refs[2 * band :]
    (bias, a_hbm, gqkv_hbm, o_hbm, gy_hbm), refs = refs[:5], refs[5:]
    v_hbm, emb_hbm, refs = refs[:band], refs[band : 2 * band], refs[2 * band :]
    (send, keep, a, gqkv, o, gy, visible, emb, out, sems, out_sems) = refs
    size = out.shape[2]
    pairs = [(a_hbm, a)]
    for i in range(blocks):
        pairs.append((gqkv_hbm.at[pl.ds(i * size, size), :], gqkv.at[i]))
    pairs += [(o_hbm, o), (gy_hbm, gy)]
    for n in range(band):
        pairs += [(v_hbm[n], visible.at[n]), (emb_hbm[n], emb.at[n])]
    loads = copies(pairs, sems, start=False)
    for copy in loads:
        copy.start()
    always = core[0] >= 0

    def stored(i):
        at = pl.ds(i * size, size)
        return [
            pltpu.make_async_copy(out.at[i, n], ref.at[at, :], out_sems.at[i, n])
            for n, ref in enumerate((send, keep))
        ]

    def finish(i, low, at=slice(None)):
        to_halves(core[0], low, out.at[i, 0], out.at[i, 1], at)

    loads[0].wait()
    for i in range(blocks):
        loads[1 + i].wait()

        @pl.when(always)
        def _():
            finish(i, mm_nt(a[...], gqkv[i]).astype(BF))

        for copy in stored(i):
            copy.start()
    for copy in loads[1 + blocks :]:
        copy.wait()

    @pl.when(always)
    def _():
        finish(blocks, mm_nt(o[...], gy[...]).astype(BF))

    for copy in stored(blocks):
        copy.start()

    def embed(at):
        total = mm_tn(visible[0, :, at], emb[0])
        for n in range(1, band):
            total = total + mm_tn(visible[n, :, at], emb[n])
        return total.astype(BF)

    @pl.when(always)
    def _():
        over = visible.shape[2] - size
        finish(blocks + 1, embed(slice(0, size)))
        finish(blocks + 2, embed(slice(size, size + over)), slice(0, over))
        ours, cots = sums[0][0:9, :], kept[0][0:1, :]
        for n in range(1, band):
            ours = ours + sums[n][0:9, :]
            cots = cots + kept[n][0:1, :]
        hidden = [bias[n] for n in range(bias.shape[0])]
        rest = jnp.zeros((size - over - 10 - bias.shape[0], size), F32)
        small = jnp.concatenate([ours, cots, *hidden, rest], axis=0)
        finish(blocks + 2, small.astype(BF), slice(over, size))

    for i in range(blocks + 1, blocks + 3):
        for copy in stored(i):
            copy.start()
    for i in range(blocks + 3):
        for copy in stored(i):
            copy.wait()


def rest_gradients(core, a_t, gqkv_t, o_t, gy_t, bias, visible, emb, kept, sums):
    features, total = a_t.shape
    blocks = gqkv_t.shape[0] // features
    band = len(emb)
    steps = blocks + 3
    s = jax.ShapeDtypeStruct((steps * features, features // 2), BF)
    return pl.pallas_call(
        functools.partial(rest_kernel, band, blocks),
        grid_spec=pltpu.PrefetchScalarGridSpec(
            num_scalar_prefetch=1,
            grid=(1,),
            in_specs=[whole(x.shape) for x in (*kept, *sums, bias)]
            + [FAR] * 4
            + [ANYWHERE] * (2 * band),
            out_specs=[FAR, FAR],
            scratch_shapes=[
                pltpu.VMEM((features, total), BF),
                pltpu.VMEM((blocks, features, total), BF),
                pltpu.VMEM((features, total), BF),
                pltpu.VMEM((features, total), BF),
                pltpu.VMEM((band,) + visible[0].shape, BF),
                pltpu.VMEM((band,) + emb[0].shape, BF),
                pltpu.VMEM((steps, 2, features, features // 2), BF),
                pltpu.SemaphoreType.DMA((3 + blocks + 2 * band,)),
                pltpu.SemaphoreType.DMA((steps, 2)),
            ],
        ),
        out_shape=[s, s],
        cost_estimate=takes(8.0),
        compiler_params=PARAMS,
    )(core, *kept, *sums, bias, a_t, gqkv_t, o_t, gy_t, *visible, *emb)


def done_kernel(count, n_vectors, sides, *refs):
    parts_hbm, refs = refs[:4], refs[4:]
    outs, vectors = refs[: -4 - n_vectors], refs[-4 - n_vectors : -4]
    parts, held, in_sems, sems = refs[-4:]
    size = held.shape[1]
    cut = size // 2
    per_half = count // 2
    loads = []
    for i in range(per_half):
        at = pl.ds(i * size, size)
        pairs = [(ref.at[at, :], parts.at[n, at, :]) for n, ref in enumerate(parts_hbm)]
        loads.append(copies(pairs, in_sems.at[i]))
    places = done_places(size, [out.shape for out in outs])
    made = []
    for n, (row, which, i, j, high) in enumerate(places):
        made.append(
            pltpu.make_async_copy(
                held.at[row // size, pl.ds(row % size, high), :],
                outs[which].at[pl.ds(i, high), pl.ds(j, size)],
                sems.at[n],
            )
        )
    for b in [i + j for i in range(per_half) for j in (0, per_half)]:
        at = slice((b % per_half) * size, (b % per_half + 1) * size)
        if b < per_half:
            for copy in loads[b]:
                copy.wait()
        mine = jnp.where(sides[1] == b // per_half, parts[0, at, :], parts[1, at, :])
        theirs = jnp.where(sides[2] == b // per_half, parts[2, at, :], parts[3, at, :])
        held[b, :, :cut] = jnp.where(sides[0] == 0, mine, theirs).astype(F32)
        held[b, :, cut:] = jnp.where(sides[0] == 0, theirs, mine).astype(F32)
        for copy, place in zip(made, places):
            if place[0] // size == b:
                copy.start()
    row = (places[-1][0] + places[-1][4]) % size
    for ref in vectors:
        for j in range(ref.shape[1] // size):
            for i in range(ref.shape[0]):
                ref[i : i + 1, j * size : (j + 1) * size] = held[count - 1, row : row + 1, :]
                row += 1
    for copy in made:
        copy.wait()


def done_places(size, shapes):
    row, places = 0, []
    for n, (high, wide) in enumerate(shapes):
        for j in range(wide // size):
            for i in range(0, high, size):
                places.append((row, n, i, j * size, min(size, high - i)))
                row += min(size, high - i)
    return places


def done(sides, parts, shapes, vectors=()):
    rows, cut = parts[0].shape
    size = 2 * cut
    count = 2 * rows // size
    return pl.pallas_call(
        functools.partial(done_kernel, count, len(vectors)),
        grid_spec=pltpu.PrefetchScalarGridSpec(
            num_scalar_prefetch=1,
            grid=(1,),
            in_specs=[ANYWHERE] * 4,
            out_specs=[FAR] * len(shapes) + [whole(x) for x in vectors],
            scratch_shapes=[
                pltpu.VMEM((4, rows, cut), BF),
                pltpu.VMEM((count, size, size), F32),
                pltpu.SemaphoreType.DMA((count // 2, 4)),
                pltpu.SemaphoreType.DMA((len(done_places(size, shapes)),)),
            ],
        ),
        out_shape=[jax.ShapeDtypeStruct(x, F32) for x in (*shapes, *vectors)],
        cost_estimate=takes(5.0),
        compiler_params=SMALL_PARAMS,
    )(sides, *parts)


def visible_kernel(moved, own, weight, out):
    back = moved[...] + own[...]
    out[...] = mm_nt(back[0 : out.shape[0]], weight[...]).astype(BF)


def visible_gradient(moved, own, weight, vis_count):
    ins = (moved, own, weight)
    return pl.pallas_call(
        visible_kernel,
        grid=(1,),
        in_specs=[whole(x.shape) for x in ins],
        out_specs=whole((vis_count, weight.shape[0])),
        out_shape=jax.ShapeDtypeStruct((vis_count, weight.shape[0]), BF),
        cost_estimate=takes(3.0),
        compiler_params=SMALL_PARAMS,
    )(*ins)


def add_rows(terms, starts, size):
    total = 0.0
    for term, start in zip(terms, starts):
        total = total + lax.dynamic_slice_in_dim(term, start, size, 0).astype(F32)
    return total.astype(BF)


def join_rows(side, own, got):
    return jnp.where(
        side == 0, jnp.concatenate([own, got], axis=0), jnp.concatenate([got, own], axis=0)
    )


def shift(x, by, size):
    return lax.ppermute(x, "band", [(i, (i + by) % size) for i in range(size)])


def after(x, *others):
    return lax.optimization_barrier((x, *others))[0]


class Ring:
    def __init__(self, dp, band):
        me, z = lax.axis_index("dp"), lax.axis_index("band")
        self.dp = dp
        bits = []
        while (2 << len(bits)) < dp:
            bits.append(len(bits) + 1)
        self.stages = []
        sides = []
        for up, down in zip(bits, reversed(bits)):
            pairs = [(i, i ^ (1 << (down if i & 1 else up))) for i in range(dp)]
            both = ((me >> up) & 1, (me >> down) & 1)
            sides.append(both)
            self.stages.append(("dp", pairs, jnp.where(me & 1 == 1, both[1], both[0])))
        step = 1
        while step < band:
            pairs = [(i, i ^ step) for i in range(band)]
            side = (z // step) & 1
            sides.append((side, side))
            self.stages.append(("band", pairs, side))
            step *= 2
        core = me & 1
        self.core = core.astype(jnp.int32)[None]
        first = sides[0]
        mine = jnp.where(core == 1, first[1], first[0])
        theirs = jnp.where(core == 1, first[0], first[1])
        self.sides = jnp.stack([core, mine, theirs]).astype(jnp.int32)

    def swap_cores(self, x):
        return lax.ppermute(x, "dp", [(i, i ^ 1) for i in range(self.dp)])

    def swap(self, x, i):
        axis, pairs, _side = self.stages[i]
        return lax.ppermute(x, axis, pairs)


class Sum:
    def __init__(self, ring, keep, send):
        self.ring = ring
        zero = jnp.int32(0)
        self.terms, self.starts = [keep], [zero, zero]
        self.base, self.size = zero, keep.shape[0]
        self.stage = 0
        self.last = len(ring.stages)
        self.flight = [ring.swap_cores(send)]

    def rows(self, start):
        return add_rows(self.terms, [start - x for x in self.starts], self.size)

    def left(self):
        return self.stage < 2 * self.last

    def step(self):
        n, last = self.stage, self.last - 1
        self.stage += 1
        if n < last:
            self.terms += self.flight
            side = self.ring.stages[n][2].astype(jnp.int32)
            self.size //= 2
            send = self.rows(self.base + (1 - side) * self.size)
            self.base = self.base + side * self.size
            self.starts.append(self.base)
        elif n == last:
            self.terms += self.flight
            send = self.own = self.rows(self.base)
        elif n <= 2 * last:
            got = self.flight[0]
            if n == last + 1:
                self.own = (self.own.astype(F32) + got.astype(F32)).astype(BF)
            else:
                side = self.ring.stages[2 * last - n + 1][2]
                self.own = join_rows(side, self.own, got)
            send = self.own
        else:
            return self.swap_cores()
        self.flight = [self.ring.swap(send, min(n, 2 * last - n))]
        return send

    def swap_cores(self):
        self.halves = (self.own, self.flight[0])
        self.flight = [self.ring.swap_cores(x) for x in self.halves]
        return self.halves[1]

    def done(self, shapes, vectors=()):
        return done(self.ring.sides, [*self.halves, *self.flight], shapes, vectors)


class Trip:
    def __init__(self, x, band):
        self.band = band
        self.flight = [shift(x, 1, band)]

    def on(self, own):
        going = self.flight[0] + own
        self.flight = [shift(going, 1, self.band)]
        return going


def meet(flights, *others):
    arrays = [x for f in flights for x in f.flight]
    out = lax.optimization_barrier((*arrays, *others))
    at = 0
    for f in flights:
        f.flight = list(out[at : at + len(f.flight)])
        at += len(f.flight)
    return out[at:]


def body(
    dp, band,
    visible, clip_long, patch_order, embed_weight, embed_bias, mask_token,
    norm1_gain, norm1_bias, qkv_weight, qv_bias, proj_weight, proj_bias,
    norm2_gain, norm2_bias, fc1_weight, fc1_bias, fc2_weight, fc2_bias, cotangent,
):
    features = embed_weight.shape[1]
    hidden = fc1_weight.shape[1]
    total = patch_order.shape[1]
    rows = total // band
    vis_count, enc = visible.shape
    z = lax.axis_index("band")
    ring = Ring(dp, band)
    stages = len(ring.stages)

    order = patch_order[0]
    half = vis_count // 2
    middle = total // 2
    visible_at = jnp.where(
        clip_long[0] == 1,
        order[:vis_count],
        jnp.concatenate([order[:half], order[middle : middle + vis_count - half]]),
    )
    notes = jnp.stack(
        [visible_at // 64, visible_at % 64, jnp.broadcast_to(clip_long, (vis_count,))]
    ).astype(BF)
    notes = jnp.pad(notes, ((0, NOTE - 3), (0, enc - vis_count)), mode="edge")
    block = jnp.concatenate([visible, notes], axis=0)
    sources = [((z - k) % band).astype(jnp.int32)[None] for k in range(band)]
    moving = shift(block, 1, band)

    rowid = z * rows + jnp.arange(rows, dtype=jnp.int32)
    places = jnp.stack([row_layout(x, rowid, total)[0] for x in (True, False)])
    quads = z * rows + WIN * jnp.arange(LANES, dtype=jnp.int32)
    positions = []
    for place in (
        row_layout(True, quads, total)[1],
        row_layout(False, quads, total)[1],
        row_layout(True, rowid[:LANES], total)[2],
    ):
        positions += sincos_rows(place, features // 2)
    vectors = (
        mask_token, norm1_gain, norm1_bias, qv_bias, proj_bias, norm2_gain, norm2_bias, fc2_bias,
        embed_bias, fc1_bias,
    )
    cols = stack_columns([x if x.ndim == 2 else x[None] for x in vectors], features)
    weights = (embed_weight, qkv_weight, proj_weight, fc1_weight, fc2_weight, *positions)

    saved, kept, blocks = None, [], [block]
    for k in range(band):
        *saved, sums = forward(
            sources[k], blocks[k], places, cols, cotangent, weights, vis_count, saved
        )
        kept.append(sums)
        if k + 1 < band:
            blocks.append(after(moving, sums))
        if k + 2 < band:
            moving = shift(blocks[-1], 1, band)
    (x_t, a_t, qkv_t, probs, o_t, act_t, gh_t, c_t, x1_t, ch_t, gc_t) = saved

    send, keep, fc1b_grad = ff_gradients(ring.core, act_t, cotangent, c_t, gh_t)
    ff = Sum(ring, keep, send)
    old, emb, sums_b, trip = None, [None] * band, [None] * band, None
    back_order = list(range(1, band)) + [0]
    ready = [send]
    for n, k in enumerate(back_order):
        args = [after(gc_t, *ready), x1_t, cotangent, qkv_t, probs, x_t, ch_t]
        *old, emb[k], sums_b[k] = backward(
            sources[k], block.shape[0], kept[k], cols, args, (proj_weight, qkv_weight), old
        )
        flights = [[ff], [], [ff, trip], [ff, trip]][n]
        emb[k], sums_b[k] = meet(flights, emb[k], sums_b[k])
        ready = [ff.step()] if ff in flights else []
        if n == 0:
            trip = Trip(emb[k], band)
        elif n == 2:
            ready.append(trip.on(emb[back_order[1]]))
    gqkv_t, gy_t = old

    send, keep = rest_gradients(
        ring.core, after(a_t, *ready), gqkv_t, o_t, gy_t, fc1b_grad, blocks, emb, kept, sums_b
    )
    send, keep = meet([ff], send, keep)
    rest = Sum(ring, keep, send)
    ready = [ff.step()]
    meet([rest], *ready)
    block_out, waits, ff_grads = None, 0, None
    ff_shapes = [(hidden, features), (features, hidden)]
    ends = 2 * stages - 1
    outputs = {0: (0, band - 2), 1: (band - 2, 1), ends - 2: (band - 1, 1)}
    for n in range(ends):
        ready = [rest.step()]
        if n and ff.left() and not waits:
            ff.flight[0] = after(ff.flight[0], *ready)
            ready.append(ff.step())
            waits = 1 if ff.stage == ends else 0
        else:
            waits = max(waits - 1, 0)
        flights = [rest] if waits or n == 0 else [rest, ff]
        if n == ends - 1:
            ready.append(trip.on(emb[back_order[2]]))
        if n in outputs:
            block_out = output(
                after(x1_t, *ready), act_t, fc2_weight, fc2_bias[None], *outputs[n], block_out
            )
            (block_out,) = meet(flights, block_out)
        elif n == ends - 1 and not ff.left():
            ff.flight[0] = after(ff.flight[0], *ready)
            ff_grads = meet([rest, trip], *ff.done(ff_shapes))
        elif n == ends - 1:
            meet([rest, trip, ff])
        else:
            meet(flights)
    ready = [rest.step()]
    visible_grad = visible_gradient(
        after(trip.flight[0], *ready), emb[0], embed_weight, vis_count
    )
    (visible_grad,) = meet([rest], visible_grad)
    if ff_grads is None:
        while ff.left():
            ff.step()
        ff_grads = ff.done(ff_shapes)
    fc2_grad, fc1_grad = ff_grads
    row = (1, features)
    (
        qkv_grad, proj_grad, embed_grad,
        projb, qvb, gain1, bias1, mask, embb, gain2, bias2, fc2b, fc1b,
    ) = rest.done(
        [(features, 3 * features), (features, features), (enc, features)],
        [row, (2, features)] + [row] * 7 + [(1, hidden)],
    )
    return (
        block_out,
        visible_grad,
        embed_grad,
        embb[0],
        mask[0],
        gain1[0],
        bias1[0],
        qkv_grad,
        qvb,
        proj_grad,
        projb[0],
        gain2[0],
        bias2[0],
        fc1_grad,
        fc1b[0],
        fc2_grad,
        fc2b[0],
    )


def solution(mesh):
    split = P(("dp", "band"), None)
    in_specs = (split, P(("dp", "band")), split) + (P(),) * 15 + (split,)
    out_specs = (split, split) + (P(),) * 15
    return jax.shard_map(
        functools.partial(body, mesh.shape["dp"], mesh.shape["band"]),
        mesh=mesh,
        in_specs=in_specs,
        out_specs=out_specs,
        check_vma=False,
    )
```
